32 devices in a mesh: ctx: 16 (over z, y, x), fsdp: 2 (over core).
Axes of the slice: x: 2, y: 2, z: 4, core: 2. Of those that a mesh axis runs over, the one named last changes fastest.
Arguments:
- hidden_in: bfloat16 [2, 2048, 2048], P('fsdp', 'ctx'), may hold values from -6 to 6
- gain_attn: bfloat16 [2048], P(('ctx', 'fsdp')), may hold values from 0.099609375 to 1.8984375
- w_query: bfloat16 [2048, 3072], P(('ctx', 'fsdp')), may hold values from -0.25 to 0.25
- w_kv_down: bfloat16 [2048, 576], P(('ctx', 'fsdp')), may hold values from -0.125 to 0.125
- gain_kv: bfloat16 [512], P(('ctx', 'fsdp')), may hold values from 0.099609375 to 1.8984375
- w_kv_up: bfloat16 [512, 4096], P(('ctx', 'fsdp')), may hold values from -0.25 to 0.25
- w_out: bfloat16 [2048, 2048], P(('ctx', 'fsdp')), may hold values from -0.5 to 0.5
- gain_ffn: bfloat16 [2048], P(('ctx', 'fsdp')), may hold values from 0.099609375 to 1.8984375
- w_router: bfloat16 [2048, 16], P(('ctx', 'fsdp')), may hold values from -0.0625 to 0.0625
- shared_gate: bfloat16 [2048, 2816], P(('ctx', 'fsdp')), may hold values from -0.125 to 0.125
- shared_up: bfloat16 [2048, 2816], P(('ctx', 'fsdp')), may hold values from -0.125 to 0.125
- shared_down: bfloat16 [2816, 2048], P(('ctx', 'fsdp')), may hold values from -0.109375 to 0.109375
- expert_gate: bfloat16 [16, 2048, 1408], P('ctx', None, 'fsdp'), may hold values from -0.125 to 0.125
- expert_up: bfloat16 [16, 2048, 1408], P('ctx', None, 'fsdp'), may hold values from -0.125 to 0.125
- expert_down: bfloat16 [16, 2048, 1408], P('ctx', None, 'fsdp'), may hold values from -0.3125 to 0.3125
- routes: int32 [2, 2048, 6], P('fsdp', 'ctx'), may hold values from 0 to 15, all different within a row; in each aligned block of 128 rows (0 to 127, 128 to 255, ..., all dimensions but the last counted through in order) at most 64 rows name the same one
- cotangent: bfloat16 [2, 2048, 2048], P('fsdp', 'ctx'), may hold values from -6 to 6
Outputs:
- hidden_out: bfloat16 [2, 2048, 2048], P('fsdp', 'ctx')
- grad_hidden_in: float32 [2, 2048, 2048], P('fsdp', 'ctx')
- grad_gain_attn: float32 [2048], P(('ctx', 'fsdp'))
- grad_w_query: float32 [2048, 3072], P(('ctx', 'fsdp'))
- grad_w_kv_down: float32 [2048, 576], P(('ctx', 'fsdp'))
- grad_gain_kv: float32 [512], P(('ctx', 'fsdp'))
- grad_w_kv_up: float32 [512, 4096], P(('ctx', 'fsdp'))
- grad_w_out: float32 [2048, 2048], P(('ctx', 'fsdp'))
- grad_gain_ffn: float32 [2048], P(('ctx', 'fsdp'))
- grad_w_router: float32 [2048, 16], P(('ctx', 'fsdp'))
- grad_shared_gate: float32 [2048, 2816], P(('ctx', 'fsdp'))
- grad_shared_up: float32 [2048, 2816], P(('ctx', 'fsdp'))
- grad_shared_down: float32 [2816, 2048], P(('ctx', 'fsdp'))
- grad_expert_gate: float32 [16, 2048, 1408], P('ctx', None, 'fsdp')
- grad_expert_up: float32 [16, 2048, 1408], P('ctx', None, 'fsdp')
- grad_expert_down: float32 [16, 2048, 1408], P('ctx', None, 'fsdp')
The draws below stay inside these ranges and needn't reach their ends.
Inputs may be any that keep to these rules, and one draw needn't show every extreme that they name: `routes`: each token names 6 different experts. In each aligned block of 128 tokens of a sequence (the tokens of one device), no expert is named by more than 64 tokens.
All inputs are finite; a program needn't handle non-finite values.
Results may differ from the reference program's by a relative error of at most 0.023.
Values may be sent and summed in bfloat16 or wider, within the bound.
No kernel may reach another device: no remote copies, remote signals or barrier semaphores. Data moves between devices by JAX's collectives and lax.ppermute only.
A program may use at most 448 MiB of HBM per device.

```python
import math
import jax
import jax.numpy as jnp
import numpy as np
from jax import lax

D = 2048
HEADS = 16
NOPE = 128
ROPE = 64
VHEAD = 128
KVR = 512
EFF = 1408
SFF = 2816
TOP = 6
SEQ_DEV = 128
SEQ = 2048
SEQS = 2
EXPERTS = 16
SLOT_CAP = 64
N_CTX = 16


def block_scale(key, shape, cuts, least, top_value):
    def one(position, parts):
        heights = jax.random.uniform(jax.random.fold_in(jax.random.fold_in(key, 6), position), (parts,), jnp.float32, least / len(cuts), top_value / len(cuts))
        return jnp.repeat(jnp.exp(heights), shape[position] // parts).reshape((-1,) + (1,) * (len(shape) - position - 1))

    level = one(*cuts[0])
    for cut in cuts[1:]:
        level = level * one(*cut)
    return level


def assign_block(key, own, number, rows, amount, top, limit, skew):
    order = jax.random.permutation(key, amount)
    heavy_load, usual = load_shares(amount, rows * top, limit, skew, True), load_shares(amount, rows * top, limit, skew, False)
    places = jnp.arange(amount)

    def named(tallies, offset_by):
        used = int((tallies > 0).sum())
        fixed = max(1, used // 4)
        passed = fixed + (places - fixed + offset_by * (used - fixed)) % max(1, amount - fixed)
        return jnp.zeros((amount,), jnp.int32).at[order[jnp.where(places < fixed, places, passed)]].set(jnp.asarray(tallies, jnp.int32))

    tallies = jnp.where(number % 4 == 0, named(heavy_load, number // 4), named(usual, number - number // 4 - 1))
    mixed = jax.random.permutation(jax.random.fold_in(own, 3), amount)
    source_of, receiver = mixed[0:amount // 2 * 2:2], mixed[1:amount // 2 * 2:2]
    slack = jnp.minimum(tallies[source_of] - 1, limit - tallies[receiver]) // 2
    slack = jnp.where((source_of == order[0]) | (receiver == order[0]) | (tallies[receiver] == 0), 0, jnp.maximum(slack, 0))
    passed = jax.random.randint(jax.random.fold_in(own, 4), (amount // 2,), 0, 1 << 20) % (slack + 1)
    tallies = tallies.at[source_of].add(-passed).at[receiver].add(passed)
    members = jnp.searchsorted(jnp.cumsum(tallies), jnp.arange(rows * top), side="right").astype(jnp.int32)
    grid = members.reshape(top, rows).T
    grid = grid[jax.random.permutation(jax.random.fold_in(own, 1), rows)]
    offset_by = jax.random.randint(jax.random.fold_in(own, 2), (rows, 1), 0, top)
    return jnp.take_along_axis(grid, (jnp.arange(top)[None, :] + offset_by) % top, axis=1)


def load_shares(number_of, total, bound, slope, full):
    weights = [(1 << 20) // math.isqrt(standing ** slope) + 1 for standing in range(1, number_of + 1)]
    largest = bound if full else min(bound, max(-(-total // number_of), total * weights[0] // sum(weights)))
    least = 1 if total - largest >= number_of - 1 else 0
    given, surplus = [largest] + [least] * (number_of - 1), total - largest - least * (number_of - 1)
    while surplus > 0:
        movable = [i for i in range(1, number_of) if given[i] < largest] or [i for i in range(1, number_of) if given[i] < bound]
        pool, budget = sum([weights[i] for i in movable]), surplus
        for i in movable:
            more = min(bound - given[i], max(1, budget * weights[i] // pool), surplus)
            given[i] = given[i] + more
            surplus = surplus - more
    return np.array(given)


def normal_values(rng, shape, spread, limit, cuts=(), held_as=jnp.bfloat16):
    values = spread * jax.random.normal(rng, shape, jnp.float32)
    if cuts:
        values = values * block_scale(rng, shape, cuts, -0.22, 0.18)
    return jnp.clip(values, -limit, limit).astype(held_as)


def setup_inputs(seed: int = 0) -> dict:
    key_list = jax.random.split(jax.random.key(seed), 18)
    hidden_in = normal_values(key_list[0], (SEQS, SEQ, D), 1.0, 6.0, ((0, 2), (1, 16)))
    gain_attn = jnp.clip(1.0 + 0.18 * jax.random.normal(key_list[1], (D,), jnp.float32), 0.099609375, 1.8984375).astype(jnp.bfloat16)
    w_query = normal_values(key_list[2], (D, HEADS * (NOPE + ROPE)), (D // 4) ** -0.5, 0.25, ((0, 32),))
    w_kv_down = normal_values(key_list[3], (D, KVR + ROPE), D ** -0.5, 0.125, ((0, 32),))
    gain_kv = jnp.clip(1.0 + 0.18 * jax.random.normal(key_list[4], (KVR,), jnp.float32), 0.099609375, 1.8984375).astype(jnp.bfloat16)
    w_kv_up = normal_values(key_list[5], (KVR, HEADS * (NOPE + VHEAD)), KVR ** -0.5, 0.25, ((0, 32),))
    w_out = normal_values(key_list[6], (HEADS * VHEAD, D), (HEADS * VHEAD // 16) ** -0.5, 0.5, ((0, 32),))
    gain_ffn = jnp.clip(1.0 + 0.18 * jax.random.normal(key_list[7], (D,), jnp.float32), 0.099609375, 1.8984375).astype(jnp.bfloat16)
    w_router = normal_values(key_list[8], (D, EXPERTS), (4 * D) ** -0.5, 0.0625, ((0, 32),))
    shared_gate = normal_values(key_list[9], (D, SFF), D ** -0.5, 0.125, ((0, 32),))
    shared_up = normal_values(key_list[10], (D, SFF), D ** -0.5, 0.125, ((0, 32),))
    shared_down = normal_values(key_list[11], (SFF, D), SFF ** -0.5, 0.109375, ((0, 32),))
    expert_gate = normal_values(key_list[12], (EXPERTS, D, EFF), D ** -0.5, 0.125, ((0, 16), (2, 2)))
    expert_up = normal_values(key_list[13], (EXPERTS, D, EFF), D ** -0.5, 0.125, ((0, 16), (2, 2)))
    expert_down = normal_values(key_list[14], (EXPERTS, D, EFF), (EFF // 4) ** -0.5, 0.3125, ((0, 16), (2, 2)))
    routes_keys = jax.random.split(jax.random.fold_in(key_list[15], 1), SEQS * SEQ // SEQ_DEV)
    routes_turns = jax.random.permutation(jax.random.fold_in(key_list[15], 3), SEQS * SEQ // SEQ_DEV)
    routes = jax.vmap(lambda own, number: assign_block(jax.random.fold_in(key_list[15], 2), own, number, SEQ_DEV, EXPERTS, TOP, SLOT_CAP, 0))(routes_keys, routes_turns).reshape((SEQS, SEQ, TOP))
    cotangent = normal_values(key_list[16], (SEQS, SEQ, D), 1.0, 6.0, ((0, 2), (1, 16)))
    return dict(hidden_in=hidden_in, gain_attn=gain_attn, w_query=w_query, w_kv_down=w_kv_down, gain_kv=gain_kv, w_kv_up=w_kv_up, w_out=w_out, gain_ffn=gain_ffn, w_router=w_router, shared_gate=shared_gate, shared_up=shared_up, shared_down=shared_down, expert_gate=expert_gate, expert_up=expert_up, expert_down=expert_down, routes=routes, cotangent=cotangent)


epsilon = 1e-06
rope_base = 10000.0
masked_score = -1e+30

@jax.custom_vjp
def low(v):
    return lax.optimization_barrier(v.astype(jnp.bfloat16)).astype(jnp.float32)

@jax.custom_vjp
def low_back(v):
    return v

def low_keep(v):
    return (low(v), None)

def low_pass(kept, grad):
    return (grad,)

def back_keep(v):
    return (v, None)

def back_low(kept, grad):
    return (low(grad),)
low.defvjp(low_keep, low_pass)
low_back.defvjp(back_keep, back_low)

def product(left, right):
    return jnp.dot(left, right, precision=lax.Precision.HIGHEST)

def rms_norm(values, gain):
    return values * lax.rsqrt(lax.optimization_barrier(jnp.mean(values * values, axis=-1, keepdims=True)) + epsilon) * gain

def rope_tables(positions):
    half_width = ROPE // 2
    frequency = jnp.exp(jnp.arange(half_width, dtype=jnp.float32) * (-math.log(rope_base) / half_width))
    angles = positions[:, None] * frequency[None, :]
    angles = jnp.concatenate([angles, angles], axis=-1)
    return (jnp.cos(angles), jnp.sin(angles))

def rotate(values, cosine, sine):
    half_width = values.shape[-1] // 2
    turned = jnp.concatenate([-values[..., half_width:], values[..., :half_width]], axis=-1)
    return values * cosine + turned * sine

def attention(queries, keys, values):
    length = queries.shape[0]
    key_span = min(512, length)
    score_scale = 1.0 / math.sqrt(NOPE + ROPE)
    key_pos = jnp.arange(length, dtype=jnp.int32)

    def per_block(offset):
        query_rows = lax.dynamic_slice_in_dim(queries, offset, key_span, 0)
        scores = jnp.einsum('qhd,khd->hqk', query_rows, keys, precision=lax.Precision.HIGHEST) * score_scale
        scores = low_back(scores)
        query_pos = offset + jnp.arange(key_span, dtype=jnp.int32)
        visible = key_pos[None, :] <= query_pos[:, None]
        scores = jnp.where(visible[None], scores, masked_score)
        weights = low(jax.nn.softmax(scores, axis=-1))
        return jnp.einsum('hqk,khv->qhv', weights, values, precision=lax.Precision.HIGHEST)
    offsets = jnp.arange(length // key_span, dtype=jnp.int32) * key_span
    outcome = lax.map(jax.checkpoint(per_block), offsets)
    return outcome.reshape(length, HEADS * VHEAD)

def slot_targets(route_ids):
    length = route_ids.shape[0]
    hot = (route_ids[:, :, None] == jnp.arange(EXPERTS, dtype=jnp.int32)[None, None, :]).astype(jnp.int32)
    hot = hot.reshape(length // SEQ_DEV, SEQ_DEV * TOP, EXPERTS)
    earlier = jnp.cumsum(hot, axis=1) - hot
    ordinal = lax.optimization_barrier(jnp.sum(earlier * hot, axis=-1)).reshape(length, TOP)
    part_of = (jnp.arange(length, dtype=jnp.int32) // SEQ_DEV)[:, None]
    return route_ids * (N_CTX * SLOT_CAP) + part_of * SLOT_CAP + ordinal

def expert_apply(operands):
    gate_w, up_w, down_w, entries = operands
    gate_pre = low_back(product(entries, gate_w))
    up_pre = low_back(product(entries, up_w))
    middle = low(jax.nn.silu(gate_pre) * up_pre)
    return jnp.einsum('rf,df->rd', middle, down_w, precision=lax.Precision.HIGHEST)

def sequence_forward(params, tokens, route_ids):
    attn_gain, query_w, reduce_w, kv_gain, expand_w, output_w, ffn_gain, router_w, shared_gate_w, shared_up_w, shared_down_w, gate_w, up_w, down_w = params
    length = tokens.shape[0]
    cosine, sine = rope_tables(jnp.arange(length, dtype=jnp.float32))
    normed = low(rms_norm(tokens, attn_gain))
    query_pre = low_back(product(normed, query_w)).reshape(length, HEADS, NOPE + ROPE)
    queries = low(jnp.concatenate([query_pre[..., :NOPE], rotate(query_pre[..., NOPE:], cosine[:, None, :], sine[:, None, :])], axis=-1))
    compressed = low_back(product(normed, reduce_w))
    latent = low(rms_norm(compressed[:, :KVR], kv_gain))
    key_rope = rotate(compressed[:, KVR:], cosine, sine)
    expanded = low_back(product(latent, expand_w)).reshape(length, HEADS, NOPE + VHEAD)
    keys = low(jnp.concatenate([expanded[..., :NOPE], jnp.broadcast_to(key_rope[:, None, :], (length, HEADS, ROPE))], axis=-1))
    values = low(expanded[..., NOPE:])
    attended = low(low_back(attention(queries, keys, values)))
    residual = tokens + low_back(product(attended, output_w))
    ffn_in = low(rms_norm(residual, ffn_gain))
    logits = low_back(product(ffn_in, router_w))
    gate_share = jax.nn.softmax(jnp.take_along_axis(logits, route_ids, axis=-1), axis=-1)
    shared_gate_pre = low_back(product(ffn_in, shared_gate_w))
    shared_up_pre = low_back(product(ffn_in, shared_up_w))
    shared_mid = low(jax.nn.silu(shared_gate_pre) * shared_up_pre)
    shared_out = low_back(product(shared_mid, shared_down_w))
    targets = slot_targets(route_ids).reshape(-1)
    slots = jnp.zeros((EXPERTS * N_CTX * SLOT_CAP, D), jnp.float32).at[targets].add(jnp.repeat(ffn_in, TOP, axis=0))
    slots = low_back(slots).reshape(EXPERTS, N_CTX * SLOT_CAP, D)
    outputs = lax.map(jax.checkpoint(expert_apply), (gate_w, up_w, down_w, slots))
    outputs = low(low_back(outputs)).reshape(EXPERTS * N_CTX * SLOT_CAP, D)
    picked = outputs[targets].reshape(length, TOP, D)
    routed = lax.optimization_barrier(jnp.sum(gate_share[..., None] * picked, axis=1))
    return residual + shared_out + routed

def reference(hidden_in, gain_attn, w_query, w_kv_down, gain_kv, w_kv_up, w_out, gain_ffn, w_router, shared_gate, shared_up, shared_down, expert_gate, expert_up, expert_down, routes, cotangent):
    params = (gain_attn.astype(jnp.float32), w_query.astype(jnp.float32), w_kv_down.astype(jnp.float32), gain_kv.astype(jnp.float32), w_kv_up.astype(jnp.float32), w_out.astype(jnp.float32), gain_ffn.astype(jnp.float32), w_router.astype(jnp.float32), shared_gate.astype(jnp.float32), shared_up.astype(jnp.float32), shared_down.astype(jnp.float32), expert_gate.astype(jnp.float32), expert_up.astype(jnp.float32), expert_down.astype(jnp.float32))
    tokens = hidden_in.astype(jnp.float32)

    def forward(weights, inputs):

        def per_sequence(operands):
            return sequence_forward(weights, operands[0], operands[1])
        return lax.map(per_sequence, (inputs, routes))
    outcome, pullback = jax.vjp(forward, params, tokens)
    grad_params, grad_tokens = pullback(cotangent.astype(jnp.float32))
    return (outcome.astype(jnp.bfloat16), grad_tokens, grad_params[0], grad_params[1], grad_params[2], grad_params[3], grad_params[4], grad_params[5], grad_params[6], grad_params[7], grad_params[8], grad_params[9], grad_params[10], grad_params[11], grad_params[12], grad_params[13])
```

```python
import functools
import math

import jax
import jax.numpy as jnp
from jax import lax
from jax.experimental import pallas as pl
from jax.experimental.pallas import tpu as pltpu
from jax.sharding import PartitionSpec as P

HEADS = 16
NOPE = 128
ROPE = 64
VHEAD = 128
KVR = 512
TOP = 6
QK = NOPE + ROPE

epsilon = 1e-06
rope_base = 10000.0
masked_score = -1e30
score_scale = 1.0 / math.sqrt(QK)

bf16 = jnp.bfloat16
f32 = jnp.float32


def mm(left, right):
    return jnp.dot(left, right, preferred_element_type=f32)


def mm_nt(left, right):
    return lax.dot_general(left, right, (((1,), (1,)), ((), ())), preferred_element_type=f32)


def mm_tn(left, right):
    return lax.dot_general(left, right, (((0,), (0,)), ((), ())), preferred_element_type=f32)


def rms_factor(values):
    return lax.rsqrt(jnp.mean(values * values, axis=-1, keepdims=True) + epsilon)


def rms_backward(values, factor, gain, upstream):
    weighted = upstream * gain
    inner_mean = jnp.mean(weighted * values, axis=-1, keepdims=True)
    grad_in = factor * weighted - values * (factor * factor * factor) * inner_mean
    grad_gain = jnp.sum(upstream * values * factor, axis=0)
    return (grad_in, grad_gain)


def rope_tables(positions):
    half_width = ROPE // 2
    frequency = jnp.exp(jnp.arange(half_width, dtype=f32) * (-math.log(rope_base) / half_width))
    angles = positions.astype(f32)[:, None] * frequency[None, :]
    angles = jnp.concatenate([angles, angles], axis=-1)
    return (jnp.cos(angles), jnp.sin(angles))


def rotate(values, cosine, sine):
    half_width = values.shape[-1] // 2
    turned = jnp.concatenate([-values[..., half_width:], values[..., :half_width]], axis=-1)
    return values * cosine + turned * sine


def unrotate(upstream, cosine, sine):
    half_width = upstream.shape[-1] // 2
    rotated = upstream * sine
    turned = jnp.concatenate([rotated[..., half_width:], -rotated[..., :half_width]], axis=-1)
    return upstream * cosine + turned


def swiglu(gate_pre, up_pre):
    return (jax.nn.silu(gate_pre) * up_pre).astype(bf16)


def swiglu_grads(gate_pre, up_pre, grad_mid):
    squash = jax.nn.sigmoid(gate_pre)
    grad_gate = grad_mid * up_pre * squash * (1.0 + gate_pre * (1.0 - squash))
    grad_up = grad_mid * (gate_pre * squash)
    return (grad_gate.astype(bf16), grad_up.astype(bf16))


def exchanges():
    return lax.axis_size("ctx") == 16


def ctx_order():
    span = jnp.arange(lax.axis_size("ctx"), dtype=jnp.int32)
    return span ^ lax.axis_index("ctx") if exchanges() else span


def by_order(values):
    return jnp.take(values, ctx_order(), axis=0, mode="clip")


def hop(value, mask):
    return lax.ppermute(value, "ctx", [(i, i ^ mask) for i in range(16)])


def gather_ctx(block):
    if not exchanges():
        return lax.all_gather(block, "ctx", axis=0)
    half = block.shape[0] // 2
    held = {0: block}
    held[4] = hop(block, 4)
    held[8] = hop(block, 8)
    held[12] = hop(held[4], 8)
    for base in (0, 4, 8, 12):
        held[base ^ 1] = hop(held[base], 1)
        held[base ^ 2] = hop(held[base], 2)
        first = hop(held[base ^ 1][:half], 2)
        second = hop(held[base ^ 2][half:], 1)
        held[base ^ 3] = jnp.concatenate([first, second], axis=0)
    return jnp.stack([held[j] for j in range(16)])


def scatter_ctx(blocks):
    if not exchanges():
        return lax.psum_scatter(blocks.astype(bf16), "ctx", scatter_dimension=0).astype(f32)
    half = blocks.shape[1] // 2
    from_12 = from_8 = None
    total = None
    for base in (12, 8, 4, 0):
        far = blocks[base ^ 3].astype(bf16)
        one, two = (blocks[base ^ 1].astype(f32), blocks[base ^ 2].astype(f32))
        first = hop(far[:half], 2).astype(f32)
        second = hop(far[half:], 1).astype(f32)
        one = jnp.concatenate([one[:half] + first, one[half:]], axis=0).astype(bf16)
        two = jnp.concatenate([two[:half], two[half:] + second], axis=0).astype(bf16)
        total = blocks[base].astype(f32) + hop(one, 1).astype(f32) + hop(two, 2).astype(f32)
        if base == 12:
            from_12 = hop(total.astype(bf16), 8)
        elif base == 8:
            from_8 = hop(total.astype(bf16), 8)
        elif base == 4:
            from_4 = hop((total + from_12.astype(f32)).astype(bf16), 4)
    return total + from_8.astype(f32) + from_4.astype(f32)


def swap_cores(value):
    return lax.ppermute(value, "fsdp", [(0, 1), (1, 0)])


def gather_fsdp(block):
    if lax.axis_size("fsdp") == 2:
        return [block, swap_cores(block)]
    whole = lax.all_gather(block, "fsdp", axis=0)
    return [whole[i] for i in range(lax.axis_size("fsdp"))]


def scatter_fsdp(parts):
    if lax.axis_size("fsdp") == 2:
        return parts[0].astype(f32) + swap_cores(parts[1].astype(bf16)).astype(f32)
    stacked = jnp.stack([part.astype(bf16) for part in parts])
    return lax.psum_scatter(stacked, "fsdp", scatter_dimension=0).astype(f32)


def in_fsdp_order(parts):
    if lax.axis_size("fsdp") == 2:
        low = lax.axis_index("fsdp") == 0
        return [jnp.where(low, parts[0], parts[1]), jnp.where(low, parts[1], parts[0])]
    return parts


def to_owner(blocks):
    return lax.all_to_all(blocks, "ctx", split_axis=0, concat_axis=0, tiled=True)


def attend_kernel(key_tile, reach, pos_ref, query_ref, key_ref, value_ref, out_ref, low_ref, lse_ref):
    queries = query_ref[...]
    rows = queries.shape[0]
    positions = pos_ref[...]
    tiles = (pl.program_id(0) + 1) * reach // key_tile

    def step(index, carry):
        top, total, running = carry
        keys = key_ref[pl.ds(index * key_tile, key_tile), :]
        values = value_ref[pl.ds(index * key_tile, key_tile), :]
        scores = mm_nt(queries, keys) * score_scale
        key_pos = index * key_tile + lax.broadcasted_iota(jnp.int32, scores.shape, 1)
        scores = jnp.where(key_pos <= positions, scores, masked_score)
        new_top = jnp.maximum(top, jnp.max(scores, axis=-1, keepdims=True))
        weights = jnp.exp(scores - new_top)
        shrink = jnp.exp(top - new_top)
        total = total * shrink + jnp.sum(weights, axis=-1, keepdims=True)
        running = running * shrink + mm(weights.astype(bf16), values)
        return (new_top, total, running)

    start = (
        jnp.full((rows, 1), masked_score, f32),
        jnp.zeros((rows, 1), f32),
        jnp.zeros((rows, VHEAD), f32),
    )
    top, total, running = lax.fori_loop(0, tiles, step, start)
    outcome = running / total
    out_ref[...] = outcome
    low_ref[...] = outcome.astype(bf16)
    lse_ref[...] = top + jnp.log(total)


def attend_grad_kernel(
    key_tile, reach, pos_ref, query_ref, key_ref, value_ref, out_ref, lse_ref, grad_ref,
    dquery_ref, dkey_ref, dvalue_ref,
):
    @pl.when(pl.program_id(0) == 0)
    def clear():
        dkey_ref[...] = jnp.zeros_like(dkey_ref)
        dvalue_ref[...] = jnp.zeros_like(dvalue_ref)

    queries = query_ref[...]
    grads = grad_ref[...]
    positions = pos_ref[...]
    lse = lse_ref[...]
    delta = jnp.sum(grads.astype(f32) * out_ref[...], axis=-1, keepdims=True)
    tiles = (pl.program_id(0) + 1) * reach // key_tile

    def step(index, dquery):
        span = pl.ds(index * key_tile, key_tile)
        keys = key_ref[span, :]
        values = value_ref[span, :]
        scores = mm_nt(queries, keys) * score_scale
        key_pos = index * key_tile + lax.broadcasted_iota(jnp.int32, scores.shape, 1)
        probs = jnp.where(key_pos <= positions, jnp.exp(scores - lse), 0.0)
        dprobs = mm_nt(grads, values)
        dscores = (probs * (dprobs - delta)).astype(bf16)
        dvalue_ref[span, :] += mm_tn(probs.astype(bf16), grads)
        dkey_ref[span, :] += mm_tn(dscores, queries)
        return dquery + mm(dscores, keys)

    dquery_ref[...] = lax.fori_loop(0, tiles, step, jnp.zeros(queries.shape, f32))


def attention_tiles(rows, keys):
    tile = min(512, keys)
    row_tile = rows * tile // keys
    return (row_tile, tile)


def attend(positions, queries, keys, values):
    rows, count = queries.shape[0], keys.shape[0]
    row_tile, tile = attention_tiles(rows, count)
    whole = lambda width: pl.BlockSpec((count, width), lambda i: (0, 0))
    part = lambda width: pl.BlockSpec((row_tile, width), lambda i: (i, 0))
    return pl.pallas_call(
        functools.partial(attend_kernel, tile, tile),
        grid=(rows // row_tile,),
        in_specs=[part(1), part(QK), whole(QK), whole(VHEAD)],
        out_specs=[part(VHEAD), part(VHEAD), part(1)],
        out_shape=[
            jax.ShapeDtypeStruct((rows, VHEAD), f32),
            jax.ShapeDtypeStruct((rows, VHEAD), bf16),
            jax.ShapeDtypeStruct((rows, 1), f32),
        ],
        compiler_params=pltpu.CompilerParams(vmem_limit_bytes=48 * 1024 * 1024),
        cost_estimate=pl.CostEstimate(
            flops=rows * count * (QK + VHEAD),
            bytes_accessed=4 * (rows + count) * (QK + VHEAD),
            transcendentals=rows * count // 2,
        ),
        name="attend",
    )(positions, queries, keys, values)


def attend_grad(positions, queries, keys, values, outcome, lse, grads):
    rows, count = queries.shape[0], keys.shape[0]
    row_tile, tile = attention_tiles(rows, count)
    whole = lambda width: pl.BlockSpec((count, width), lambda i: (0, 0))
    part = lambda width: pl.BlockSpec((row_tile, width), lambda i: (i, 0))
    return pl.pallas_call(
        functools.partial(attend_grad_kernel, tile, tile),
        grid=(rows // row_tile,),
        in_specs=[part(1), part(QK), whole(QK), whole(VHEAD), part(VHEAD), part(1), part(VHEAD)],
        out_specs=[part(QK), whole(QK), whole(VHEAD)],
        out_shape=[
            jax.ShapeDtypeStruct((rows, QK), f32),
            jax.ShapeDtypeStruct((count, QK), f32),
            jax.ShapeDtypeStruct((count, VHEAD), f32),
        ],
        compiler_params=pltpu.CompilerParams(vmem_limit_bytes=48 * 1024 * 1024),
        cost_estimate=pl.CostEstimate(
            flops=rows * count * (3 * QK + 2 * VHEAD),
            bytes_accessed=8 * (rows + count) * (QK + VHEAD),
            transcendentals=rows * count // 2,
        ),
        name="attend_grad",
    )(positions, queries, keys, values, outcome, lse, grads)


def shards(
    hidden_in, gain_attn, w_query, w_kv_down, gain_kv, w_kv_up, w_out, gain_ffn, w_router,
    shared_gate, shared_up, shared_down, expert_gate, expert_up, expert_down, routes, cotangent,
):
    part, width = hidden_in.shape[1:]
    ctx, fsdp = lax.axis_size("ctx"), lax.axis_size("fsdp")
    ctx_rank = lax.axis_index("ctx")
    length = part * ctx
    rows = w_query.shape[0]
    experts = w_router.shape[1]
    order = ctx_order()

    def split_width(values):
        lead = values.shape[:-1]
        grid = values.reshape(*lead, ctx, fsdp, rows)
        grid = jnp.moveaxis(jnp.take(grid, order, axis=len(lead), mode="clip"), -2, 0)
        return [v.reshape(*lead, ctx * rows) for v in in_fsdp_order([grid[i] for i in range(fsdp)])]

    def join_width(parts):
        lead = parts[0].shape[:-1]
        parts = [v.reshape(*lead, ctx, rows) for v in in_fsdp_order(list(parts))]
        grid = jnp.stack(parts, axis=-2)
        grid = jnp.take(grid, order, axis=len(lead), mode="clip")
        return grid.reshape(*lead, width)

    columns = HEADS * QK + KVR + ROPE
    extra = [
        w_router,
        gain_attn[:, None],
        gain_ffn[:, None],
        jnp.pad(gain_kv, (0, rows - gain_kv.shape[0]))[:, None],
    ]
    extra_width = experts + 3
    padding = -(columns + extra_width) % 128
    packed = jnp.concatenate(
        [w_query, w_kv_down] + extra + [jnp.zeros((rows, padding), bf16)], axis=1
    )
    packed_parts = [v.reshape(ctx * rows, -1) for v in gather_fsdp(gather_ctx(packed))]
    small = [v[:, columns : columns + extra_width] for v in packed_parts]
    small_natural = jnp.take(
        jnp.stack([v.reshape(ctx, rows, extra_width) for v in in_fsdp_order(small)], axis=1),
        order, axis=0, mode="clip",
    )
    router_full = small_natural[..., :experts].reshape(width, experts)
    ffn_gain = small_natural[..., experts + 1].reshape(width).astype(f32)
    kv_gain = small_natural[..., : gain_kv.shape[0], experts + 2].reshape(KVR).astype(f32)
    attn_gain = jnp.concatenate([v[:, experts] for v in small]).astype(f32)

    parts_of_head = ctx // HEADS
    query_part = part // parts_of_head
    up_rows = w_kv_up.shape[0]
    up_blocks = w_kv_up.reshape(up_rows, HEADS, NOPE + VHEAD).transpose(1, 0, 2)
    up_blocks = to_owner(jnp.repeat(up_blocks, parts_of_head, axis=0))
    expand = jnp.stack(in_fsdp_order(gather_fsdp(up_blocks)), axis=1).reshape(KVR, NOPE + VHEAD)

    hidden_shared = shared_gate.shape[1] // ctx
    shared_blocks = jnp.concatenate(
        [
            shared_gate.reshape(rows, ctx, hidden_shared),
            shared_up.reshape(rows, ctx, hidden_shared),
        ],
        axis=2,
    ).transpose(1, 0, 2)
    shared_blocks = to_owner(shared_blocks)
    shared_in = jnp.stack(in_fsdp_order(gather_fsdp(shared_blocks)), axis=1).reshape(
        width, 2 * hidden_shared
    )
    shared_back = jnp.concatenate(in_fsdp_order(gather_fsdp(shared_down)), axis=0)
    gate_parts = gather_fsdp(expert_gate[0])
    up_parts = gather_fsdp(expert_up[0])
    down_parts = gather_fsdp(expert_down[0])
    output_parts = [v.reshape(ctx * rows, width) for v in gather_fsdp(gather_ctx(w_out))]
    upstream_low = cotangent.reshape(part, width)
    upstream_all = gather_ctx(upstream_low)

    slot_cap = min(part, part * TOP * 4 // (3 * experts))
    route_rows = routes.reshape(part, TOP)
    chosen_hot = route_rows[:, :, None] == jnp.arange(experts, dtype=jnp.int32)[None, None, :]
    named = jnp.any(chosen_hot, axis=1).astype(bf16)
    named_all = by_order(to_owner(named.T))
    until = jnp.arange(part)[:, None] <= jnp.arange(part)[None, :]
    ordinal = mm(named_all, until.astype(bf16)) - 1.0
    slots = jnp.arange(slot_cap, dtype=f32)[None, :, None]
    pick = ((ordinal[:, None, :] == slots) & (named_all[:, None, :] > 0)).astype(bf16)

    tokens = hidden_in.astype(f32).reshape(part, width)
    attn_factor = rms_factor(tokens)
    tokens_split = jnp.concatenate(split_width(tokens), axis=-1)
    normed_low = (tokens_split * attn_factor * attn_gain).astype(bf16)
    span = ctx * rows
    normed_parts = [normed_low[:, i * span : (i + 1) * span] for i in range(fsdp)]
    projected = sum(mm(v, w[:, :columns]) for v, w in zip(normed_parts, packed_parts))
    cosine, sine = rope_tables(ctx_rank * part + jnp.arange(part, dtype=jnp.int32))
    queries = projected[:, : HEADS * QK].reshape(part, HEADS, QK)
    query_low = jnp.concatenate(
        [queries[..., :NOPE], rotate(queries[..., NOPE:], cosine[:, None, :], sine[:, None, :])],
        axis=-1,
    ).astype(bf16)
    compressed = projected[:, HEADS * QK :]
    latent_raw = compressed[:, :KVR]
    kv_factor = rms_factor(latent_raw)
    latent_low = (latent_raw * kv_factor * kv_gain).astype(bf16)
    key_rope = rotate(compressed[:, KVR:], cosine, sine).astype(bf16)

    def to_heads(values):
        split = values.reshape(parts_of_head, query_part, HEADS, values.shape[-1])
        sent = split.transpose(2, 0, 1, 3).reshape(ctx, query_part, values.shape[-1])
        return to_owner(sent).reshape(ctx * query_part, values.shape[-1])

    def from_heads(values):
        back = to_owner(values.reshape(ctx, query_part, values.shape[-1]))
        back = back.reshape(HEADS, parts_of_head, query_part, values.shape[-1])
        return back.transpose(1, 2, 0, 3).reshape(part, HEADS, values.shape[-1])

    query_head = to_heads(query_low)
    latent_all = by_order(gather_ctx(jnp.concatenate([latent_low, key_rope], axis=-1)))
    latent_all = latent_all.reshape(length, KVR + ROPE)
    expanded = mm(latent_all[:, :KVR], expand).astype(bf16)
    key_head = jnp.concatenate([expanded[:, :NOPE], latent_all[:, KVR:]], axis=-1)
    value_head = expanded[:, NOPE:]
    first_row = (ctx_rank % parts_of_head) * query_part
    query_pos = (
        jnp.arange(ctx, dtype=jnp.int32)[:, None] * part
        + first_row
        + jnp.arange(query_part, dtype=jnp.int32)[None, :]
    ).reshape(ctx * query_part, 1)
    outcome, outcome_low, lse = attend(query_pos, query_head, key_head, value_head)
    attended = from_heads(outcome_low).reshape(part, HEADS * VHEAD)
    attended_parts = split_width(attended)
    residual = tokens + sum(mm(v, w) for v, w in zip(attended_parts, output_parts))

    ffn_factor = rms_factor(residual)
    ffn_low = (residual * ffn_factor * ffn_gain).astype(bf16)
    ffn_all = gather_ctx(ffn_low)
    logits = mm(ffn_low, router_full)
    chosen = jnp.sum(jnp.where(chosen_hot, logits[:, None, :], 0.0), axis=-1)
    gate_share = jax.nn.softmax(chosen, axis=-1)
    gates_own = jnp.sum(jnp.where(chosen_hot, gate_share[..., None], 0.0), axis=1)
    gates_all = by_order(to_owner(gates_own.T))
    slot_gates = jnp.sum(pick.astype(f32) * gates_all[:, None, :], axis=-1).reshape(-1, 1)

    def pick_rows(blocks):
        chosen_rows = jnp.einsum("bst,btd->bsd", pick, blocks, preferred_element_type=f32)
        return chosen_rows.astype(bf16).reshape(ctx * slot_cap, width)

    def place_rows(values):
        return jnp.einsum(
            "bst,bsd->btd", pick, values.reshape(ctx, slot_cap, width), preferred_element_type=f32
        )

    entries = pick_rows(ffn_all)
    grad_rows = pick_rows(upstream_all)
    gate_pre = [mm(entries, w) for w in gate_parts]
    up_pre = [mm(entries, w) for w in up_parts]
    middle = [swiglu(g, u) for g, u in zip(gate_pre, up_pre)]
    expert_low = sum(mm_nt(m, w) for m, w in zip(middle, down_parts)).astype(bf16)
    ffn_flat = ffn_all.reshape(length, width)
    upstream_flat = upstream_all.reshape(length, width)
    shared_pre = mm(ffn_flat, shared_in)
    shared_gate_pre, shared_up_pre = shared_pre[:, :hidden_shared], shared_pre[:, hidden_shared:]
    shared_mid = swiglu(shared_gate_pre, shared_up_pre)

    expert_f32 = expert_low.astype(f32)
    slot_dgates = jnp.sum(grad_rows.astype(f32) * expert_f32, axis=-1).reshape(ctx, slot_cap)
    token_dgates = jnp.sum(pick.astype(f32) * slot_dgates[:, :, None], axis=1)
    grad_entries = (slot_gates * grad_rows.astype(f32)).astype(bf16)
    grad_middle = [mm(grad_entries, w) for w in down_parts]
    pairs = [swiglu_grads(g, u, d) for g, u, d in zip(gate_pre, up_pre, grad_middle)]
    entry_grad = sum(
        mm_nt(pair[0], g) + mm_nt(pair[1], u) for pair, g, u in zip(pairs, gate_parts, up_parts)
    ).astype(bf16)
    shared_grad_mid = mm_nt(upstream_flat, shared_back)
    shared_pair = jnp.concatenate(
        swiglu_grads(shared_gate_pre, shared_up_pre, shared_grad_mid), axis=-1
    )
    ffn_grad_part = mm_nt(shared_pair, shared_in).reshape(ctx, part, width) + place_rows(entry_grad)
    ffn_grad = scatter_ctx(ffn_grad_part.astype(bf16))
    dgates_own = to_owner(by_order(token_dgates)).T
    grad_gates = jnp.sum(jnp.where(chosen_hot, dgates_own[:, None, :], 0.0), axis=-1)

    scaled = (slot_gates * expert_f32).astype(bf16)
    out_part = mm(shared_mid, shared_back).reshape(ctx, part, width) + place_rows(scaled)
    hidden_out = (residual + scatter_ctx(out_part.astype(bf16))).astype(bf16)

    def sum_weight(left, rights):
        return scatter_fsdp([mm_tn(left, right) for right in rights])[None]

    grad_expert_down = sum_weight(grad_entries, middle)
    grad_expert_gate = sum_weight(entries, [pair[0] for pair in pairs])
    grad_expert_up = sum_weight(entries, [pair[1] for pair in pairs])
    down_rows = shared_down.shape[0]
    grad_back = mm_tn(shared_mid, upstream_flat).reshape(fsdp, down_rows, width)
    grad_shared_down = scatter_fsdp(in_fsdp_order([grad_back[i] for i in range(fsdp)]))
    grad_in = mm_tn(ffn_flat, shared_pair).reshape(ctx, fsdp, rows, 2 * hidden_shared)
    grad_in = scatter_fsdp(in_fsdp_order([grad_in[:, i] for i in range(fsdp)]))
    grad_in = to_owner(grad_in.astype(bf16)).astype(f32).transpose(1, 0, 2)
    grad_shared_gate = grad_in[..., :hidden_shared].reshape(rows, ctx * hidden_shared)
    grad_shared_up = grad_in[..., hidden_shared:].reshape(rows, ctx * hidden_shared)

    grad_chosen = gate_share * (
        grad_gates - jnp.sum(gate_share * grad_gates, axis=-1, keepdims=True)
    )
    grad_logits = jnp.sum(jnp.where(chosen_hot, grad_chosen[..., None], 0.0), axis=1).astype(bf16)
    grad_router = mm_tn(ffn_low, grad_logits)
    ffn_grad = ffn_grad + mm_nt(grad_logits, router_full)
    upstream = upstream_low.astype(f32)
    ffn_grad_in, grad_ffn_gain = rms_backward(residual, ffn_factor, ffn_gain, ffn_grad)
    grad_residual = upstream + ffn_grad_in
    grad_residual_low = grad_residual.astype(bf16)

    grad_attended = join_width([mm_nt(grad_residual_low, w) for w in output_parts]).astype(bf16)
    grad_head = to_heads(grad_attended.reshape(part, HEADS, VHEAD))
    grad_output = [
        mm_tn(v, grad_residual_low).reshape(ctx, rows, width) for v in attended_parts
    ]
    grad_output = scatter_ctx(scatter_fsdp(grad_output).astype(bf16))
    dquery, dkey, dvalue = attend_grad(
        query_pos, query_head, key_head, value_head, outcome, lse, grad_head
    )
    head_cos, head_sin = rope_tables(query_pos[:, 0])
    dquery = dquery * score_scale
    dquery = jnp.concatenate(
        [dquery[:, :NOPE], unrotate(dquery[:, NOPE:], head_cos, head_sin)], axis=-1
    ).astype(bf16)
    grad_query = from_heads(dquery).reshape(part, HEADS * QK)
    dkey = dkey * score_scale
    grad_expanded = jnp.concatenate([dkey[:, :NOPE], dvalue], axis=-1).astype(bf16)
    latent_part = jnp.concatenate([mm_nt(grad_expanded, expand), dkey[:, NOPE:]], axis=-1)
    latent_part = by_order(latent_part.reshape(ctx, part, KVR + ROPE).astype(bf16))
    latent_sum = scatter_ctx(latent_part)
    grad_expand = mm_tn(latent_all[:, :KVR], grad_expanded)
    grad_expand = grad_expand.reshape(ctx, fsdp, up_rows, NOPE + VHEAD)
    grad_expand = scatter_fsdp(in_fsdp_order([grad_expand[:, i] for i in range(fsdp)]))
    grad_expand = to_owner(grad_expand.astype(bf16)).astype(f32)
    grad_expand = grad_expand.reshape(HEADS, parts_of_head, up_rows, NOPE + VHEAD).sum(axis=1)
    grad_expand = grad_expand.transpose(1, 0, 2).reshape(up_rows, HEADS * (NOPE + VHEAD))
    grad_latent_raw, grad_kv_gain = rms_backward(
        latent_raw, kv_factor, kv_gain, latent_sum[:, :KVR]
    )
    grad_compressed = jnp.concatenate(
        [grad_latent_raw, unrotate(latent_sum[:, KVR:], cosine, sine)], axis=-1
    ).astype(bf16)
    grad_projected = jnp.concatenate([grad_query, grad_compressed], axis=-1)
    grad_normed = jnp.concatenate(
        [mm_nt(grad_projected, w[:, :columns]) for w in packed_parts], axis=-1
    )
    attn_grad_in, grad_attn_gain = rms_backward(tokens_split, attn_factor, attn_gain, grad_normed)
    attn_grad_in = join_width([attn_grad_in[:, i * span : (i + 1) * span] for i in range(fsdp)])
    grad_hidden_in = (grad_residual + attn_grad_in)[None]

    kv_rows = gain_kv.shape[0]
    grad_kv_rows = jnp.pad(
        grad_kv_gain.reshape(ctx * fsdp, kv_rows), ((0, 0), (0, rows - kv_rows))
    ).reshape(width, 1)
    grad_small = jnp.concatenate([grad_router, grad_ffn_gain[:, None], grad_kv_rows], axis=1)
    grad_small = [v.T for v in split_width(grad_small.T)]
    grad_packed = []
    for i in range(fsdp):
        pieces = [
            mm_tn(normed_parts[i], grad_projected).astype(bf16),
            grad_small[i].astype(bf16),
            grad_attn_gain[i * span : (i + 1) * span, None].astype(bf16),
            jnp.zeros((span, padding), bf16),
        ]
        grad_packed.append(jnp.concatenate(pieces, axis=1).reshape(ctx, rows, -1))
    grad_packed = scatter_ctx(scatter_fsdp(grad_packed).astype(bf16))
    after = columns + experts
    return (
        hidden_out[None],
        grad_hidden_in,
        grad_packed[:, after + 2],
        grad_packed[:, : HEADS * QK],
        grad_packed[:, HEADS * QK : columns],
        grad_packed[:kv_rows, after + 1],
        grad_expand,
        grad_output,
        grad_packed[:, after],
        grad_packed[:, columns:after],
        grad_shared_gate,
        grad_shared_up,
        grad_shared_down,
        grad_expert_gate,
        grad_expert_up,
        grad_expert_down,
    )


def solution(mesh):
    dense = P(("ctx", "fsdp"), None)
    gain = P(("ctx", "fsdp"))
    tokens = P("fsdp", "ctx", None)
    expert = P("ctx", None, "fsdp")
    return jax.shard_map(
        shards,
        mesh=mesh,
        in_specs=(
            tokens, gain, dense, dense, gain, dense, dense, gain, dense, dense, dense, dense,
            expert, expert, expert, tokens, tokens,
        ),
        out_specs=(
            tokens, tokens, gain, dense, dense, gain, dense, dense, gain, dense, dense, dense,
            dense, expert, expert, expert,
        ),
        check_vma=False,
    )
```

```python
import functools
import math

import jax
import jax.numpy as jnp
from jax import lax
from jax.experimental import pallas as pl
from jax.experimental.pallas import tpu as pltpu
from jax.sharding import PartitionSpec as P

HEADS = 16
NOPE = 128
ROPE = 64
VHEAD = 128
KVR = 512
TOP = 6
QK = NOPE + ROPE

epsilon = 1e-06
rope_base = 10000.0
masked_score = -1e30
score_scale = 1.0 / math.sqrt(QK)

bf16 = jnp.bfloat16
f32 = jnp.float32


def mm(left, right):
    return jnp.dot(left, right, preferred_element_type=f32)


def mm_nt(left, right):
    return lax.dot_general(left, right, (((1,), (1,)), ((), ())), preferred_element_type=f32)


def mm_tn(left, right):
    return lax.dot_general(left, right, (((0,), (0,)), ((), ())), preferred_element_type=f32)


def rms_factor(values):
    return lax.rsqrt(jnp.mean(values * values, axis=-1, keepdims=True) + epsilon)


def rms_backward(values, factor, gain, upstream):
    weighted = upstream * gain
    inner_mean = jnp.mean(weighted * values, axis=-1, keepdims=True)
    grad_in = factor * weighted - values * (factor * factor * factor) * inner_mean
    grad_gain = jnp.sum(upstream * values * factor, axis=0)
    return (grad_in, grad_gain)


def rope_tables(positions):
    half_width = ROPE // 2
    frequency = jnp.exp(jnp.arange(half_width, dtype=f32) * (-math.log(rope_base) / half_width))
    angles = positions.astype(f32)[:, None] * frequency[None, :]
    angles = jnp.concatenate([angles, angles], axis=-1)
    return (jnp.cos(angles), jnp.sin(angles))


def rotate(values, cosine, sine):
    half_width = values.shape[-1] // 2
    turned = jnp.concatenate([-values[..., half_width:], values[..., :half_width]], axis=-1)
    return values * cosine + turned * sine


def unrotate(upstream, cosine, sine):
    half_width = upstream.shape[-1] // 2
    rotated = upstream * sine
    turned = jnp.concatenate([rotated[..., half_width:], -rotated[..., :half_width]], axis=-1)
    return upstream * cosine + turned


def swiglu(gate_pre, up_pre):
    return (jax.nn.silu(gate_pre) * up_pre).astype(bf16)


def swiglu_grads(gate_pre, up_pre, grad_mid):
    squash = jax.nn.sigmoid(gate_pre)
    grad_gate = grad_mid * up_pre * squash * (1.0 + gate_pre * (1.0 - squash))
    grad_up = grad_mid * (gate_pre * squash)
    return (grad_gate.astype(bf16), grad_up.astype(bf16))


def exchanges():
    return lax.axis_size("ctx") == 16


def hop(value, mask):
    return lax.ppermute(value, "ctx", [(i, i ^ mask) for i in range(16)])


def gather_ctx(block):
    if not exchanges():
        return [(jnp.int32(0), lax.all_gather(block, "ctx", axis=0))]
    own = lax.axis_index("ctx")
    far = hop(block, 8)
    bases = [(block, hop(block, 4)), (far, hop(far, 4))]
    pieces = []
    for piece, pair in enumerate(bases):
        whole = jnp.zeros((8,) + block.shape, block.dtype)
        for high, middle in enumerate(pair):
            one, two = hop(middle, 1), hop(middle, 2)
            three = hop(one, 2) if high == piece else hop(two, 1)
            for mask, value in enumerate((middle, one, two, three)):
                place = (own ^ (4 * high + mask)) & 7
                whole = lax.dynamic_update_slice_in_dim(whole, value[None], place, 0)
        pieces.append(((own >> 3) ^ piece, whole))
    return pieces


def scatter_ctx(pieces):
    if not exchanges():
        return lax.psum_scatter(pieces[0].astype(bf16), "ctx", scatter_dimension=0).astype(f32)
    own = lax.axis_index("ctx")

    def block(mask):
        return lax.dynamic_index_in_dim(pieces[mask >> 3], (own ^ mask) & 7, 0, keepdims=False)

    def send(value, mask):
        return hop(value.astype(bf16), mask).astype(f32)

    def group(base):
        one, two = block(base ^ 1), block(base ^ 2)
        if base in (0, 12):
            one = one.astype(f32) + send(block(base ^ 3), 2)
        else:
            two = two.astype(f32) + send(block(base ^ 3), 1)
        return block(base).astype(f32) + send(one, 1) + send(two, 2)

    from_4 = send(group(4), 4)
    from_12 = send(group(12), 4)
    from_8 = send(group(8) + from_12, 8)
    return group(0) + from_4 + from_8


def halves(blocks):
    if not exchanges():
        return [blocks]
    half = lax.axis_index("ctx") >> 3
    return [lax.dynamic_slice_in_dim(blocks, (half ^ piece) * 8, 8, 0) for piece in (0, 1)]


def swap_cores(value):
    return lax.ppermute(value, "fsdp", [(0, 1), (1, 0)])


def gather_fsdp(block):
    if lax.axis_size("fsdp") == 2:
        return [block, swap_cores(block)]
    whole = lax.all_gather(block, "fsdp", axis=0)
    return [whole[i] for i in range(lax.axis_size("fsdp"))]


def scatter_fsdp(parts):
    if lax.axis_size("fsdp") == 2:
        return parts[0].astype(f32) + swap_cores(parts[1].astype(bf16)).astype(f32)
    stacked = jnp.stack([part.astype(bf16) for part in parts])
    return lax.psum_scatter(stacked, "fsdp", scatter_dimension=0).astype(f32)


def in_fsdp_order(parts):
    if lax.axis_size("fsdp") == 2:
        low = lax.axis_index("fsdp") == 0
        return [jnp.where(low, parts[0], parts[1]), jnp.where(low, parts[1], parts[0])]
    return parts


def to_owner(blocks):
    return lax.all_to_all(blocks, "ctx", split_axis=0, concat_axis=0, tiled=True)


LANES = 128
WIDE = NOPE + 2 * ROPE
megabytes = 1024 * 1024


def turn_columns(weights):
    half = weights.shape[-1] // 2
    return jnp.concatenate([-weights[..., half:], weights[..., :half]], axis=-1)


def project_kernel(
    base_ref, tokens_ref, gain_ref, kv_gain_ref, table_ref, query_w_ref, reduce_ref, expand_ref, *rest
):
    normed_ref, query_ref, key_ref, value_ref, latent_ref = rest[-5:]
    tokens = tokens_ref[...].astype(f32)
    normed = (tokens * rms_factor(tokens) * gain_ref[...]).astype(bf16)
    normed_ref[...] = normed
    table = table_ref[...]
    first_half = lax.broadcasted_iota(jnp.int32, table.shape, 1) < ROPE

    def rope(values):
        scaled = values * table
        return scaled + pltpu.roll(scaled, ROPE, 1)

    queries = mm(normed, query_w_ref[...])
    query_ref[:, :NOPE] = queries[:, :NOPE].astype(bf16)
    query_ref[:, NOPE:] = jnp.where(first_half, rope(queries[:, NOPE:]), 0.0).astype(bf16)
    compressed = mm(normed, reduce_ref[...])
    raw = compressed[:, :KVR]
    latent = (raw * rms_factor(raw) * kv_gain_ref[...]).astype(bf16)
    latent_ref[...] = latent
    expanded = mm(latent, expand_ref[...]).astype(bf16)
    key_ref[:, :NOPE] = expanded[:, :NOPE]
    key_ref[:, NOPE:] = rope(compressed[:, KVR:]).astype(bf16)
    value_ref[...] = expanded[:, NOPE:]


def project(pieces, gain, kv_gain, table, query_w, reduce_w, expand):
    length, width = table.shape[0], query_w.shape[0]
    tile = 256
    widths = [width, WIDE, WIDE, VHEAD, KVR]
    held = []
    for half, tokens in pieces:
        count = tokens.shape[0] * tokens.shape[1]
        steps = count // tile
        own = lambda i, base: (i, 0)
        at = lambda i, base, steps=steps: (base[0] * steps + i, 0)
        fixed = lambda i, base: (0, 0)
        whole = lambda shape: pl.BlockSpec(shape, fixed, pipeline_mode=pl.Buffered(1))
        held = pl.pallas_call(
            project_kernel,
            grid_spec=pltpu.PrefetchScalarGridSpec(
                num_scalar_prefetch=1,
                grid=(steps,),
                in_specs=[
                    pl.BlockSpec((tile, width), own),
                    whole((1, width)),
                    whole((1, KVR)),
                    pl.BlockSpec((tile, LANES), at),
                    whole((width, WIDE)),
                    whole((width, KVR + LANES)),
                    whole((KVR, NOPE + VHEAD)),
                ]
                + [pl.BlockSpec(memory_space=pl.ANY)] * len(held),
                out_specs=[pl.BlockSpec((tile, w), at) for w in widths],
            ),
            out_shape=[jax.ShapeDtypeStruct((length, w), bf16) for w in widths],
            input_output_aliases={8 + i: i for i in range(len(held))},
            compiler_params=pltpu.CompilerParams(vmem_limit_bytes=56 * megabytes),
            cost_estimate=pl.CostEstimate(
                flops=2 * count * width * (WIDE + KVR + LANES),
                bytes_accessed=4 * count * width + 2 * width * (WIDE + KVR + LANES),
                transcendentals=0,
            ),
            name="project",
        )(half[None], tokens.reshape(count, width), gain, kv_gain, table, query_w, reduce_w, expand, *held)
    return held


def attend_kernel(key_tile, reach, pos_ref, query_ref, key_ref, value_ref, out_ref, low_ref, lse_ref):
    queries = query_ref[...]
    rows = queries.shape[0]
    positions = pos_ref[...]
    tiles = (pl.program_id(0) + 1) * reach // key_tile

    def step(index, carry):
        top, total, running = carry
        keys = key_ref[pl.ds(index * key_tile, key_tile), :]
        values = value_ref[pl.ds(index * key_tile, key_tile), :]
        scores = mm_nt(queries, keys) * score_scale
        key_pos = index * key_tile + lax.broadcasted_iota(jnp.int32, scores.shape, 1)
        scores = jnp.where(key_pos <= positions, scores, masked_score)
        new_top = jnp.maximum(top, jnp.max(scores, axis=-1, keepdims=True))
        weights = jnp.exp(scores - new_top)
        shrink = jnp.exp(top - new_top)
        total = total * shrink + jnp.sum(weights, axis=-1, keepdims=True)
        running = running * shrink + mm(weights.astype(bf16), values)
        return (new_top, total, running)

    start = (
        jnp.full((rows, 1), masked_score, f32),
        jnp.zeros((rows, 1), f32),
        jnp.zeros((rows, VHEAD), f32),
    )
    top, total, running = lax.fori_loop(0, tiles, step, start)
    outcome = running / total
    out_ref[...] = outcome
    low_ref[...] = outcome.astype(bf16)
    lse_ref[...] = top + jnp.log(total)


def attend_grad_kernel(
    key_tile, reach, pos_ref, table_ref, query_ref, key_ref, value_ref, out_ref, lse_ref, grad_ref,
    expand_ref, dquery_ref, dexpand_ref, dlatent_ref, dkey_ref, dvalue_ref,
):
    @pl.when(pl.program_id(0) == 0)
    def clear():
        dkey_ref[...] = jnp.zeros_like(dkey_ref)
        dvalue_ref[...] = jnp.zeros_like(dvalue_ref)

    queries = query_ref[...]
    grads = grad_ref[...]
    positions = pos_ref[...]
    lse = lse_ref[...]
    delta = jnp.sum(grads.astype(f32) * out_ref[...], axis=-1, keepdims=True)
    tiles = (pl.program_id(0) + 1) * reach // key_tile

    def step(index, dquery):
        span = pl.ds(index * key_tile, key_tile)
        keys = key_ref[span, :]
        values = value_ref[span, :]
        scores = mm_nt(queries, keys) * score_scale
        key_pos = index * key_tile + lax.broadcasted_iota(jnp.int32, scores.shape, 1)
        probs = jnp.where(key_pos <= positions, jnp.exp(scores - lse), 0.0)
        dprobs = mm_nt(grads, values)
        dscores = (probs * (dprobs - delta)).astype(bf16)
        dvalue_ref[span, :] += mm_tn(probs.astype(bf16), grads)
        dkey_ref[span, :] += mm_tn(dscores, queries)
        return dquery + mm(dscores, keys)

    dquery = lax.fori_loop(0, tiles, step, jnp.zeros(queries.shape, f32)) * score_scale
    dquery_ref[:, :NOPE] = dquery[:, :NOPE].astype(bf16)
    dquery_ref[:, NOPE:] = (dquery[:, NOPE:] * table_ref[...]).astype(bf16)

    @pl.when(pl.program_id(0) == pl.num_programs(0) - 1)
    def finish():
        def rows(index, carry):
            span = pl.ds(index * key_tile, key_tile)
            dkey = dkey_ref[span, :] * score_scale
            low = jnp.concatenate([dkey[:, :NOPE], dvalue_ref[span, :]], axis=-1).astype(bf16)
            dexpand_ref[span, :] = low
            dlatent_ref[span, :KVR] = mm_nt(low, expand_ref[...]).astype(bf16)
            dlatent_ref[span, KVR:] = dkey[:, NOPE:].astype(bf16)
            return carry

        lax.fori_loop(0, dkey_ref.shape[0] // key_tile, rows, 0)


def attention_tiles(rows, keys):
    tile = min(512, keys)
    row_tile = rows * tile // keys
    return (row_tile, tile)


def attend(positions, queries, keys, values):
    rows, count = queries.shape[0], keys.shape[0]
    row_tile, tile = attention_tiles(rows, count)
    whole = lambda width: pl.BlockSpec((count, width), lambda i: (0, 0))
    part = lambda width: pl.BlockSpec((row_tile, width), lambda i: (i, 0))
    return pl.pallas_call(
        functools.partial(attend_kernel, tile, tile),
        grid=(rows // row_tile,),
        in_specs=[part(1), part(WIDE), whole(WIDE), whole(VHEAD)],
        out_specs=[part(VHEAD), part(VHEAD), part(1)],
        out_shape=[
            jax.ShapeDtypeStruct((rows, VHEAD), f32),
            jax.ShapeDtypeStruct((rows, VHEAD), bf16),
            jax.ShapeDtypeStruct((rows, 1), f32),
        ],
        compiler_params=pltpu.CompilerParams(vmem_limit_bytes=48 * megabytes),
        cost_estimate=pl.CostEstimate(
            flops=rows * count * (QK + VHEAD) * 2,
            bytes_accessed=4 * (rows + count) * (QK + VHEAD),
            transcendentals=rows * count // 2,
        ),
        name="attend",
    )(positions, queries, keys, values)


def attend_grad(positions, table, queries, keys, values, outcome, lse, grads, expand):
    rows, count = queries.shape[0], keys.shape[0]
    row_tile, tile = attention_tiles(rows, count)
    whole = lambda width: pl.BlockSpec((count, width), lambda i: (0, 0))
    part = lambda width: pl.BlockSpec((row_tile, width), lambda i: (i, 0))
    return pl.pallas_call(
        functools.partial(attend_grad_kernel, tile, tile),
        grid=(rows // row_tile,),
        in_specs=[
            part(1), part(LANES), part(WIDE), whole(WIDE), whole(VHEAD), part(VHEAD), part(1),
            part(VHEAD), pl.BlockSpec(expand.shape, lambda i: (0, 0)),
        ],
        out_specs=[part(WIDE), whole(NOPE + VHEAD), whole(KVR + LANES)],
        out_shape=[
            jax.ShapeDtypeStruct((rows, WIDE), bf16),
            jax.ShapeDtypeStruct((count, NOPE + VHEAD), bf16),
            jax.ShapeDtypeStruct((count, KVR + LANES), bf16),
        ],
        scratch_shapes=[pltpu.VMEM((count, WIDE), f32), pltpu.VMEM((count, VHEAD), f32)],
        compiler_params=pltpu.CompilerParams(vmem_limit_bytes=48 * megabytes),
        cost_estimate=pl.CostEstimate(
            flops=rows * count * (3 * QK + 2 * VHEAD) * 2,
            bytes_accessed=8 * (rows + count) * (QK + VHEAD),
            transcendentals=rows * count // 2,
        ),
        name="attend_grad",
    )(positions, table, queries, keys, values, outcome, lse, grads, expand)


def project_grad_kernel(
    base_ref, dquery_ref, dexpand_ref, normed_ref, latent_ref, query_w_ref, *rest
):
    dnormed_ref, dquery_w_ref, dexpand_w_ref = rest[-3:]
    first = pl.program_id(0) == 0
    if len(rest) == 5:
        query_sum, expand_sum = rest[0][...], rest[1][...]
    else:
        query_sum, expand_sum = 0.0, 0.0
    dquery = dquery_ref[...]
    dnormed_ref[...] = mm_nt(dquery, query_w_ref[...]).astype(bf16)
    query_add = mm_tn(normed_ref[...], dquery)
    expand_add = mm_tn(latent_ref[...], dexpand_ref[...])

    @pl.when(first)
    def start():
        dquery_w_ref[...] = query_sum + query_add
        dexpand_w_ref[...] = expand_sum + expand_add

    @pl.when(jnp.logical_not(first))
    def go_on():
        dquery_w_ref[...] += query_add
        dexpand_w_ref[...] += expand_add


def project_grad(order, count, dquery, dexpand, normed, latent, query_w):
    length, width = normed.shape
    tile = 256
    steps = count // tile
    pieces, sums = [], []
    for half in order:
        at = lambda i, base: (base[0] * steps + i, 0)
        fixed = lambda i, base: (0, 0)
        whole = lambda shape: pl.BlockSpec(shape, fixed, pipeline_mode=pl.Buffered(1))
        sum_shapes = [(width, WIDE), (KVR, NOPE + VHEAD)]
        piece, *sums = pl.pallas_call(
            project_grad_kernel,
            grid_spec=pltpu.PrefetchScalarGridSpec(
                num_scalar_prefetch=1,
                grid=(steps,),
                in_specs=[
                    pl.BlockSpec((tile, WIDE), at),
                    pl.BlockSpec((tile, NOPE + VHEAD), at),
                    pl.BlockSpec((tile, width), at),
                    pl.BlockSpec((tile, KVR), at),
                    whole((width, WIDE)),
                ]
                + [whole(shape) for shape in sum_shapes[: len(sums)]],
                out_specs=[pl.BlockSpec((tile, width), lambda i, base: (i, 0))]
                + [pl.BlockSpec(shape, fixed) for shape in sum_shapes],
            ),
            out_shape=[jax.ShapeDtypeStruct((count, width), bf16)]
            + [jax.ShapeDtypeStruct(shape, f32) for shape in sum_shapes],
            compiler_params=pltpu.CompilerParams(vmem_limit_bytes=56 * megabytes),
            cost_estimate=pl.CostEstimate(
                flops=4 * count * (width + KVR) * WIDE,
                bytes_accessed=4 * count * width,
                transcendentals=0,
            ),
            name="project_grad",
        )(half[None], dquery, dexpand, normed, latent, query_w, *sums)
        pieces.append(piece)
    return pieces, sums


def experts_kernel(parts, group, base_ref, *refs):
    ffn_ref, up_ref, pick_ref, gates_ref = refs[:4]
    gate_refs, rise_refs, down_refs = (refs[4 + i * parts : 4 + (i + 1) * parts] for i in range(3))
    sgate_ref, sup_ref, sdown_ref = refs[4 + 3 * parts : 7 + 3 * parts]
    outs = refs[-(7 + 3 * parts) :]
    out_ref, db_ref, entries_ref, dy_ref, dgate_ref, mid_ref, pair_ref = outs[:7]
    m_refs, dg_refs, du_refs = (outs[7 + i * parts : 7 + (i + 1) * parts] for i in range(3))
    slots = pick_ref.shape[1]
    hidden = mid_ref.shape[-1]

    for block in range(group):
        span = pl.ds(block * slots, slots)
        pick = pick_ref[block]
        entries_ref[span, :] = mm(pick, ffn_ref[block]).astype(bf16)
        dy_ref[span, :] = mm(pick, up_ref[block]).astype(bf16)
    gates = jnp.concatenate(
        [
            jnp.sum(pick_ref[b].astype(f32) * gates_ref[b], axis=-1, keepdims=True)
            for b in range(group)
        ],
        axis=0,
    )
    entries = entries_ref[...]
    grad_rows = dy_ref[...]
    dy = (gates * grad_rows.astype(f32)).astype(bf16)
    y = jnp.zeros(entries.shape, f32)
    for p in range(parts):
        gate = mm(entries, gate_refs[p][...])
        rise = mm(entries, rise_refs[p][...])
        middle = swiglu(gate, rise)
        m_refs[p][...] = middle
        y = y + mm_nt(middle, down_refs[p][...])
        dm = mm(dy, down_refs[p][...])
        dg, du = swiglu_grads(gate, rise, dm)
        dg_refs[p][...] = dg
        du_refs[p][...] = du
    y = y.astype(bf16).astype(f32)
    dgates = jnp.sum(grad_rows.astype(f32) * y, axis=-1, keepdims=True)
    scaled = (gates * y).astype(bf16)
    dy_ref[...] = dy
    db = jnp.zeros(entries.shape, f32)
    for p in range(parts):
        db = db + mm_nt(dg_refs[p][...], gate_refs[p][...])
        db = db + mm_nt(du_refs[p][...], rise_refs[p][...])
    db = db.astype(bf16)
    for block in range(group):
        pick = pick_ref[block]
        span = slice(block * slots, (block + 1) * slots)
        dgate_ref[block] = jnp.sum(pick.astype(f32) * dgates[span], axis=0, keepdims=True)
        tokens = ffn_ref[block]
        upstream = up_ref[block]
        sgate = mm(tokens, sgate_ref[...])
        sup = mm(tokens, sup_ref[...])
        middle = swiglu(sgate, sup)
        mid_ref[block] = middle
        dsg, dsu = swiglu_grads(sgate, sup, mm_nt(upstream, sdown_ref[...]))
        pair_ref[block, 0] = dsg
        pair_ref[block, 1] = dsu
        out_ref[block] = (mm(middle, sdown_ref[...]) + mm_tn(pick, scaled[span])).astype(bf16)
        db_ref[block] = (
            mm_nt(dsg, sgate_ref[...]) + mm_nt(dsu, sup_ref[...]) + mm_tn(pick, db[span])
        ).astype(bf16)


def expert_layers(pieces, upstream, pick, gates, gate_w, up_w, down_w, sgate, sup, sdown):
    ctx, slots, part = pick.shape
    width, hidden = sgate.shape
    parts = len(gate_w)
    group = max(1, 512 // part)
    outs, dbs, held = [], [], []
    inner = [w.shape[1] for w in gate_w]
    for half, tokens in pieces:
        blocks = tokens.shape[0]
        steps = blocks // group
        own3 = lambda i, base: (i, 0, 0)
        at2 = lambda i, base, steps=steps: (base[0] * steps + i, 0)
        at3 = lambda i, base, steps=steps: (base[0] * steps + i, 0, 0)
        at4 = lambda i, base, steps=steps: (base[0] * steps + i, 0, 0, 0)
        fixed = lambda i, base: (0, 0)
        weights = [*gate_w, *up_w, *down_w, sgate, sup, sdown]
        held_specs = [
            pl.BlockSpec((group * slots, width), at2),
            pl.BlockSpec((group * slots, width), at2),
            pl.BlockSpec((group, 1, part), at3),
            pl.BlockSpec((group, part, hidden), at3),
            pl.BlockSpec((group, 2, part, hidden), at4),
        ] + [pl.BlockSpec((group * slots, w), at2) for w in inner * 3]
        held_shapes = [
            jax.ShapeDtypeStruct((ctx * slots, width), bf16),
            jax.ShapeDtypeStruct((ctx * slots, width), bf16),
            jax.ShapeDtypeStruct((ctx, 1, part), f32),
            jax.ShapeDtypeStruct((ctx, part, hidden), bf16),
            jax.ShapeDtypeStruct((ctx, 2, part, hidden), bf16),
        ] + [jax.ShapeDtypeStruct((ctx * slots, w), bf16) for w in inner * 3]
        count = blocks * slots
        out, db, *held = pl.pallas_call(
            functools.partial(experts_kernel, parts, group),
            grid_spec=pltpu.PrefetchScalarGridSpec(
                num_scalar_prefetch=1,
                grid=(steps,),
                in_specs=[
                    pl.BlockSpec((group, part, width), own3),
                    pl.BlockSpec((group, part, width), at3),
                    pl.BlockSpec((group, slots, part), at3),
                    pl.BlockSpec((group, 1, part), at3),
                ]
                + [pl.BlockSpec(w.shape, fixed, pipeline_mode=pl.Buffered(1)) for w in weights]
                + [pl.BlockSpec(memory_space=pl.ANY)] * len(held),
                out_specs=[pl.BlockSpec((group, part, width), own3)] * 2 + held_specs,
            ),
            out_shape=[jax.ShapeDtypeStruct((blocks, part, width), bf16)] * 2 + held_shapes,
            input_output_aliases={5 + len(weights) + i: 2 + i for i in range(len(held))},
            compiler_params=pltpu.CompilerParams(vmem_limit_bytes=60 * megabytes),
            cost_estimate=pl.CostEstimate(
                flops=12 * count * width * sum(inner) + 12 * blocks * part * width * hidden,
                bytes_accessed=8 * blocks * part * width + 6 * width * sum(inner),
                transcendentals=count * sum(inner),
            ),
            name="expert_layers",
        )(half[None], tokens, upstream, pick, gates, *weights, *held)
        outs.append(out)
        dbs.append(db)
    entries, dy, dgates, mid, pair = held[:5]
    middles, dgs, dus = (held[5 + i * parts : 5 + (i + 1) * parts] for i in range(3))
    return outs, dbs, entries, dy, dgates[:, 0], mid, pair, middles, dgs, dus


def shards(
    hidden_in, gain_attn, w_query, w_kv_down, gain_kv, w_kv_up, w_out, gain_ffn, w_router,
    shared_gate, shared_up, shared_down, expert_gate, expert_up, expert_down, routes, cotangent,
):
    part, width = hidden_in.shape[1:]
    ctx, fsdp = lax.axis_size("ctx"), lax.axis_size("fsdp")
    ctx_rank = lax.axis_index("ctx")
    length = part * ctx
    rows = w_query.shape[0]
    experts = w_router.shape[1]
    parts_of_head = ctx // HEADS
    query_part = part // parts_of_head
    first_row = (ctx_rank % parts_of_head) * query_part
    everywhere = ("ctx", "fsdp")

    def to_columns(values):
        blocks = to_owner(values)
        return jnp.stack(in_fsdp_order(gather_fsdp(blocks)), axis=1).reshape(-1, values.shape[-1])

    def to_rows(columns, count):
        grid = columns.reshape(ctx, fsdp, count, columns.shape[-1])
        grid = scatter_fsdp(in_fsdp_order([grid[:, i] for i in range(fsdp)]))
        return to_owner(grid.astype(bf16)).astype(f32)

    def head_blocks(values):
        blocks = values.reshape(values.shape[0], HEADS, -1).transpose(1, 0, 2)
        return jnp.repeat(blocks, parts_of_head, axis=0)

    def from_head_blocks(blocks):
        blocks = blocks.reshape(HEADS, parts_of_head, *blocks.shape[1:]).sum(axis=1)
        return blocks.transpose(1, 0, 2).reshape(blocks.shape[1], -1)

    compressed_width = KVR + ROPE
    turned_width = compressed_width + ROPE
    kv_rows = gain_kv.shape[0]
    small_width = turned_width + experts + 3
    small = jnp.concatenate(
        [
            w_kv_down,
            turn_columns(w_kv_down[:, KVR:]),
            w_router,
            gain_attn[:, None],
            gain_ffn[:, None],
            jnp.pad(gain_kv, (0, rows - kv_rows))[:, None],
            jnp.zeros((rows, -small_width % 128), bf16),
        ],
        axis=1,
    )
    small_full = lax.all_gather(small, everywhere, axis=0, tiled=True)
    reduce_full = small_full[:, :compressed_width]
    router_full = small_full[:, turned_width : small_width - 3]
    attn_gain = small_full[:, small_width - 3].astype(f32)
    ffn_gain = small_full[:, small_width - 2].astype(f32)
    kv_gain = small_full[:, small_width - 1].reshape(ctx * fsdp, rows)[:, :kv_rows]
    kv_gain = kv_gain.reshape(KVR).astype(f32)

    tokens_low = hidden_in.reshape(part, width)
    upstream_low = cotangent.reshape(part, width)
    tokens_all = gather_ctx(tokens_low)
    query_blocks = head_blocks(w_query)
    query_blocks = jnp.concatenate([query_blocks, turn_columns(query_blocks[..., NOPE:])], axis=-1)
    query_w = to_columns(query_blocks)
    expand = to_columns(head_blocks(w_kv_up))
    output_full = lax.all_gather(w_out, everywhere, axis=0, tiled=True)
    upstream_late, _ = lax.optimization_barrier((upstream_low, tokens_all[-1][1]))
    upstream_all = lax.all_gather(upstream_late, "ctx", axis=0)

    hidden_shared = shared_gate.shape[1] // ctx
    shared_blocks = jnp.concatenate(
        [
            shared_gate.reshape(rows, ctx, hidden_shared),
            shared_up.reshape(rows, ctx, hidden_shared),
        ],
        axis=2,
    ).transpose(1, 0, 2)
    shared_in = to_columns(shared_blocks)
    shared_in = (shared_in[:, :hidden_shared], shared_in[:, hidden_shared:])
    shared_back = jnp.concatenate(in_fsdp_order(gather_fsdp(shared_down)), axis=0)
    gate_parts = gather_fsdp(expert_gate[0])
    up_parts = gather_fsdp(expert_up[0])
    down_parts = gather_fsdp(expert_down[0])

    slot_cap = min(part, part * TOP * 4 // (3 * experts))
    route_rows = routes.reshape(part, TOP)
    chosen_hot = route_rows[:, :, None] == jnp.arange(experts, dtype=jnp.int32)[None, None, :]
    named = jnp.any(chosen_hot, axis=1).astype(bf16)
    named_all = to_owner(named.T)
    until = jnp.arange(part)[:, None] <= jnp.arange(part)[None, :]
    ordinal = mm(named_all, until.astype(bf16)) - 1.0
    slots = jnp.arange(slot_cap, dtype=f32)[None, :, None]
    pick = ((ordinal[:, None, :] == slots) & (named_all[:, None, :] > 0)).astype(bf16)

    cosine, sine = rope_tables(jnp.arange(length, dtype=jnp.int32))
    table = jnp.concatenate([cosine, sine], axis=-1)
    normed_all, query_all, key_head, value_head, latent_all = project(
        tokens_all, attn_gain[None], kv_gain[None], table, query_w, small_full, expand
    )

    def query_rows(values):
        if parts_of_head == 1:
            return values
        blocks = values.reshape(ctx, part, values.shape[-1])
        blocks = lax.dynamic_slice_in_dim(blocks, first_row, query_part, 1)
        return blocks.reshape(ctx * query_part, values.shape[-1])

    def all_rows(values):
        if parts_of_head == 1:
            return values.reshape(ctx, part, values.shape[-1])
        blocks = values.reshape(ctx, query_part, values.shape[-1])
        start = jnp.zeros((ctx, part, values.shape[-1]), values.dtype)
        return lax.dynamic_update_slice_in_dim(start, blocks, first_row, 1)

    query_head = query_rows(query_all)

    def to_heads(values):
        split = values.reshape(parts_of_head, query_part, HEADS, values.shape[-1])
        sent = split.transpose(2, 0, 1, 3).reshape(ctx, query_part, values.shape[-1])
        return to_owner(sent).reshape(ctx * query_part, values.shape[-1])

    def from_heads(values):
        back = to_owner(values.reshape(ctx, query_part, values.shape[-1]))
        back = back.reshape(HEADS, parts_of_head, query_part, values.shape[-1])
        return back.transpose(1, 2, 0, 3).reshape(part, HEADS, values.shape[-1])

    query_pos = query_rows(jnp.arange(length, dtype=jnp.int32)[:, None])
    outcome, outcome_low, lse = attend(query_pos, query_head, key_head, value_head)
    attended = from_heads(outcome_low).reshape(part, HEADS * VHEAD)
    tokens = tokens_low.astype(f32)
    residual = tokens + mm(attended, output_full)

    ffn_factor = rms_factor(residual)
    ffn_low = (residual * ffn_factor * ffn_gain).astype(bf16)
    ffn_all = gather_ctx(ffn_low)
    logits = mm(ffn_low, router_full)
    chosen = jnp.sum(jnp.where(chosen_hot, logits[:, None, :], 0.0), axis=-1)
    gate_share = jax.nn.softmax(chosen, axis=-1)
    gates_own = jnp.sum(jnp.where(chosen_hot, gate_share[..., None], 0.0), axis=1)
    gates_all = to_owner(gates_own.T)
    out_parts, grad_parts, entries, grad_entries, token_dgates, shared_mid, shared_pair, *hidden = (
        expert_layers(
            ffn_all, upstream_all, pick, gates_all[:, None, :], gate_parts, up_parts, down_parts,
            *shared_in, shared_back,
        )
    )
    middle, gate_low, up_low = hidden
    ffn_grad = scatter_ctx(grad_parts)
    dgates_own = to_owner(token_dgates).T
    grad_gates = jnp.sum(jnp.where(chosen_hot, dgates_own[:, None, :], 0.0), axis=-1)
    out_parts, _ = lax.optimization_barrier((out_parts, ffn_grad))
    hidden_out = (residual + scatter_ctx(out_parts)).astype(bf16)

    def sum_weight(left, rights):
        return scatter_fsdp([mm_tn(left, right) for right in rights])[None]

    grad_expert_down = sum_weight(grad_entries, middle)
    grad_expert_gate = sum_weight(entries, gate_low)
    grad_expert_up = sum_weight(entries, up_low)
    down_rows = shared_down.shape[0]
    shared_mid = shared_mid.reshape(length, hidden_shared)
    upstream_flat = upstream_all.reshape(length, width)
    grad_back = mm_tn(shared_mid, upstream_flat).reshape(fsdp, down_rows, width)
    grad_shared_down = scatter_fsdp(in_fsdp_order([grad_back[i] for i in range(fsdp)]))
    grad_in = sum(
        jnp.einsum(
            "btd,bgtf->dgf",
            blocks,
            lax.dynamic_slice_in_dim(shared_pair, half * blocks.shape[0], blocks.shape[0], 0),
            preferred_element_type=f32,
        )
        for half, blocks in ffn_all
    ).reshape(width, 2 * hidden_shared)
    grad_in = to_rows(grad_in, rows).transpose(1, 0, 2)
    grad_shared_gate = grad_in[..., :hidden_shared].reshape(rows, ctx * hidden_shared)
    grad_shared_up = grad_in[..., hidden_shared:].reshape(rows, ctx * hidden_shared)

    grad_chosen = gate_share * (
        grad_gates - jnp.sum(gate_share * grad_gates, axis=-1, keepdims=True)
    )
    grad_logits = jnp.sum(jnp.where(chosen_hot, grad_chosen[..., None], 0.0), axis=1).astype(bf16)
    grad_router = mm_tn(ffn_low, grad_logits)
    ffn_grad = ffn_grad + mm_nt(grad_logits, router_full)
    upstream = upstream_low.astype(f32)
    ffn_grad_in, grad_ffn_gain = rms_backward(residual, ffn_factor, ffn_gain, ffn_grad)
    grad_residual = upstream + ffn_grad_in
    grad_residual_low = grad_residual.astype(bf16)

    grad_attended = mm_nt(grad_residual_low, output_full).astype(bf16)
    grad_head = to_heads(grad_attended.reshape(part, HEADS, VHEAD))
    grad_output = lax.psum_scatter(
        mm_tn(attended, grad_residual_low).astype(bf16), everywhere, scatter_dimension=0, tiled=True
    ).astype(f32)
    grad_query, grad_expanded, latent_part = attend_grad(
        query_pos, query_rows(table), query_head, key_head, value_head, outcome, lse, grad_head, expand
    )
    latent_sum = scatter_ctx(halves(latent_part.reshape(ctx, part, KVR + LANES)))
    order = [half for half, _ in tokens_all]
    normed_parts, (grad_query_w, grad_expand) = project_grad(
        order, length // len(order), all_rows(grad_query).reshape(length, WIDE), grad_expanded,
        normed_all, latent_all, query_w,
    )
    grad_normed = scatter_ctx([v.reshape(-1, part, width) for v in normed_parts])

    own_rows = ctx_rank * part
    own_normed = lax.dynamic_slice_in_dim(normed_all, own_rows, part, 0)
    latent_raw = mm(own_normed, reduce_full[:, :KVR])
    grad_latent_raw, _ = rms_backward(
        latent_raw, rms_factor(latent_raw), kv_gain, latent_sum[:, :KVR]
    )
    own_cos = lax.dynamic_slice_in_dim(cosine, own_rows, part, 0)
    own_sin = lax.dynamic_slice_in_dim(sine, own_rows, part, 0)
    grad_compressed = jnp.concatenate(
        [grad_latent_raw, unrotate(latent_sum[:, KVR:compressed_width], own_cos, own_sin)], axis=-1
    ).astype(bf16)
    grad_small = jnp.concatenate(
        [
            mm_tn(own_normed, grad_compressed).astype(bf16),
            jnp.zeros((width, ROPE), bf16),
            grad_router.astype(bf16),
            grad_ffn_gain[:, None].astype(bf16),
            jnp.zeros((width, small.shape[1] - small_width + 2), bf16),
        ],
        axis=1,
    ).reshape(ctx, fsdp, rows, small.shape[1])
    grad_small = scatter_fsdp(in_fsdp_order([grad_small[:, i] for i in range(fsdp)]))
    grad_small = scatter_ctx(halves(grad_small.astype(bf16)))
    grad_reduce = grad_small[:, :compressed_width]
    turned = grad_query_w[:, QK:]
    turned = jnp.concatenate([turned[:, ROPE // 2 :], -turned[:, : ROPE // 2]], axis=-1)
    grad_query_w = jnp.concatenate(
        [grad_query_w[:, :NOPE], grad_query_w[:, NOPE:QK] + turned], axis=-1
    )
    grad_query_w = from_head_blocks(to_rows(grad_query_w, rows))
    grad_expand = from_head_blocks(to_rows(grad_expand, kv_rows))

    grad_normed = grad_normed + mm_nt(grad_compressed, reduce_full)
    attn_grad_in, _ = rms_backward(tokens, rms_factor(tokens), attn_gain, grad_normed)
    grad_hidden_in = (grad_residual + attn_grad_in)[None]

    def gain_grad(gain, pairs):
        total = sum(jnp.sum(w.astype(f32) * g, axis=-1) for w, g in pairs)
        return total / gain.astype(f32)

    grad_attn_gain = gain_grad(gain_attn, [(w_query, grad_query_w), (w_kv_down, grad_reduce)])
    grad_kv_gain = gain_grad(gain_kv, [(w_kv_up, grad_expand)])
    after = turned_width + experts
    return (
        hidden_out[None],
        grad_hidden_in,
        grad_attn_gain,
        grad_query_w,
        grad_reduce,
        grad_kv_gain,
        grad_expand,
        grad_output,
        grad_small[:, after],
        grad_small[:, turned_width:after],
        grad_shared_gate,
        grad_shared_up,
        grad_shared_down,
        grad_expert_gate,
        grad_expert_up,
        grad_expert_down,
    )


def solution(mesh):
    dense = P(("ctx", "fsdp"), None)
    gain = P(("ctx", "fsdp"))
    tokens = P("fsdp", "ctx", None)
    expert = P("ctx", None, "fsdp")
    return jax.shard_map(
        shards,
        mesh=mesh,
        in_specs=(
            tokens, gain, dense, dense, gain, dense, dense, gain, dense, dense, dense, dense,
            expert, expert, expert, tokens, tokens,
        ),
        out_specs=(
            tokens, tokens, gain, dense, dense, gain, dense, dense, gain, dense, dense, dense,
            dense, expert, expert, expert,
        ),
        check_vma=False,
    )
```

```python
import functools
import math

import jax
import jax.numpy as jnp
from jax import lax
from jax.experimental import pallas as pl
from jax.experimental.pallas import tpu as pltpu
from jax.sharding import PartitionSpec as P

HEADS = 16
NOPE = 128
ROPE = 64
VHEAD = 128
KVR = 512
TOP = 6
QK = NOPE + ROPE

epsilon = 1e-06
rope_base = 10000.0
masked_score = -1e30
score_scale = 1.0 / math.sqrt(QK)

bf16 = jnp.bfloat16
f32 = jnp.float32


def mm(left, right):
    return jnp.dot(left, right, preferred_element_type=f32)


def mm_nt(left, right):
    return lax.dot_general(left, right, (((1,), (1,)), ((), ())), preferred_element_type=f32)


def mm_tn(left, right):
    return lax.dot_general(left, right, (((0,), (0,)), ((), ())), preferred_element_type=f32)


def rms_factor(values):
    return lax.rsqrt(jnp.mean(values * values, axis=-1, keepdims=True) + epsilon)


def rms_backward(values, factor, gain, upstream):
    weighted = upstream * gain
    inner_mean = jnp.mean(weighted * values, axis=-1, keepdims=True)
    grad_in = factor * weighted - values * (factor * factor * factor) * inner_mean
    grad_gain = jnp.sum(upstream * values * factor, axis=0)
    return (grad_in, grad_gain)


def rope_tables(positions):
    half_width = ROPE // 2
    frequency = jnp.exp(jnp.arange(half_width, dtype=f32) * (-math.log(rope_base) / half_width))
    angles = positions.astype(f32)[:, None] * frequency[None, :]
    angles = jnp.concatenate([angles, angles], axis=-1)
    return (jnp.cos(angles), jnp.sin(angles))


def rotate(values, cosine, sine):
    half_width = values.shape[-1] // 2
    turned = jnp.concatenate([-values[..., half_width:], values[..., :half_width]], axis=-1)
    return values * cosine + turned * sine


def unrotate(upstream, cosine, sine):
    half_width = upstream.shape[-1] // 2
    rotated = upstream * sine
    turned = jnp.concatenate([rotated[..., half_width:], -rotated[..., :half_width]], axis=-1)
    return upstream * cosine + turned


def swiglu(gate_pre, up_pre):
    return (jax.nn.silu(gate_pre) * up_pre).astype(bf16)


def swiglu_grads(gate_pre, up_pre, grad_mid):
    squash = jax.nn.sigmoid(gate_pre)
    grad_gate = grad_mid * up_pre * squash * (1.0 + gate_pre * (1.0 - squash))
    grad_up = grad_mid * (gate_pre * squash)
    return (grad_gate.astype(bf16), grad_up.astype(bf16))


def exchanges():
    return lax.axis_size("ctx") == 16


def hop(value, mask):
    return lax.ppermute(value, "ctx", [(i, i ^ mask) for i in range(16)])


def together(*values):
    return lax.optimization_barrier(values)


def gather_ctx(block, *stages):
    held = None
    if not exchanges():
        for stage in stages:
            held = stage(held)
        whole = lax.all_gather(block, "ctx", axis=0)
        at = lambda piece, mask: [(whole, 8 * piece + 4 * group + mask) for group in (0, 1)]
        return [[at(piece, mask) for mask in range(4)] for piece in range(whole.shape[0] // 8)], held

    def end(number, *hops):
        nonlocal held
        if number < len(stages):
            held = stages[number](held)
        held, *hops = together(held, *hops)
        return hops

    near, far, one, two = end(0, *(hop(block, mask) for mask in (4, 8, 1, 2)))
    far_near, near_one, near_two, three = end(
        1, hop(far, 4), hop(near, 1), hop(near, 2), hop(two, 1)
    )
    pair = jnp.stack([far, far_near])
    near_three, far_one, far_two = end(2, hop(three, 4), hop(pair, 1), hop(pair, 2))
    far_three = end(3, hop(far_two[0], 1), hop(far_one[1], 2))
    pairs = [(block, near), (one, near_one), (two, near_two), (three, near_three)]
    alone = lambda values: [(value[None], 0) for value in values]
    both = lambda values: [(values, 0), (values, 1)]
    return [
        [alone(values) for values in pairs],
        [both(pair), both(far_one), both(far_two), alone(far_three)],
    ], held


def block_operands(piece):
    blocks = [block for mask in piece for block in mask]
    specs = [
        pl.BlockSpec(
            (1, *array.shape[1:]), lambda i, base, at=at: (at, 0, 0), pipeline_mode=pl.Buffered(1)
        )
        for array, at in blocks
    ]
    return [array for array, _ in blocks], specs


def block_of_step(refs, mask):
    return jnp.where(pl.program_id(0) == 0, refs[2 * mask][0], refs[2 * mask + 1][0])


def plus(*values):
    return sum(value.astype(f32) for value in values)


def plane_hops(pieces):
    return [[hop(value, mask) for mask, value in enumerate(piece) if mask] for piece in pieces]


def line_hops(pieces, arrived):
    near, far = (plus(piece[0], *values) for piece, values in zip(pieces, arrived))
    sent = ((near[1], 4), (far[0], 8), (far[1], 12))
    return near[0], [hop(value.astype(bf16), mask) for value, mask in sent]


def whole_sum(pieces):
    whole = jnp.stack([jnp.stack(piece, axis=1) for piece in pieces])
    whole = whole.reshape(-1, *whole.shape[3:])
    return lax.psum_scatter(whole, "ctx", scatter_dimension=0).astype(f32)


def scatter_ctx(pieces, beside_plane=(), beside_line=(), near=None):
    if not exchanges():
        return whole_sum(pieces), beside_plane, beside_line
    near = near or plane_hops(pieces[:1])
    near, far, beside_plane = together(near, plane_hops(pieces[1:]), beside_plane)
    own, arrived = line_hops(pieces, [*near, *far])
    arrived, beside_line = together(arrived, beside_line)
    return plus(own, *arrived), beside_plane, beside_line


def piece_place(piece):
    if not exchanges():
        return jnp.array([piece, 0, 0], jnp.int32)
    own = lax.axis_index("ctx")
    return jnp.stack([(own >> 3) ^ piece, own & 3, (own >> 2) & 1])


def piece_order():
    masks = [p * 8 + g * 4 + m for p in (0, 1) for m in range(4) for g in (0, 1)]
    return jnp.array(masks, jnp.int32) ^ lax.axis_index("ctx")


def in_pieces(blocks):
    if not exchanges():
        groups = blocks.reshape(-1, 2, 4, *blocks.shape[1:])
        return [[piece[:, mask] for mask in range(4)] for piece in groups]
    ordered = jnp.take(blocks, piece_order(), axis=0, mode="clip")
    ordered = ordered.reshape(2, 4, 2, *blocks.shape[1:])
    return [[ordered[p, m] for m in range(4)] for p in (0, 1)]


def swap_cores(value):
    return lax.ppermute(value, "fsdp", [(0, 1), (1, 0)])


def gather_fsdp(block):
    if lax.axis_size("fsdp") == 2:
        return [block, swap_cores(block)]
    whole = lax.all_gather(block, "fsdp", axis=0)
    return [whole[i] for i in range(lax.axis_size("fsdp"))]


def scatter_fsdp(parts):
    if lax.axis_size("fsdp") == 2:
        return parts[0].astype(f32) + swap_cores(parts[1].astype(bf16)).astype(f32)
    stacked = jnp.stack([part.astype(bf16) for part in parts])
    return lax.psum_scatter(stacked, "fsdp", scatter_dimension=0).astype(f32)


def in_fsdp_order(parts):
    if lax.axis_size("fsdp") == 2:
        low = lax.axis_index("fsdp") == 0
        return [jnp.where(low, parts[0], parts[1]), jnp.where(low, parts[1], parts[0])]
    return parts


def to_owner(blocks):
    return lax.all_to_all(blocks, "ctx", split_axis=0, concat_axis=0, tiled=True)


LANES = 128
WIDE = NOPE + 2 * ROPE
megabytes = 1024 * 1024


def turn_columns(weights):
    half = weights.shape[-1] // 2
    return jnp.concatenate([-weights[..., half:], weights[..., :half]], axis=-1)


def project_kernel(base_ref, *refs):
    token_refs = refs[:8]
    gain_ref, kv_gain_ref, table_ref, query_w_ref, reduce_ref, expand_ref = refs[8:14]
    normed_ref, query_ref, key_ref, value_ref, latent_ref = refs[-5:]
    part = token_refs[0].shape[1]
    first_half = lax.broadcasted_iota(jnp.int32, (part, LANES), 1) < ROPE
    for mask in range(4):
        span = pl.ds(pl.multiple_of((mask ^ base_ref[1]) * part, part), part)
        tokens = block_of_step(token_refs, mask).astype(f32)
        normed = (tokens * rms_factor(tokens) * gain_ref[...]).astype(bf16)
        normed_ref[span, :] = normed
        table = table_ref[span, :]

        def rope(values):
            scaled = values * table
            return scaled + pltpu.roll(scaled, ROPE, 1)

        queries = mm(normed, query_w_ref[...])
        query_ref[span, :NOPE] = queries[:, :NOPE].astype(bf16)
        query_ref[span, NOPE:] = jnp.where(first_half, rope(queries[:, NOPE:]), 0.0).astype(bf16)
        compressed = mm(normed, reduce_ref[...])
        raw = compressed[:, :KVR]
        latent = (raw * rms_factor(raw) * kv_gain_ref[...]).astype(bf16)
        latent_ref[span, :] = latent
        expanded = mm(latent, expand_ref[...]).astype(bf16)
        key_ref[span, :NOPE] = expanded[:, :NOPE]
        key_ref[span, NOPE:] = rope(compressed[:, KVR:]).astype(bf16)
        value_ref[span, :] = expanded[:, NOPE:]


def project(pieces, gain, kv_gain, table, query_w, reduce_w, expand):
    length, width = table.shape[0], query_w.shape[0]
    widths = [width, WIDE, WIDE, VHEAD, KVR]
    held = []
    for piece, blocks in enumerate(pieces):
        blocks, block_specs = block_operands(blocks)
        steps, part = 2, blocks[0].shape[1]
        tile = 4 * part
        at = lambda i, base: (base[0] * 2 + (i ^ base[2]), 0)
        fixed = lambda i, base: (0, 0)
        whole = lambda shape: pl.BlockSpec(shape, fixed, pipeline_mode=pl.Buffered(1))
        count = steps * tile
        held = pl.pallas_call(
            project_kernel,
            grid_spec=pltpu.PrefetchScalarGridSpec(
                num_scalar_prefetch=1,
                grid=(steps,),
                in_specs=block_specs
                + [
                    whole((1, width)),
                    whole((1, KVR)),
                    pl.BlockSpec((tile, LANES), at),
                    whole((width, WIDE)),
                    whole((width, KVR + LANES)),
                    whole((KVR, NOPE + VHEAD)),
                ]
                + [pl.BlockSpec(memory_space=pl.ANY)] * len(held),
                out_specs=[pl.BlockSpec((tile, w), at) for w in widths],
            ),
            out_shape=[jax.ShapeDtypeStruct((length, w), bf16) for w in widths],
            input_output_aliases={15 + i: i for i in range(len(held))},
            compiler_params=pltpu.CompilerParams(vmem_limit_bytes=56 * megabytes),
            cost_estimate=pl.CostEstimate(
                flops=2 * count * width * (WIDE + KVR + LANES),
                bytes_accessed=4 * count * width + 2 * width * (WIDE + KVR + LANES),
                transcendentals=0,
            ),
            name="project",
        )(piece_place(piece), *blocks, gain, kv_gain, table, query_w, reduce_w, expand, *held)
    return held


def attend_kernel(key_tile, reach, pos_ref, query_ref, key_ref, value_ref, out_ref, low_ref, lse_ref):
    queries = query_ref[...]
    rows = queries.shape[0]
    positions = pos_ref[...]
    tiles = (pl.program_id(0) + 1) * reach // key_tile

    def step(index, carry):
        top, total, running = carry
        keys = key_ref[pl.ds(index * key_tile, key_tile), :]
        values = value_ref[pl.ds(index * key_tile, key_tile), :]
        scores = mm_nt(queries, keys) * score_scale
        key_pos = index * key_tile + lax.broadcasted_iota(jnp.int32, scores.shape, 1)
        scores = jnp.where(key_pos <= positions, scores, masked_score)
        new_top = jnp.maximum(top, jnp.max(scores, axis=-1, keepdims=True))
        weights = jnp.exp(scores - new_top)
        shrink = jnp.exp(top - new_top)
        total = total * shrink + jnp.sum(weights, axis=-1, keepdims=True)
        running = running * shrink + mm(weights.astype(bf16), values)
        return (new_top, total, running)

    start = (
        jnp.full((rows, 1), masked_score, f32),
        jnp.zeros((rows, 1), f32),
        jnp.zeros((rows, VHEAD), f32),
    )
    top, total, running = lax.fori_loop(0, tiles, step, start)
    outcome = running / total
    out_ref[...] = outcome
    low_ref[...] = outcome.astype(bf16)
    lse_ref[...] = top + jnp.log(total)


def attend_grad_kernel(
    key_tile, reach, pos_ref, table_ref, query_ref, key_ref, value_ref, out_ref, lse_ref, grad_ref,
    expand_ref, dquery_ref, dexpand_ref, dlatent_ref, dkey_ref, dvalue_ref,
):
    @pl.when(pl.program_id(0) == 0)
    def clear():
        dkey_ref[...] = jnp.zeros_like(dkey_ref)
        dvalue_ref[...] = jnp.zeros_like(dvalue_ref)

    queries = query_ref[...]
    grads = grad_ref[...]
    positions = pos_ref[...]
    lse = lse_ref[...]
    delta = jnp.sum(grads.astype(f32) * out_ref[...], axis=-1, keepdims=True)
    tiles = (pl.program_id(0) + 1) * reach // key_tile

    def step(index, dquery):
        span = pl.ds(index * key_tile, key_tile)
        keys = key_ref[span, :]
        values = value_ref[span, :]
        scores = mm_nt(queries, keys) * score_scale
        key_pos = index * key_tile + lax.broadcasted_iota(jnp.int32, scores.shape, 1)
        probs = jnp.where(key_pos <= positions, jnp.exp(scores - lse), 0.0)
        dprobs = mm_nt(grads, values)
        dscores = (probs * (dprobs - delta)).astype(bf16)
        dvalue_ref[span, :] += mm_tn(probs.astype(bf16), grads)
        dkey_ref[span, :] += mm_tn(dscores, queries)
        return dquery + mm(dscores, keys)

    dquery = lax.fori_loop(0, tiles, step, jnp.zeros(queries.shape, f32)) * score_scale
    scaled = dquery[:, NOPE:] * table_ref[...]
    lanes = lax.broadcasted_iota(jnp.int32, scaled.shape, 1)
    half = ROPE // 2
    turned = jnp.where(lanes < half, pltpu.roll(scaled, half, 1), -pltpu.roll(scaled, LANES - half, 1))
    dquery_ref[:, :NOPE] = dquery[:, :NOPE].astype(bf16)
    dquery_ref[:, NOPE:] = (scaled + turned)[:, :ROPE].astype(bf16)

    @pl.when(pl.program_id(0) == pl.num_programs(0) - 1)
    def finish():
        def rows(index, carry):
            span = pl.ds(index * key_tile, key_tile)
            dkey = dkey_ref[span, :] * score_scale
            low = jnp.concatenate([dkey[:, :NOPE], dvalue_ref[span, :]], axis=-1).astype(bf16)
            dexpand_ref[span, :] = low
            dlatent_ref[span, :KVR] = mm_nt(low, expand_ref[...]).astype(bf16)
            dlatent_ref[span, KVR:] = dkey[:, NOPE:].astype(bf16)
            return carry

        lax.fori_loop(0, dkey_ref.shape[0] // key_tile, rows, 0)


def attention_tiles(rows, keys):
    tile = min(512, keys)
    row_tile = rows * tile // keys
    return (row_tile, tile)


def attend(positions, queries, keys, values):
    rows, count = queries.shape[0], keys.shape[0]
    row_tile, tile = attention_tiles(rows, count)
    whole = lambda width: pl.BlockSpec((count, width), lambda i: (0, 0))
    part = lambda width: pl.BlockSpec((row_tile, width), lambda i: (i, 0))
    return pl.pallas_call(
        functools.partial(attend_kernel, tile, tile),
        grid=(rows // row_tile,),
        in_specs=[part(1), part(WIDE), whole(WIDE), whole(VHEAD)],
        out_specs=[part(VHEAD), part(VHEAD), part(1)],
        out_shape=[
            jax.ShapeDtypeStruct((rows, VHEAD), f32),
            jax.ShapeDtypeStruct((rows, VHEAD), bf16),
            jax.ShapeDtypeStruct((rows, 1), f32),
        ],
        compiler_params=pltpu.CompilerParams(vmem_limit_bytes=48 * megabytes),
        cost_estimate=pl.CostEstimate(
            flops=rows * count * (QK + VHEAD) * 2,
            bytes_accessed=4 * (rows + count) * (QK + VHEAD),
            transcendentals=rows * count // 2,
        ),
        name="attend",
    )(positions, queries, keys, values)


def attend_grad(positions, table, queries, keys, values, outcome, lse, grads, expand):
    rows, count = queries.shape[0], keys.shape[0]
    row_tile, tile = attention_tiles(rows, count)
    whole = lambda width: pl.BlockSpec((count, width), lambda i: (0, 0))
    part = lambda width: pl.BlockSpec((row_tile, width), lambda i: (i, 0))
    return pl.pallas_call(
        functools.partial(attend_grad_kernel, tile, tile),
        grid=(rows // row_tile,),
        in_specs=[
            part(1), part(LANES), part(WIDE), whole(WIDE), whole(VHEAD), part(VHEAD), part(1),
            part(VHEAD), pl.BlockSpec(expand.shape, lambda i: (0, 0)),
        ],
        out_specs=[part(QK), whole(NOPE + VHEAD), whole(KVR + LANES)],
        out_shape=[
            jax.ShapeDtypeStruct((rows, QK), bf16),
            jax.ShapeDtypeStruct((count, NOPE + VHEAD), bf16),
            jax.ShapeDtypeStruct((count, KVR + LANES), bf16),
        ],
        scratch_shapes=[pltpu.VMEM((count, WIDE), f32), pltpu.VMEM((count, VHEAD), f32)],
        compiler_params=pltpu.CompilerParams(vmem_limit_bytes=48 * megabytes),
        cost_estimate=pl.CostEstimate(
            flops=rows * count * (3 * QK + 2 * VHEAD) * 2,
            bytes_accessed=8 * (rows + count) * (QK + VHEAD),
            transcendentals=rows * count // 2,
        ),
        name="attend_grad",
    )(positions, table, queries, keys, values, outcome, lse, grads, expand)


def copy_blocks(base_ref, source, target, copied):
    step = pl.program_id(0)
    first = (base_ref[0] * 2 + (step ^ base_ref[2])) * 4

    def copies(group):
        return [
            pltpu.make_async_copy(
                source[2 * mask + group].at[0],
                target.at[first + (mask ^ base_ref[1])],
                copied.at[mask],
            )
            for mask in range(4)
        ]

    def each(act):
        for group in (0, 1):

            @pl.when(step == group)
            def run():
                for copy in copies(group):
                    act(copy)

    each(lambda copy: copy.start())
    return lambda: each(lambda copy: copy.wait())


def pick_all(pick_ref, gates_ref, blocks):
    return jnp.concatenate(
        [
            jnp.sum(pick_ref[block].astype(f32) * gates_ref[block], axis=-1, keepdims=True)
            for block in blocks
        ],
        axis=0,
    )


def forward_kernel(parts, base_ref, *refs):
    *refs, copied = refs
    ffn_refs, (pick_ref, gates_ref) = refs[:8], refs[8:10]
    gate_refs, rise_refs, down_refs = (refs[10 + i * parts : 10 + (i + 1) * parts] for i in range(3))
    sgate_ref, sup_ref, sdown_ref = refs[10 + 3 * parts : 13 + 3 * parts]
    outs = refs[-(10 + 3 * parts) :]
    out_refs, (tokens_ref, entries_ref, y_ref) = outs[:4], outs[4:7]
    mid_ref, sg_ref, su_ref = outs[7:10]
    m_refs, g_refs, u_refs = (outs[10 + i * parts : 10 + (i + 1) * parts] for i in range(3))
    slots = pick_ref.shape[1]
    blocks = [mask ^ base_ref[1] for mask in range(4)]
    spans = [slice(mask * slots, (mask + 1) * slots) for mask in range(4)]
    wait = copy_blocks(base_ref, ffn_refs, tokens_ref, copied)

    for mask, (block, span) in enumerate(zip(blocks, spans)):
        tokens = block_of_step(ffn_refs, mask)
        entries_ref[span, :] = mm(pick_ref[block], tokens).astype(bf16)
    gates = pick_all(pick_ref, gates_ref, blocks)
    entries = entries_ref[...]
    y = jnp.zeros(entries.shape, f32)
    for p in range(parts):
        gate = mm_nt(entries, gate_refs[p][...])
        rise = mm_nt(entries, rise_refs[p][...])
        g_refs[p][...] = gate.astype(bf16)
        u_refs[p][...] = rise.astype(bf16)
        middle = swiglu(gate, rise)
        m_refs[p][...] = middle
        y = y + mm(middle, down_refs[p][...])
    y = y.astype(bf16)
    y_ref[...] = y
    scaled = (gates * y.astype(f32)).astype(bf16)
    for mask, (block, span) in enumerate(zip(blocks, spans)):
        tokens = block_of_step(ffn_refs, mask)
        sgate = mm(tokens, sgate_ref[...])
        sup = mm(tokens, sup_ref[...])
        sg_ref[block] = sgate.astype(bf16)
        su_ref[block] = sup.astype(bf16)
        middle = swiglu(sgate, sup)
        mid_ref[block] = middle
        placed = mm_tn(pick_ref[block], scaled[span])
        out_refs[mask][0] = (mm(middle, sdown_ref[...]) + placed).astype(bf16)
    wait()


def backward_kernel(parts, base_ref, *refs):
    *refs, copied = refs
    up_refs, (pick_ref, gates_ref, y_ref, sg_ref, su_ref) = refs[:8], refs[8:13]
    g_refs, u_refs = (refs[13 + i * parts : 13 + (i + 1) * parts] for i in range(2))
    rest = refs[13 + 2 * parts :]
    gate_refs, rise_refs, down_refs = (rest[i * parts : (i + 1) * parts] for i in range(3))
    sgate_ref, sup_ref, sdown_ref = rest[3 * parts : 3 + 3 * parts]
    outs = refs[-(8 + 2 * parts) :]
    db_refs, (ups_ref, dy_ref, dgate_ref, pair_ref) = outs[:4], outs[4:8]
    dg_refs, du_refs = (outs[8 + i * parts : 8 + (i + 1) * parts] for i in range(2))
    slots = pick_ref.shape[1]
    blocks = [mask ^ base_ref[1] for mask in range(4)]
    spans = [slice(mask * slots, (mask + 1) * slots) for mask in range(4)]
    wait = copy_blocks(base_ref, up_refs, ups_ref, copied)

    for mask, (block, span) in enumerate(zip(blocks, spans)):
        upstream = block_of_step(up_refs, mask)
        dy_ref[span, :] = mm(pick_ref[block], upstream).astype(bf16)
    gates = pick_all(pick_ref, gates_ref, blocks)
    grad_rows = dy_ref[...].astype(f32)
    dgates = jnp.sum(grad_rows * y_ref[...].astype(f32), axis=-1, keepdims=True)
    dy = (gates * grad_rows).astype(bf16)
    dy_ref[...] = dy
    db = jnp.zeros(dy.shape, f32)
    for p in range(parts):
        dm = mm_nt(dy, down_refs[p][...])
        dg, du = swiglu_grads(g_refs[p][...].astype(f32), u_refs[p][...].astype(f32), dm)
        dg_refs[p][...] = dg
        du_refs[p][...] = du
        db = db + mm(dg, gate_refs[p][...]) + mm(du, rise_refs[p][...])
    db = db.astype(bf16)
    for mask, (block, span) in enumerate(zip(blocks, spans)):
        pick = pick_ref[block]
        dgate_ref[block] = jnp.sum(pick.astype(f32) * dgates[span], axis=0, keepdims=True)
        upstream = block_of_step(up_refs, mask)
        sgate, sup = sg_ref[block].astype(f32), su_ref[block].astype(f32)
        dsg, dsu = swiglu_grads(sgate, sup, mm_nt(upstream, sdown_ref[...]))
        pair_ref[0, block] = dsg
        pair_ref[1, block] = dsu
        db_refs[mask][0] = (
            mm_nt(dsg, sgate_ref[...]) + mm_nt(dsu, sup_ref[...]) + mm_tn(pick, db[span])
        ).astype(bf16)
    wait()


def expert_call(kernel, name, piece, blocks, tiled, weights, held_shapes, held, part, width, flops):
    operands, specs = block_operands(blocks)
    fixed = lambda i, base: (0, 0)

    groups = held_shapes[0][0].shape[0] // 4

    def spec(shape, axis=0):
        tile = tuple(n // groups if d == axis else n for d, n in enumerate(shape))
        at = lambda i, base: tuple(
            base[0] * 2 + (i ^ base[2]) if d == axis else 0 for d in range(len(shape))
        )
        return pl.BlockSpec(tile, at)

    out_specs = [pl.BlockSpec((1, part, width), lambda i, base: (i, 0, 0))] * 4
    for shape, axis in held_shapes:
        out_specs.append(
            pl.BlockSpec(memory_space=pl.ANY) if axis is None else spec(shape.shape, axis)
        )
    results = pl.pallas_call(
        kernel,
        grid_spec=pltpu.PrefetchScalarGridSpec(
            num_scalar_prefetch=1,
            grid=(2,),
            in_specs=specs
            + [spec(v.shape) for v in tiled]
            + [pl.BlockSpec(w.shape, fixed, pipeline_mode=pl.Buffered(1)) for w in weights]
            + [pl.BlockSpec(memory_space=pl.ANY)] * len(held),
            out_specs=out_specs,
            scratch_shapes=[pltpu.SemaphoreType.DMA((4,))],
        ),
        out_shape=[jax.ShapeDtypeStruct((2, part, width), bf16)] * 4
        + [shape for shape, _ in held_shapes],
        input_output_aliases={
            1 + len(operands) + len(tiled) + len(weights) + i: 4 + i for i in range(len(held))
        },
        compiler_params=pltpu.CompilerParams(vmem_limit_bytes=60 * megabytes),
        cost_estimate=pl.CostEstimate(
            flops=flops, bytes_accessed=40 * megabytes, transcendentals=1 << 20
        ),
        name=name,
    )(piece_place(piece), *operands, *tiled, *weights, *held)
    return results[:4], results[4:]


def expert_layers(pieces, ups, pick, gates, gate_w, up_w, down_w, sgate, sup, sdown):
    ctx, slots, part = pick.shape
    width, hidden = sgate.shape
    parts = len(gate_w)
    inner = [w.shape[0] for w in gate_w]
    weights = [*gate_w, *up_w, *down_w, sgate, sup, sdown]
    whole = lambda *shape, dtype=bf16: jax.ShapeDtypeStruct(shape, dtype)
    blocks = (whole(ctx, part, width), None)
    rows = (whole(ctx * slots, width), 0)
    units = [(whole(ctx * slots, w), 0) for w in inner]
    shared = (whole(ctx, part, hidden), 0)
    count = len(pieces)
    flops = 6 * (ctx * slots * width * sum(inner) + ctx * part * width * hidden) // count
    forward = functools.partial(forward_kernel, parts)
    backward = functools.partial(backward_kernel, parts)
    forward_shapes = [blocks, rows, rows, shared, shared, shared, *units * 3]
    backward_shapes = [
        blocks, rows, (whole(ctx, 1, part, dtype=f32), 0), (whole(2, ctx, part, hidden), 1), *units * 2
    ]
    outs, dbs, out_hops, db_hops, done, back = [], [], [], [], [], []
    for piece in range(count):
        out, done = expert_call(
            forward, "experts_forward", piece, pieces[piece], [pick, gates], weights,
            forward_shapes, done, part, width, flops,
        )
        if piece == 1 and exchanges():
            out, done, out_hops = together(out, done, out_hops)
        outs.append(out)
        if exchanges():
            out_hops = [*out_hops, *plane_hops([out])]
    tokens, entries, y, mid, sg, su, *units = done
    m, g, u = (units[i * parts : (i + 1) * parts] for i in range(3))
    for piece in range(count):
        db, back = expert_call(
            backward, "experts_backward", piece, ups[piece], [pick, gates, y, sg, su, *g, *u], weights,
            backward_shapes, back, part, width, flops,
        )
        if exchanges():
            if piece == 0:
                db, back, out_hops = together(db, back, out_hops)
            else:
                db, back, db_hops = together(db, back, db_hops)
            if piece == 0:
                db_hops = plane_hops([db])
        dbs.append(db)
    ups_flat, dy, dgates, pair, *units = back
    dg, du = (units[i * parts : (i + 1) * parts] for i in range(2))
    sources = tokens, ups_flat, mid, pair[0], pair[1]
    return (outs, out_hops), (dbs, db_hops), sources, entries, dy, dgates, m, dg, du


def shards(
    hidden_in, gain_attn, w_query, w_kv_down, gain_kv, w_kv_up, w_out, gain_ffn, w_router,
    shared_gate, shared_up, shared_down, expert_gate, expert_up, expert_down, routes, cotangent,
):
    part, width = hidden_in.shape[1:]
    ctx, fsdp = lax.axis_size("ctx"), lax.axis_size("fsdp")
    ctx_rank = lax.axis_index("ctx")
    length = part * ctx
    rows = w_query.shape[0]
    experts = w_router.shape[1]
    parts_of_head = ctx // HEADS
    query_part = part // parts_of_head
    first_row = (ctx_rank % parts_of_head) * query_part
    everywhere = ("ctx", "fsdp")

    def join_rows(parts):
        if fsdp != 2:
            return jnp.stack(parts, axis=1).reshape(-1, parts[0].shape[-1])
        rank = lax.axis_index("fsdp")
        whole = jnp.zeros((ctx, 2) + parts[0].shape[1:], parts[0].dtype)
        for place, value in ((rank, parts[0]), (1 - rank, parts[1])):
            whole = lax.dynamic_update_slice_in_dim(whole, value[:, None], place, 1)
        return whole.reshape(-1, parts[0].shape[-1])

    def to_rows(columns, count):
        grid = columns.reshape(ctx, fsdp, count, columns.shape[-1])
        grid = scatter_fsdp(in_fsdp_order([grid[:, i] for i in range(fsdp)]))
        return to_owner(grid.astype(bf16)).astype(f32)

    def head_blocks(values):
        blocks = values.reshape(values.shape[0], HEADS, -1).transpose(1, 0, 2)
        return jnp.repeat(blocks, parts_of_head, axis=0)

    def from_head_blocks(blocks):
        blocks = blocks.reshape(HEADS, parts_of_head, *blocks.shape[1:]).sum(axis=1)
        return blocks.transpose(1, 0, 2).reshape(blocks.shape[1], -1)

    compressed_width = KVR + ROPE
    turned_width = compressed_width + ROPE
    kv_rows = gain_kv.shape[0]
    small_width = turned_width + experts + 3
    small = jnp.concatenate(
        [
            w_kv_down,
            turn_columns(w_kv_down[:, KVR:]),
            w_router,
            gain_attn[:, None],
            gain_ffn[:, None],
            jnp.pad(gain_kv, (0, rows - kv_rows))[:, None],
            jnp.zeros((rows, -small_width % 128), bf16),
        ],
        axis=1,
    )
    small_full = lax.all_gather(small, everywhere, axis=0, tiled=True)
    reduce_full = small_full[:, :compressed_width]
    router_full = small_full[:, turned_width : small_width - 3]
    attn_gain = small_full[:, small_width - 3].astype(f32)
    ffn_gain = small_full[:, small_width - 2].astype(f32)
    kv_gain = small_full[:, small_width - 1].reshape(ctx * fsdp, rows)[:, :kv_rows]
    kv_gain = kv_gain.reshape(KVR).astype(f32)

    tokens_low = hidden_in.reshape(part, width)
    upstream_low = cotangent.reshape(part, width)
    hidden_shared = shared_gate.shape[1] // ctx
    query_blocks = head_blocks(w_query)
    route_rows = routes.reshape(part, TOP)
    chosen_hot = route_rows[:, :, None] == jnp.arange(experts, dtype=jnp.int32)[None, None, :]
    columns = [
        query_blocks,
        turn_columns(query_blocks[..., NOPE:]),
        head_blocks(w_kv_up).reshape(ctx, rows, -1),
        jnp.any(chosen_hot, axis=1).astype(bf16).T.reshape(ctx, rows, -1),
    ]
    column_blocks = jnp.concatenate(columns, axis=-1)
    expand_end = WIDE + columns[2].shape[-1]

    def joined_stage(received):
        return received, join_rows(gather_fsdp(received[..., :expand_end]))

    tokens_all, (received, by_rows) = gather_ctx(
        tokens_low, lambda _: None, lambda _: None, lambda _: to_owner(column_blocks), joined_stage
    )
    named_all = received[..., expand_end:].reshape(ctx, part)
    query_w = by_rows[:, :WIDE]
    expand = by_rows[:, WIDE:].reshape(KVR, NOPE + VHEAD)
    output_full = lax.all_gather(w_out, everywhere, axis=0, tiled=True)

    upstream_late, gate_late, up_late, _ = lax.optimization_barrier(
        (upstream_low, shared_gate, shared_up, tokens_all[-1][3][1][0])
    )
    columns = [v.reshape(rows, ctx, hidden_shared) for v in (gate_late, up_late)]
    shared_blocks = jnp.concatenate(columns, axis=2).transpose(1, 0, 2)
    shared_back = jnp.concatenate(in_fsdp_order(gather_fsdp(shared_down)), axis=0)
    gate_parts = gather_fsdp(expert_gate[0].T)
    up_parts = gather_fsdp(expert_up[0].T)
    down_parts = gather_fsdp(expert_down[0].T)

    slot_cap = min(part, part * TOP * 4 // (3 * experts))
    until = jnp.arange(part)[:, None] <= jnp.arange(part)[None, :]
    ordinal = mm(named_all, until.astype(bf16)) - 1.0
    slots = jnp.arange(slot_cap, dtype=f32)[None, :, None]
    pick = ((ordinal[:, None, :] == slots) & (named_all[:, None, :] > 0)).astype(bf16)

    cosine, sine = rope_tables(jnp.arange(length, dtype=jnp.int32))
    table = jnp.concatenate([cosine, sine], axis=-1)
    def query_rows(values):
        if parts_of_head == 1:
            return values
        blocks = values.reshape(ctx, part, values.shape[-1])
        blocks = lax.dynamic_slice_in_dim(blocks, first_row, query_part, 1)
        return blocks.reshape(ctx * query_part, values.shape[-1])

    def to_heads(values):
        split = values.reshape(parts_of_head, query_part, HEADS, values.shape[-1])
        sent = split.transpose(2, 0, 1, 3).reshape(ctx, query_part, values.shape[-1])
        return to_owner(sent).reshape(ctx * query_part, values.shape[-1])

    def from_heads(values):
        back = to_owner(values.reshape(ctx, query_part, values.shape[-1]))
        back = back.reshape(HEADS, parts_of_head, query_part, values.shape[-1])
        return back.transpose(1, 2, 0, 3).reshape(part, HEADS, values.shape[-1])

    query_pos = query_rows(jnp.arange(length, dtype=jnp.int32)[:, None])

    def first_stage(_):
        return project(
            tokens_all, attn_gain[None], kv_gain[None], table, query_w, small_full, expand
        )

    def second_stage(projected):
        _, query_all, key_head, value_head, _ = projected
        outcome = attend(query_pos, query_rows(query_all), key_head, value_head)
        return projected, outcome, to_owner(shared_blocks)

    def third_stage(held):
        projected, (outcome, outcome_low, lse), shared_in = held
        shared_in = join_rows(gather_fsdp(shared_in))
        return projected, outcome, lse, from_heads(outcome_low), shared_in

    upstream_all, (projected, outcome, lse, attended, shared_in) = gather_ctx(
        upstream_late, first_stage, second_stage, third_stage
    )
    shared_in = (shared_in[:, :hidden_shared], shared_in[:, hidden_shared:])
    normed_all, query_all, key_head, value_head, latent_all = projected
    query_head = query_rows(query_all)
    attended = attended.reshape(part, HEADS * VHEAD)
    tokens = tokens_low.astype(f32)
    residual = tokens + mm(attended, output_full)

    ffn_factor = rms_factor(residual)
    ffn_low = (residual * ffn_factor * ffn_gain).astype(bf16)
    logits = mm(ffn_low, router_full)
    chosen = jnp.sum(jnp.where(chosen_hot, logits[:, None, :], 0.0), axis=-1)
    gate_share = jax.nn.softmax(chosen, axis=-1)
    gates_own = jnp.sum(jnp.where(chosen_hot, gate_share[..., None], 0.0), axis=1)
    ffn_all, gates_all = gather_ctx(ffn_low, lambda _: None, lambda _: to_owner(gates_own.T))
    query_late, _ = lax.optimization_barrier((w_query, ffn_all[-1][3][1][0]))
    query_full = lax.all_gather(query_late, everywhere, axis=0, tiled=True)
    (out_parts, out_arrived), (grad_parts, grad_arrived), *rest = expert_layers(
        ffn_all, upstream_all, pick, gates_all[:, None, :], gate_parts, up_parts, down_parts,
        *shared_in, shared_back,
    )
    flat, entries, grad_entries, token_dgates, middle, gate_low, up_low = rest
    tokens_flat, upstream_flat, shared_mid, *shared_pair = (
        v.reshape(length, v.shape[-1]) for v in flat
    )

    sums = [(middle, grad_entries), (gate_low, entries), (up_low, entries)]
    sums = [[mm_tn(left, right) for left in lefts] for lefts, right in sums]
    sums = [[own, *(v.astype(bf16) for v in others)] for own, *others in sums]
    shared_sums = [mm_tn(shared_mid, upstream_flat), *(mm_tn(tokens_flat, v) for v in shared_pair)]
    ffn_grad, (sums, dgates_own), (shared_sums, query_full) = scatter_ctx(
        grad_parts, (sums, to_owner(token_dgates[:, 0])), (shared_sums, query_full), grad_arrived
    )
    grad_gates = jnp.sum(jnp.where(chosen_hot, dgates_own.T[:, None, :], 0.0), axis=-1)
    grad_expert_down, grad_expert_gate, grad_expert_up = (scatter_fsdp(v).T[None] for v in sums)
    down_rows = shared_down.shape[0]
    grad_back = shared_sums[0].reshape(fsdp, down_rows, width)
    grad_shared_down = scatter_fsdp(in_fsdp_order([grad_back[i] for i in range(fsdp)]))
    grad_in = to_rows(jnp.concatenate(shared_sums[1:], axis=-1), rows).transpose(1, 0, 2)
    grad_shared_gate = grad_in[..., :hidden_shared].reshape(rows, ctx * hidden_shared)
    grad_shared_up = grad_in[..., hidden_shared:].reshape(rows, ctx * hidden_shared)

    grad_chosen = gate_share * (
        grad_gates - jnp.sum(gate_share * grad_gates, axis=-1, keepdims=True)
    )
    grad_logits = jnp.sum(jnp.where(chosen_hot, grad_chosen[..., None], 0.0), axis=1).astype(bf16)
    grad_router = mm_tn(ffn_low, grad_logits)
    ffn_grad = ffn_grad + mm_nt(grad_logits, router_full)
    upstream = upstream_low.astype(f32)
    ffn_grad_in, grad_ffn_gain = rms_backward(residual, ffn_factor, ffn_gain, ffn_grad)
    grad_residual = upstream + ffn_grad_in
    grad_residual_low = grad_residual.astype(bf16)

    grad_attended = mm_nt(grad_residual_low, output_full).astype(bf16)
    grad_head = to_heads(grad_attended.reshape(part, HEADS, VHEAD))
    output_heads = attended.reshape(part, ctx, fsdp, rows)
    if exchanges():
        output_heads = jnp.take(output_heads, piece_order(), axis=1, mode="clip")
    output_heads = in_fsdp_order([output_heads[:, :, i].reshape(part, -1) for i in range(fsdp)])
    grad_output = [mm_tn(v, grad_residual_low) for v in output_heads]
    grad_output = scatter_fsdp(grad_output).astype(bf16).reshape(ctx, rows, width)
    if exchanges():
        grad_output = grad_output.reshape(2, 4, 2, rows, width)
        output_pieces = [[grad_output[p, m] for m in range(4)] for p in range(2)]
    else:
        output_pieces = in_pieces(grad_output)
    attention_grads = attend_grad(
        query_pos, query_rows(table), query_head, key_head, value_head, outcome, lse, grad_head, expand
    )
    latent_blocks = lambda v: in_pieces(v.reshape(ctx, part, KVR + LANES))
    if exchanges():
        out_sum, out_line = line_hops(out_parts, out_arrived)
        attention_grads, output_arrived, out_line = together(
            attention_grads, plane_hops(output_pieces), out_line
        )
        out_sum = plus(out_sum, *out_line)
        grad_query, grad_expanded, latent_part = attention_grads
        output_sum, output_line = line_hops(output_pieces, output_arrived)
        latent_pieces = latent_blocks(latent_part)
        arrived, output_line, query_own = together(
            plane_hops(latent_pieces), output_line, from_heads(grad_query)
        )
        grad_output = plus(output_sum, *output_line)
        latent_sum, latent_line = line_hops(latent_pieces, arrived)
        grad_normed = mm_nt(query_own.reshape(part, HEADS * QK), query_full)
        latent_line, grad_normed, grad_query, grad_expanded = together(
            latent_line, grad_normed, grad_query, grad_expanded
        )
        latent_sum = plus(latent_sum, *latent_line)
    else:
        grad_query, grad_expanded, latent_part = attention_grads
        out_sum = whole_sum(out_parts)
        grad_output = whole_sum(output_pieces)
        latent_sum = whole_sum(latent_blocks(latent_part))
        grad_normed = mm_nt(from_heads(grad_query).reshape(part, HEADS * QK), query_full)

    grad_query_w = mm_tn(query_rows(normed_all), grad_query).reshape(ctx, fsdp, rows, QK)
    grad_expand = mm_tn(latent_all, grad_expanded).reshape(ctx, fsdp, rows, -1)
    by_heads = jnp.concatenate([grad_query_w, grad_expand], axis=-1)
    by_heads = to_rows(by_heads.reshape(width, by_heads.shape[-1]), rows)
    grad_query_w = from_head_blocks(by_heads[..., :QK])
    grad_expand = from_head_blocks(by_heads[..., QK:].reshape(ctx, kv_rows, NOPE + VHEAD))

    own_rows = ctx_rank * part
    own_normed = lax.dynamic_slice_in_dim(normed_all, own_rows, part, 0)
    latent_raw = mm(own_normed, reduce_full[:, :KVR])
    grad_latent_raw, _ = rms_backward(
        latent_raw, rms_factor(latent_raw), kv_gain, latent_sum[:, :KVR]
    )
    own_cos = lax.dynamic_slice_in_dim(cosine, own_rows, part, 0)
    own_sin = lax.dynamic_slice_in_dim(sine, own_rows, part, 0)
    grad_compressed = jnp.concatenate(
        [grad_latent_raw, unrotate(latent_sum[:, KVR:compressed_width], own_cos, own_sin)], axis=-1
    ).astype(bf16)
    grad_small = jnp.concatenate(
        [
            mm_tn(own_normed, grad_compressed).astype(bf16),
            grad_router.astype(bf16),
            grad_ffn_gain[:, None].astype(bf16),
            jnp.zeros((width, -(compressed_width + experts + 1) % 128), bf16),
        ],
        axis=1,
    ).reshape(ctx, fsdp, rows, -1)
    grad_small = scatter_fsdp(in_fsdp_order([grad_small[:, i] for i in range(fsdp)]))
    grad_small, _, _ = scatter_ctx(in_pieces(grad_small.astype(bf16)))
    grad_reduce = grad_small[:, :compressed_width]
    grad_normed = grad_normed + mm_nt(grad_compressed, reduce_full)
    attn_grad_in, _ = rms_backward(tokens, rms_factor(tokens), attn_gain, grad_normed)
    grad_hidden_in = (grad_residual + attn_grad_in)[None]

    def gain_grad(gain, pairs):
        total = sum(jnp.sum(w.astype(f32) * g, axis=-1) for w, g in pairs)
        return total / gain.astype(f32)

    grad_attn_gain = gain_grad(gain_attn, [(w_query, grad_query_w), (w_kv_down, grad_reduce)])
    grad_kv_gain = gain_grad(gain_kv, [(w_kv_up, grad_expand)])
    out_sum, kept, _ = lax.optimization_barrier((out_sum, residual, latent_sum))
    hidden_out = (kept + out_sum).astype(bf16)
    after = compressed_width + experts
    return (
        hidden_out[None],
        grad_hidden_in,
        grad_attn_gain,
        grad_query_w,
        grad_reduce,
        grad_kv_gain,
        grad_expand,
        grad_output,
        grad_small[:, after],
        grad_small[:, compressed_width:after],
        grad_shared_gate,
        grad_shared_up,
        grad_shared_down,
        grad_expert_gate,
        grad_expert_up,
        grad_expert_down,
    )


def solution(mesh):
    dense = P(("ctx", "fsdp"), None)
    gain = P(("ctx", "fsdp"))
    tokens = P("fsdp", "ctx", None)
    expert = P("ctx", None, "fsdp")
    return jax.shard_map(
        shards,
        mesh=mesh,
        in_specs=(
            tokens, gain, dense, dense, gain, dense, dense, gain, dense, dense, dense, dense,
            expert, expert, expert, tokens, tokens,
        ),
        out_specs=(
            tokens, tokens, gain, dense, dense, gain, dense, dense, gain, dense, dense, dense,
            dense, expert, expert, expert,
        ),
        check_vma=False,
    )
```

```python
import functools
import math

import jax
import jax.numpy as jnp
from jax import lax
from jax.experimental import pallas as pl
from jax.experimental.pallas import tpu as pltpu
from jax.sharding import PartitionSpec as P

HEADS = 16
NOPE = 128
ROPE = 64
VHEAD = 128
KVR = 512
TOP = 6
QK = NOPE + ROPE

epsilon = 1e-06
rope_base = 10000.0
masked_score = -1e30
score_scale = 1.0 / math.sqrt(QK)

bf16 = jnp.bfloat16
f32 = jnp.float32


def mm(left, right):
    return jnp.dot(left, right, preferred_element_type=f32)


def mm_nt(left, right):
    return lax.dot_general(left, right, (((1,), (1,)), ((), ())), preferred_element_type=f32)


def mm_tn(left, right):
    return lax.dot_general(left, right, (((0,), (0,)), ((), ())), preferred_element_type=f32)


def rms_factor(values):
    return lax.rsqrt(jnp.mean(values * values, axis=-1, keepdims=True) + epsilon)


def rms_backward(values, factor, gain, upstream):
    weighted = upstream * gain
    inner_mean = jnp.mean(weighted * values, axis=-1, keepdims=True)
    grad_in = factor * weighted - values * (factor * factor * factor) * inner_mean
    grad_gain = jnp.sum(upstream * values * factor, axis=0)
    return (grad_in, grad_gain)


def rope_tables(positions):
    half_width = ROPE // 2
    frequency = jnp.exp(jnp.arange(half_width, dtype=f32) * (-math.log(rope_base) / half_width))
    angles = positions.astype(f32)[:, None] * frequency[None, :]
    angles = jnp.concatenate([angles, angles], axis=-1)
    return (jnp.cos(angles), jnp.sin(angles))


def rotate(values, cosine, sine):
    half_width = values.shape[-1] // 2
    turned = jnp.concatenate([-values[..., half_width:], values[..., :half_width]], axis=-1)
    return values * cosine + turned * sine


def unrotate(upstream, cosine, sine):
    half_width = upstream.shape[-1] // 2
    rotated = upstream * sine
    turned = jnp.concatenate([rotated[..., half_width:], -rotated[..., :half_width]], axis=-1)
    return upstream * cosine + turned


def swiglu(gate_pre, up_pre):
    return (jax.nn.silu(gate_pre) * up_pre).astype(bf16)


def swiglu_grads(gate_pre, up_pre, grad_mid):
    squash = jax.nn.sigmoid(gate_pre)
    grad_gate = grad_mid * up_pre * squash * (1.0 + gate_pre * (1.0 - squash))
    grad_up = grad_mid * (gate_pre * squash)
    return (grad_gate.astype(bf16), grad_up.astype(bf16))


def exchanges():
    return lax.axis_size("ctx") == 16


def hop(value, mask):
    return lax.ppermute(value, "ctx", [(i, i ^ mask) for i in range(16)])


def together(*values):
    return lax.optimization_barrier(values)


def gather_ctx(block, *stages):
    held = None
    if not exchanges():
        whole = lax.all_gather(block, "ctx", axis=0)
        at = lambda piece, mask: [(whole, 8 * piece + 4 * group + mask) for group in (0, 1)]
        pieces = [[at(piece, mask) for mask in range(4)] for piece in range(whole.shape[0] // 8)]
        for stage in stages:
            held = stage(held, pieces)
        return pieces, held

    def end(number, *hops):
        nonlocal held
        if number < len(stages):
            held = stages[number](held, pieces)
        held, *hops = together(held, *hops)
        return hops

    pieces = []

    alone = lambda values: [(value[None], 0) for value in values]
    both = lambda values: [(values, 0), (values, 1)]
    near, far, one, two = end(0, *(hop(block, mask) for mask in (4, 8, 1, 2)))
    far_near, three, *near_others = end(
        1, hop(far, 4), hop(two, 1), *(hop(near, mask) for mask in (1, 2, 3))
    )
    pairs = zip((block, one, two, three), (near, *near_others))
    pieces = [[alone(values) for values in pairs]]
    pair = jnp.stack([far, far_near])
    far_one, far_two = end(2, hop(pair, 1), hop(pair, 2))
    far_three = end(3, hop(far_two[0], 1), hop(far_one[1], 2))
    return [*pieces, [both(pair), both(far_one), both(far_two), alone(far_three)]], held


def block_operands(piece):
    blocks = [block for mask in piece for block in mask]
    specs = [
        pl.BlockSpec(
            (1, *array.shape[1:]), lambda i, base, at=at: (at, 0, 0), pipeline_mode=pl.Buffered(1)
        )
        for array, at in blocks
    ]
    return [array for array, _ in blocks], specs


def block_of_step(refs, mask):
    return jnp.where(pl.program_id(0) == 0, refs[2 * mask][0], refs[2 * mask + 1][0])


def plus(*values):
    return sum(value.astype(f32) for value in values)


def plane_hops(pieces):
    return [[hop(value, mask) for mask, value in enumerate(piece) if mask] for piece in pieces]


def line_hops(pieces, arrived):
    near, far = (plus(piece[0], *values) for piece, values in zip(pieces, arrived))
    sent = ((near[1], 4), (far[0], 8), (far[1], 12))
    return near[0], [hop(value.astype(bf16), mask) for value, mask in sent]


def whole_sum(pieces):
    whole = jnp.stack([jnp.stack(piece, axis=1) for piece in pieces])
    whole = whole.reshape(-1, *whole.shape[3:])
    return lax.psum_scatter(whole, "ctx", scatter_dimension=0).astype(f32)


def scatter_ctx(pieces, beside_plane=(), beside_line=(), near=None):
    if not exchanges():
        return whole_sum(pieces), beside_plane, beside_line
    near = near or plane_hops(pieces[:1])
    near, far, beside_plane = together(near, plane_hops(pieces[1:]), beside_plane)
    own, arrived = line_hops(pieces, [*near, *far])
    arrived, beside_line = together(arrived, beside_line)
    return plus(own, *arrived), beside_plane, beside_line


def piece_place(piece):
    if not exchanges():
        return jnp.array([piece, 0, 0], jnp.int32)
    own = lax.axis_index("ctx")
    return jnp.stack([(own >> 3) ^ piece, own & 3, (own >> 2) & 1])


def swap_cores(value):
    return lax.ppermute(value, "fsdp", [(0, 1), (1, 0)])


def gather_fsdp(block):
    if lax.axis_size("fsdp") == 2:
        return [block, swap_cores(block)]
    whole = lax.all_gather(block, "fsdp", axis=0)
    return [whole[i] for i in range(lax.axis_size("fsdp"))]


def scatter_fsdp(parts):
    if lax.axis_size("fsdp") == 2:
        return parts[0].astype(f32) + swap_cores(parts[1].astype(bf16)).astype(f32)
    stacked = jnp.stack([part.astype(bf16) for part in parts])
    return lax.psum_scatter(stacked, "fsdp", scatter_dimension=0).astype(f32)


def in_fsdp_order(parts):
    if lax.axis_size("fsdp") == 2:
        low = lax.axis_index("fsdp") == 0
        return [jnp.where(low, parts[0], parts[1]), jnp.where(low, parts[1], parts[0])]
    return parts


def to_owner(blocks):
    return lax.all_to_all(blocks, "ctx", split_axis=0, concat_axis=0, tiled=True)


LANES = 128
WIDE = NOPE + 2 * ROPE
megabytes = 1024 * 1024


def turn_columns(weights):
    half = weights.shape[-1] // 2
    return jnp.concatenate([-weights[..., half:], weights[..., :half]], axis=-1)


def project_kernel(base_ref, *refs):
    token_refs = refs[:8]
    gain_ref, kv_gain_ref, table_ref, query_w_ref, reduce_ref, expand_ref = refs[8:14]
    normed_ref, query_ref, key_ref, value_ref, latent_ref = refs[-5:]
    part = token_refs[0].shape[1]
    first_half = lax.broadcasted_iota(jnp.int32, (part, LANES), 1) < ROPE
    for mask in range(4):
        span = pl.ds(pl.multiple_of((mask ^ base_ref[1]) * part, part), part)
        tokens = block_of_step(token_refs, mask).astype(f32)
        normed = (tokens * rms_factor(tokens) * gain_ref[...]).astype(bf16)
        normed_ref[span, :] = normed
        table = table_ref[span, :]

        def rope(values):
            scaled = values * table
            return scaled + pltpu.roll(scaled, ROPE, 1)

        queries = mm(normed, query_w_ref[...])
        query_ref[span, :NOPE] = queries[:, :NOPE].astype(bf16)
        query_ref[span, NOPE:] = jnp.where(first_half, rope(queries[:, NOPE:]), 0.0).astype(bf16)
        compressed = mm(normed, reduce_ref[...])
        raw = compressed[:, :KVR]
        latent = (raw * rms_factor(raw) * kv_gain_ref[...]).astype(bf16)
        latent_ref[span, :] = latent
        expanded = mm(latent, expand_ref[...]).astype(bf16)
        key_ref[span, :NOPE] = expanded[:, :NOPE]
        key_ref[span, NOPE:] = rope(compressed[:, KVR:]).astype(bf16)
        value_ref[span, :] = expanded[:, NOPE:]


def project(pieces, gain, kv_gain, table, query_w, reduce_w, expand):
    length, width = table.shape[0], query_w.shape[0]
    widths = [width, WIDE, WIDE, VHEAD, KVR]
    held = []
    for piece, blocks in enumerate(pieces):
        blocks, block_specs = block_operands(blocks)
        steps, part = 2, blocks[0].shape[1]
        tile = 4 * part
        at = lambda i, base: (base[0] * 2 + (i ^ base[2]), 0)
        fixed = lambda i, base: (0, 0)
        whole = lambda shape: pl.BlockSpec(shape, fixed, pipeline_mode=pl.Buffered(1))
        count = steps * tile
        held = pl.pallas_call(
            project_kernel,
            grid_spec=pltpu.PrefetchScalarGridSpec(
                num_scalar_prefetch=1,
                grid=(steps,),
                in_specs=block_specs
                + [
                    whole((1, width)),
                    whole((1, KVR)),
                    pl.BlockSpec((tile, LANES), at),
                    whole((width, WIDE)),
                    whole((width, KVR + LANES)),
                    whole((KVR, NOPE + VHEAD)),
                ]
                + [pl.BlockSpec(memory_space=pl.ANY)] * len(held),
                out_specs=[pl.BlockSpec((tile, w), at) for w in widths],
            ),
            out_shape=[jax.ShapeDtypeStruct((length, w), bf16) for w in widths],
            input_output_aliases={15 + i: i for i in range(len(held))},
            compiler_params=pltpu.CompilerParams(vmem_limit_bytes=56 * megabytes),
            cost_estimate=pl.CostEstimate(
                flops=2 * count * width * (WIDE + KVR + LANES),
                bytes_accessed=4 * count * width + 2 * width * (WIDE + KVR + LANES),
                transcendentals=0,
            ),
            name="project",
        )(piece_place(piece), *blocks, gain, kv_gain, table, query_w, reduce_w, expand, *held)
    return held


def attend_kernel(key_tile, reach, pos_ref, query_ref, key_ref, value_ref, out_ref, low_ref, lse_ref):
    queries = query_ref[...]
    rows = queries.shape[0]
    positions = pos_ref[...]
    tiles = (pl.program_id(0) + 1) * reach // key_tile

    def step(index, carry):
        top, total, running = carry
        keys = key_ref[pl.ds(index * key_tile, key_tile), :]
        values = value_ref[pl.ds(index * key_tile, key_tile), :]
        scores = mm_nt(queries, keys) * score_scale
        key_pos = index * key_tile + lax.broadcasted_iota(jnp.int32, scores.shape, 1)
        scores = jnp.where(key_pos <= positions, scores, masked_score)
        new_top = jnp.maximum(top, jnp.max(scores, axis=-1, keepdims=True))
        weights = jnp.exp(scores - new_top)
        shrink = jnp.exp(top - new_top)
        total = total * shrink + jnp.sum(weights, axis=-1, keepdims=True)
        running = running * shrink + mm(weights.astype(bf16), values)
        return (new_top, total, running)

    start = (
        jnp.full((rows, 1), masked_score, f32),
        jnp.zeros((rows, 1), f32),
        jnp.zeros((rows, VHEAD), f32),
    )
    top, total, running = lax.fori_loop(0, tiles, step, start)
    outcome = running / total
    out_ref[...] = outcome
    low_ref[...] = outcome.astype(bf16)
    lse_ref[...] = top + jnp.log(total)


def attend_grad_kernel(
    key_tile, reach, pos_ref, table_ref, query_ref, key_ref, value_ref, out_ref, lse_ref, grad_ref,
    expand_ref, dquery_ref, dexpand_ref, dlatent_ref, dkey_ref, dvalue_ref,
):
    @pl.when(pl.program_id(0) == 0)
    def clear():
        dkey_ref[...] = jnp.zeros_like(dkey_ref)
        dvalue_ref[...] = jnp.zeros_like(dvalue_ref)

    queries = query_ref[...]
    grads = grad_ref[...]
    positions = pos_ref[...]
    lse = lse_ref[...]
    delta = jnp.sum(grads.astype(f32) * out_ref[...], axis=-1, keepdims=True)
    tiles = (pl.program_id(0) + 1) * reach // key_tile

    def step(index, dquery):
        span = pl.ds(index * key_tile, key_tile)
        keys = key_ref[span, :]
        values = value_ref[span, :]
        scores = mm_nt(queries, keys) * score_scale
        key_pos = index * key_tile + lax.broadcasted_iota(jnp.int32, scores.shape, 1)
        probs = jnp.where(key_pos <= positions, jnp.exp(scores - lse), 0.0)
        dprobs = mm_nt(grads, values)
        dscores = (probs * (dprobs - delta)).astype(bf16)
        dvalue_ref[span, :] += mm_tn(probs.astype(bf16), grads)
        dkey_ref[span, :] += mm_tn(dscores, queries)
        return dquery + mm(dscores, keys)

    dquery = lax.fori_loop(0, tiles, step, jnp.zeros(queries.shape, f32)) * score_scale
    scaled = dquery[:, NOPE:] * table_ref[...]
    lanes = lax.broadcasted_iota(jnp.int32, scaled.shape, 1)
    half = ROPE // 2
    turned = jnp.where(lanes < half, pltpu.roll(scaled, half, 1), -pltpu.roll(scaled, LANES - half, 1))
    dquery_ref[:, :NOPE] = dquery[:, :NOPE].astype(bf16)
    dquery_ref[:, NOPE:] = (scaled + turned)[:, :ROPE].astype(bf16)

    @pl.when(pl.program_id(0) == pl.num_programs(0) - 1)
    def finish():
        def rows(index, carry):
            span = pl.ds(index * key_tile, key_tile)
            dkey = dkey_ref[span, :] * score_scale
            low = jnp.concatenate([dkey[:, :NOPE], dvalue_ref[span, :]], axis=-1).astype(bf16)
            dexpand_ref[span, :] = low
            dlatent_ref[span, :KVR] = mm_nt(low, expand_ref[...]).astype(bf16)
            dlatent_ref[span, KVR:] = dkey[:, NOPE : NOPE + ROPE].astype(bf16)
            return carry

        lax.fori_loop(0, dkey_ref.shape[0] // key_tile, rows, 0)


def attention_tiles(rows, keys):
    tile = min(512, keys)
    row_tile = rows * tile // keys
    return (row_tile, tile)


def attend(positions, queries, keys, values):
    rows, count = queries.shape[0], keys.shape[0]
    row_tile, tile = attention_tiles(rows, count)
    whole = lambda width: pl.BlockSpec((count, width), lambda i: (0, 0))
    part = lambda width: pl.BlockSpec((row_tile, width), lambda i: (i, 0))
    return pl.pallas_call(
        functools.partial(attend_kernel, tile, tile),
        grid=(rows // row_tile,),
        in_specs=[part(1), part(WIDE), whole(WIDE), whole(VHEAD)],
        out_specs=[part(VHEAD), part(VHEAD), part(1)],
        out_shape=[
            jax.ShapeDtypeStruct((rows, VHEAD), f32),
            jax.ShapeDtypeStruct((rows, VHEAD), bf16),
            jax.ShapeDtypeStruct((rows, 1), f32),
        ],
        compiler_params=pltpu.CompilerParams(vmem_limit_bytes=48 * megabytes),
        cost_estimate=pl.CostEstimate(
            flops=rows * count * (QK + VHEAD) * 2,
            bytes_accessed=4 * (rows + count) * (QK + VHEAD),
            transcendentals=rows * count // 2,
        ),
        name="attend",
    )(positions, queries, keys, values)


def attend_grad(positions, table, queries, keys, values, outcome, lse, grads, expand):
    rows, count = queries.shape[0], keys.shape[0]
    row_tile, tile = attention_tiles(rows, count)
    whole = lambda width: pl.BlockSpec((count, width), lambda i: (0, 0))
    part = lambda width: pl.BlockSpec((row_tile, width), lambda i: (i, 0))
    return pl.pallas_call(
        functools.partial(attend_grad_kernel, tile, tile),
        grid=(rows // row_tile,),
        in_specs=[
            part(1), part(LANES), part(WIDE), whole(WIDE), whole(VHEAD), part(VHEAD), part(1),
            part(VHEAD), pl.BlockSpec(expand.shape, lambda i: (0, 0)),
        ],
        out_specs=[part(QK), whole(NOPE + VHEAD), whole(KVR + ROPE)],
        out_shape=[
            jax.ShapeDtypeStruct((rows, QK), bf16),
            jax.ShapeDtypeStruct((count, NOPE + VHEAD), bf16),
            jax.ShapeDtypeStruct((count, KVR + ROPE), bf16),
        ],
        scratch_shapes=[pltpu.VMEM((count, WIDE), f32), pltpu.VMEM((count, VHEAD), f32)],
        compiler_params=pltpu.CompilerParams(vmem_limit_bytes=48 * megabytes),
        cost_estimate=pl.CostEstimate(
            flops=rows * count * (3 * QK + 2 * VHEAD) * 2,
            bytes_accessed=8 * (rows + count) * (QK + VHEAD),
            transcendentals=rows * count // 2,
        ),
        name="attend_grad",
    )(positions, table, queries, keys, values, outcome, lse, grads, expand)


def copy_blocks(base_ref, source, target, copied):
    step = pl.program_id(0)
    first = (base_ref[0] * 2 + (step ^ base_ref[2])) * 4

    def copies(group):
        return [
            pltpu.make_async_copy(
                source[2 * mask + group].at[0],
                target.at[first + (mask ^ base_ref[1])],
                copied.at[mask],
            )
            for mask in range(4)
        ]

    def each(act):
        for group in (0, 1):

            @pl.when(step == group)
            def run():
                for copy in copies(group):
                    act(copy)

    each(lambda copy: copy.start())
    return lambda: each(lambda copy: copy.wait())


def pick_all(pick_ref, gates_ref, blocks):
    return jnp.concatenate(
        [
            jnp.sum(pick_ref[block].astype(f32) * gates_ref[block], axis=-1, keepdims=True)
            for block in blocks
        ],
        axis=0,
    )


def forward_kernel(parts, base_ref, *refs):
    *refs, copied = refs
    ffn_refs, (pick_ref, gates_ref) = refs[:8], refs[8:10]
    gate_refs, rise_refs, down_refs = (refs[10 + i * parts : 10 + (i + 1) * parts] for i in range(3))
    sgate_ref, sup_ref, sdown_ref = refs[10 + 3 * parts : 13 + 3 * parts]
    outs = refs[-(10 + 3 * parts) :]
    out_refs, (tokens_ref, entries_ref, y_ref) = outs[:4], outs[4:7]
    mid_ref, sg_ref, su_ref = outs[7:10]
    m_refs, g_refs, u_refs = (outs[10 + i * parts : 10 + (i + 1) * parts] for i in range(3))
    slots = pick_ref.shape[1]
    blocks = [mask ^ base_ref[1] for mask in range(4)]
    spans = [slice(mask * slots, (mask + 1) * slots) for mask in range(4)]
    wait = copy_blocks(base_ref, ffn_refs, tokens_ref, copied)

    for mask, (block, span) in enumerate(zip(blocks, spans)):
        tokens = block_of_step(ffn_refs, mask)
        entries_ref[span, :] = mm(pick_ref[block], tokens).astype(bf16)
    gates = pick_all(pick_ref, gates_ref, blocks)
    entries = entries_ref[...]
    y = jnp.zeros(entries.shape, f32)
    for p in range(parts):
        gate = mm_nt(entries, gate_refs[p][...])
        rise = mm_nt(entries, rise_refs[p][...])
        g_refs[p][...] = gate.astype(bf16)
        u_refs[p][...] = rise.astype(bf16)
        middle = swiglu(gate, rise)
        m_refs[p][...] = middle
        y = y + mm(middle, down_refs[p][...])
    y = y.astype(bf16)
    y_ref[...] = y
    scaled = (gates * y.astype(f32)).astype(bf16)
    for mask, (block, span) in enumerate(zip(blocks, spans)):
        tokens = block_of_step(ffn_refs, mask)
        sgate = mm(tokens, sgate_ref[...])
        sup = mm(tokens, sup_ref[...])
        sg_ref[block] = sgate.astype(bf16)
        su_ref[block] = sup.astype(bf16)
        middle = swiglu(sgate, sup)
        mid_ref[block] = middle
        placed = mm_tn(pick_ref[block], scaled[span])
        out_refs[mask][0] = (mm(middle, sdown_ref[...]) + placed).astype(bf16)
    wait()


def backward_kernel(parts, base_ref, *refs):
    *refs, copied = refs
    up_refs, (pick_ref, gates_ref, y_ref, sg_ref, su_ref) = refs[:8], refs[8:13]
    g_refs, u_refs = (refs[13 + i * parts : 13 + (i + 1) * parts] for i in range(2))
    rest = refs[13 + 2 * parts :]
    gate_refs, rise_refs, down_refs = (rest[i * parts : (i + 1) * parts] for i in range(3))
    sgate_ref, sup_ref, sdown_ref = rest[3 * parts : 3 + 3 * parts]
    outs = refs[-(8 + 2 * parts) :]
    db_refs, (ups_ref, dy_ref, dgate_ref, pair_ref) = outs[:4], outs[4:8]
    dg_refs, du_refs = (outs[8 + i * parts : 8 + (i + 1) * parts] for i in range(2))
    slots = pick_ref.shape[1]
    blocks = [mask ^ base_ref[1] for mask in range(4)]
    spans = [slice(mask * slots, (mask + 1) * slots) for mask in range(4)]
    wait = copy_blocks(base_ref, up_refs, ups_ref, copied)

    for mask, (block, span) in enumerate(zip(blocks, spans)):
        upstream = block_of_step(up_refs, mask)
        dy_ref[span, :] = mm(pick_ref[block], upstream).astype(bf16)
    gates = pick_all(pick_ref, gates_ref, blocks)
    grad_rows = dy_ref[...].astype(f32)
    dgates = jnp.sum(grad_rows * y_ref[...].astype(f32), axis=-1, keepdims=True)
    dy = (gates * grad_rows).astype(bf16)
    dy_ref[...] = dy
    db = jnp.zeros(dy.shape, f32)
    for p in range(parts):
        dm = mm_nt(dy, down_refs[p][...])
        dg, du = swiglu_grads(g_refs[p][...].astype(f32), u_refs[p][...].astype(f32), dm)
        dg_refs[p][...] = dg
        du_refs[p][...] = du
        db = db + mm(dg, gate_refs[p][...]) + mm(du, rise_refs[p][...])
    db = db.astype(bf16)
    for mask, (block, span) in enumerate(zip(blocks, spans)):
        pick = pick_ref[block]
        dgate_ref[block] = jnp.sum(pick.astype(f32) * dgates[span], axis=0, keepdims=True)
        upstream = block_of_step(up_refs, mask)
        sgate, sup = sg_ref[block].astype(f32), su_ref[block].astype(f32)
        dsg, dsu = swiglu_grads(sgate, sup, mm_nt(upstream, sdown_ref[...]))
        pair_ref[0, block] = dsg
        pair_ref[1, block] = dsu
        db_refs[mask][0] = (
            mm_nt(dsg, sgate_ref[...]) + mm_nt(dsu, sup_ref[...]) + mm_tn(pick, db[span])
        ).astype(bf16)
    wait()


def expert_call(kernel, name, piece, blocks, tiled, weights, held_shapes, held, part, width, flops):
    operands, specs = block_operands(blocks)
    fixed = lambda i, base: (0, 0)

    groups = held_shapes[0][0].shape[0] // 4

    def spec(shape, axis=0):
        tile = tuple(n // groups if d == axis else n for d, n in enumerate(shape))
        at = lambda i, base: tuple(
            base[0] * 2 + (i ^ base[2]) if d == axis else 0 for d in range(len(shape))
        )
        return pl.BlockSpec(tile, at)

    out_specs = [pl.BlockSpec((1, part, width), lambda i, base: (i, 0, 0))] * 4
    for shape, axis in held_shapes:
        out_specs.append(
            pl.BlockSpec(memory_space=pl.ANY) if axis is None else spec(shape.shape, axis)
        )
    results = pl.pallas_call(
        kernel,
        grid_spec=pltpu.PrefetchScalarGridSpec(
            num_scalar_prefetch=1,
            grid=(2,),
            in_specs=specs
            + [spec(v.shape) for v in tiled]
            + [pl.BlockSpec(w.shape, fixed, pipeline_mode=pl.Buffered(1)) for w in weights]
            + [pl.BlockSpec(memory_space=pl.ANY)] * len(held),
            out_specs=out_specs,
            scratch_shapes=[pltpu.SemaphoreType.DMA((4,))],
        ),
        out_shape=[jax.ShapeDtypeStruct((2, part, width), bf16)] * 4
        + [shape for shape, _ in held_shapes],
        input_output_aliases={
            1 + len(operands) + len(tiled) + len(weights) + i: 4 + i for i in range(len(held))
        },
        compiler_params=pltpu.CompilerParams(vmem_limit_bytes=60 * megabytes),
        cost_estimate=pl.CostEstimate(
            flops=flops, bytes_accessed=40 * megabytes, transcendentals=1 << 20
        ),
        name=name,
    )(piece_place(piece), *operands, *tiled, *weights, *held)
    return results[:4], results[4:]


def expert_work(pick, gates, gate_w, up_w, down_w, sgate, sup, sdown):
    ctx, slots, part = pick.shape
    width, hidden = sgate.shape
    parts = len(gate_w)
    inner = [w.shape[0] for w in gate_w]
    weights = [*gate_w, *up_w, *down_w, sgate, sup, sdown]
    whole = lambda *shape, dtype=bf16: jax.ShapeDtypeStruct(shape, dtype)
    blocks = (whole(ctx, part, width), None)
    rows = (whole(ctx * slots, width), 0)
    units = [(whole(ctx * slots, w), 0) for w in inner]
    shared = (whole(ctx, part, hidden), 0)
    flops = 48 * (slots * width * sum(inner) + part * width * hidden)
    forward_shapes = [blocks, rows, rows, shared, shared, shared, *units * 3]
    dgates = (whole(ctx, 1, part, dtype=f32), 0)
    backward_shapes = [blocks, rows, dgates, (whole(2, ctx, part, hidden), 1), *units * 2]

    def forward(piece, tokens, held):
        return expert_call(
            functools.partial(forward_kernel, parts), "experts_forward", piece, tokens, [pick, gates],
            weights, forward_shapes, held, part, width, flops,
        )

    def backward(piece, upstream, done, held):
        _, _, y, _, sg, su, *units = done
        tiled = [pick, gates, y, sg, su, *units[parts:]]
        return expert_call(
            functools.partial(backward_kernel, parts), "experts_backward", piece, upstream, tiled,
            weights, backward_shapes, held, part, width, flops,
        )

    return forward, backward


def shards(
    hidden_in, gain_attn, w_query, w_kv_down, gain_kv, w_kv_up, w_out, gain_ffn, w_router,
    shared_gate, shared_up, shared_down, expert_gate, expert_up, expert_down, routes, cotangent,
):
    part, width = hidden_in.shape[1:]
    ctx, fsdp = lax.axis_size("ctx"), lax.axis_size("fsdp")
    ctx_rank = lax.axis_index("ctx")
    length = part * ctx
    rows = w_query.shape[0]
    experts = w_router.shape[1]
    parts_of_head = ctx // HEADS
    query_part = part // parts_of_head
    first_row = (ctx_rank % parts_of_head) * query_part
    everywhere = ("ctx", "fsdp")

    def join_rows(parts):
        if fsdp != 2:
            return jnp.stack(parts, axis=1).reshape(-1, parts[0].shape[-1])
        rank = lax.axis_index("fsdp")
        whole = jnp.zeros((ctx, 2) + parts[0].shape[1:], parts[0].dtype)
        for place, value in ((rank, parts[0]), (1 - rank, parts[1])):
            whole = lax.dynamic_update_slice_in_dim(whole, value[:, None], place, 1)
        return whole.reshape(-1, parts[0].shape[-1])

    def to_rows(columns, count):
        grid = columns.reshape(ctx, fsdp, count, columns.shape[-1])
        grid = scatter_fsdp(in_fsdp_order([grid[:, i] for i in range(fsdp)]))
        return to_owner(grid.astype(bf16)).astype(f32)

    def head_blocks(values):
        blocks = values.reshape(values.shape[0], HEADS, -1).transpose(1, 0, 2)
        return jnp.repeat(blocks, parts_of_head, axis=0)

    def from_head_blocks(blocks):
        blocks = blocks.reshape(HEADS, parts_of_head, *blocks.shape[1:]).sum(axis=1)
        return blocks.transpose(1, 0, 2).reshape(blocks.shape[1], -1)

    compressed_width = KVR + ROPE
    turned_width = compressed_width + ROPE
    kv_rows = gain_kv.shape[0]
    small_width = turned_width + experts + 3
    small = jnp.concatenate(
        [
            w_kv_down,
            turn_columns(w_kv_down[:, KVR:]),
            w_router,
            gain_attn[:, None],
            gain_ffn[:, None],
            jnp.pad(gain_kv, (0, rows - kv_rows))[:, None],
            jnp.zeros((rows, -small_width % 128), bf16),
        ],
        axis=1,
    )
    small_full = lax.all_gather(small, everywhere, axis=0, tiled=True)
    reduce_full = small_full[:, :compressed_width]
    router_full = small_full[:, turned_width : small_width - 3]
    attn_gain = small_full[:, small_width - 3].astype(f32)
    ffn_gain = small_full[:, small_width - 2].astype(f32)
    kv_gain = small_full[:, small_width - 1].reshape(ctx * fsdp, rows)[:, :kv_rows]
    kv_gain = kv_gain.reshape(KVR).astype(f32)

    tokens_low = hidden_in.reshape(part, width)
    upstream_low = cotangent.reshape(part, width)
    hidden_shared = shared_gate.shape[1] // ctx
    query_blocks = head_blocks(w_query)
    route_rows = routes.reshape(part, TOP)
    chosen_hot = route_rows[:, :, None] == jnp.arange(experts, dtype=jnp.int32)[None, None, :]
    columns = [
        query_blocks,
        turn_columns(query_blocks[..., NOPE:]),
        head_blocks(w_kv_up).reshape(ctx, rows, -1),
        jnp.any(chosen_hot, axis=1).astype(bf16).T.reshape(ctx, rows, -1),
    ]
    column_blocks = jnp.concatenate(columns, axis=-1)
    expand_end = WIDE + columns[2].shape[-1]

    def joined_stage(received, _):
        return received, join_rows(gather_fsdp(received[..., :expand_end]))

    tokens_all, (received, by_rows) = gather_ctx(
        tokens_low, *[lambda *_: None] * 2, lambda *_: to_owner(column_blocks), joined_stage
    )
    named_all = received[..., expand_end:].reshape(ctx, part)
    query_w = by_rows[:, :WIDE]
    expand = by_rows[:, WIDE:].reshape(KVR, NOPE + VHEAD)
    output_full = lax.all_gather(w_out, everywhere, axis=0, tiled=True)

    upstream_late, gate_late, up_late, _ = lax.optimization_barrier(
        (upstream_low, shared_gate, shared_up, tokens_all[-1][3][1][0])
    )
    columns = [v.reshape(rows, ctx, hidden_shared) for v in (gate_late, up_late)]
    shared_blocks = jnp.concatenate(columns, axis=2).transpose(1, 0, 2)
    shared_back = jnp.concatenate(in_fsdp_order(gather_fsdp(shared_down)), axis=0)
    gate_parts = gather_fsdp(expert_gate[0].T)
    up_parts = gather_fsdp(expert_up[0].T)
    down_parts = gather_fsdp(expert_down[0].T)

    slot_cap = min(part, part * TOP * 4 // (3 * experts))
    until = jnp.arange(part)[:, None] <= jnp.arange(part)[None, :]
    ordinal = mm(named_all, until.astype(bf16)) - 1.0
    slots = jnp.arange(slot_cap, dtype=f32)[None, :, None]
    pick = ((ordinal[:, None, :] == slots) & (named_all[:, None, :] > 0)).astype(bf16)

    cosine, sine = rope_tables(jnp.arange(length, dtype=jnp.int32))
    table = jnp.concatenate([cosine, sine], axis=-1)
    def query_rows(values):
        if parts_of_head == 1:
            return values
        blocks = values.reshape(ctx, part, values.shape[-1])
        blocks = lax.dynamic_slice_in_dim(blocks, first_row, query_part, 1)
        return blocks.reshape(ctx * query_part, values.shape[-1])

    def to_heads(values):
        split = values.reshape(parts_of_head, query_part, HEADS, values.shape[-1])
        sent = split.transpose(2, 0, 1, 3).reshape(ctx, query_part, values.shape[-1])
        return to_owner(sent).reshape(ctx * query_part, values.shape[-1])

    def from_heads(values):
        back = to_owner(values.reshape(ctx, query_part, values.shape[-1]))
        back = back.reshape(HEADS, parts_of_head, query_part, values.shape[-1])
        return back.transpose(1, 2, 0, 3).reshape(part, HEADS, values.shape[-1])

    query_pos = query_rows(jnp.arange(length, dtype=jnp.int32)[:, None])

    def first_stage(*_):
        return project(
            tokens_all, attn_gain[None], kv_gain[None], table, query_w, small_full, expand
        )

    def second_stage(projected, _):
        _, query_all, key_head, value_head, _ = projected
        outcome = attend(query_pos, query_rows(query_all), key_head, value_head)
        return projected, outcome, to_owner(shared_blocks)

    def third_stage(held, _):
        projected, (outcome, outcome_low, lse), shared_in = held
        shared_in = join_rows(gather_fsdp(shared_in))
        return projected, outcome, lse, from_heads(outcome_low), shared_in

    upstream_all, (projected, outcome, lse, attended, shared_in) = gather_ctx(
        upstream_late, first_stage, second_stage, third_stage
    )
    shared_in = (shared_in[:, :hidden_shared], shared_in[:, hidden_shared:])
    normed_all, query_all, key_head, value_head, latent_all = projected
    query_head = query_rows(query_all)
    attended = attended.reshape(part, HEADS * VHEAD)
    tokens = tokens_low.astype(f32)
    residual = tokens + mm(attended, output_full)

    ffn_factor = rms_factor(residual)
    ffn_low = (residual * ffn_factor * ffn_gain).astype(bf16)
    logits = mm(ffn_low, router_full)
    chosen = jnp.sum(jnp.where(chosen_hot, logits[:, None, :], 0.0), axis=-1)
    gate_share = jax.nn.softmax(chosen, axis=-1)
    gates_own = jnp.sum(jnp.where(chosen_hot, gate_share[..., None], 0.0), axis=1)

    work = lambda gates_all: expert_work(
        pick, gates_all[:, None, :], gate_parts, up_parts, down_parts, *shared_in, shared_back
    )

    def near_forward(gates_all, pieces):
        forward, _ = work(gates_all)
        return gates_all, forward(0, pieces[0], [])

    def near_backward(held, _):
        gates_all, (out, done) = held
        arrived = plane_hops([out]) if exchanges() else []
        db, back = work(gates_all)[1](0, upstream_all[0], done, [])
        return gates_all, out, done, db, back, arrived

    ffn_all, (gates_all, out, done, db, back, out_arrived) = gather_ctx(
        ffn_low, lambda *_: None, lambda *_: to_owner(gates_own.T), near_forward, near_backward
    )
    forward, backward = work(gates_all)
    out_parts, grad_parts, grad_arrived = [out], [db], []
    for piece in range(1, len(ffn_all)):
        if exchanges():
            grad_arrived = plane_hops([db])
        out, done = forward(piece, ffn_all[piece], done)
        out, done, grad_arrived = together(out, done, grad_arrived)
        if exchanges():
            out_arrived = [*out_arrived, *plane_hops([out])]
        db, back = backward(piece, upstream_all[piece], done, back)
        db, back, out_arrived = together(db, back, out_arrived)
        out_parts.append(out)
        grad_parts.append(db)
    query_late, _ = lax.optimization_barrier((w_query, ffn_all[-1][3][1][0]))
    query_full = lax.all_gather(query_late, everywhere, axis=0, tiled=True)
    tokens_flat, entries, _, shared_mid, _, _, *units = done
    middle = units[:fsdp]
    upstream_flat, grad_entries, token_dgates, shared_pair, *units = back
    gate_low, up_low = units[:fsdp], units[fsdp:]
    tokens_flat, upstream_flat, shared_mid, *shared_pair = (
        v.reshape(length, v.shape[-1])
        for v in (tokens_flat, upstream_flat, shared_mid, shared_pair[0], shared_pair[1])
    )

    sums = [(middle, grad_entries), (gate_low, entries), (up_low, entries)]
    sums = [[mm_tn(left, right) for left in lefts] for lefts, right in sums]
    sums = [[own, *(v.astype(bf16) for v in others)] for own, *others in sums]
    shared_sums = [mm_tn(shared_mid, upstream_flat), *(mm_tn(tokens_flat, v) for v in shared_pair)]
    ffn_grad, (sums, dgates_own), (shared_sums, query_full) = scatter_ctx(
        grad_parts, (sums, to_owner(token_dgates[:, 0])), (shared_sums, query_full), grad_arrived
    )
    grad_gates = jnp.sum(jnp.where(chosen_hot, dgates_own.T[:, None, :], 0.0), axis=-1)
    grad_chosen = gate_share * (
        grad_gates - jnp.sum(gate_share * grad_gates, axis=-1, keepdims=True)
    )
    grad_logits = jnp.sum(jnp.where(chosen_hot, grad_chosen[..., None], 0.0), axis=1).astype(bf16)
    grad_router = mm_tn(ffn_low, grad_logits)
    ffn_grad = ffn_grad + mm_nt(grad_logits, router_full)
    upstream = upstream_low.astype(f32)
    ffn_grad_in, grad_ffn_gain = rms_backward(residual, ffn_factor, ffn_gain, ffn_grad)
    grad_residual = upstream + ffn_grad_in
    grad_residual_low = grad_residual.astype(bf16)

    grad_attended = mm_nt(grad_residual_low, output_full).astype(bf16)
    grad_head = to_heads(grad_attended.reshape(part, HEADS, VHEAD))
    output_heads = attended.reshape(part, ctx, fsdp, rows)
    output_heads = in_fsdp_order([output_heads[:, :, i].reshape(part, -1) for i in range(fsdp)])
    grad_output = scatter_fsdp([mm_tn(v, grad_residual_low) for v in output_heads])
    grad_output = grad_output.astype(bf16).reshape(ctx, rows, width)
    grad_output = lax.psum_scatter(grad_output, "ctx", scatter_dimension=0).astype(f32)
    attention_grads = attend_grad(
        query_pos, query_rows(table), query_head, key_head, value_head, outcome, lse, grad_head, expand
    )
    if exchanges():
        out_sum, out_line = line_hops(out_parts, out_arrived)
        attention_grads, out_line = together(attention_grads, out_line)
        out_sum = plus(out_sum, *out_line)
    else:
        out_sum = whole_sum(out_parts)
    grad_query, grad_expanded, latent_part = attention_grads
    latent_part, query_own, sums, shared_sums = together(
        to_owner(latent_part.reshape(ctx, part, -1)), from_heads(grad_query), sums, shared_sums
    )
    latent_sum = jnp.sum(latent_part.astype(f32), axis=0)
    grad_normed = mm_nt(query_own.reshape(part, HEADS * QK), query_full)
    grad_expert_down, grad_expert_gate, grad_expert_up = (scatter_fsdp(v).T[None] for v in sums)
    down_rows = shared_down.shape[0]
    grad_back = shared_sums[0].reshape(fsdp, down_rows, width)
    grad_shared_down = scatter_fsdp(in_fsdp_order([grad_back[i] for i in range(fsdp)]))
    grad_in = to_rows(jnp.concatenate(shared_sums[1:], axis=-1), rows).transpose(1, 0, 2)
    grad_shared_gate = grad_in[..., :hidden_shared].reshape(rows, ctx * hidden_shared)
    grad_shared_up = grad_in[..., hidden_shared:].reshape(rows, ctx * hidden_shared)

    grad_query_w = mm_tn(query_rows(normed_all), grad_query).reshape(ctx, fsdp, rows, QK)
    grad_expand = mm_tn(latent_all, grad_expanded).reshape(ctx, fsdp, rows, -1)
    by_heads = jnp.concatenate([grad_query_w, grad_expand], axis=-1)
    by_heads = to_rows(by_heads.reshape(width, by_heads.shape[-1]), rows)
    grad_query_w = from_head_blocks(by_heads[..., :QK])
    grad_expand = from_head_blocks(by_heads[..., QK:].reshape(ctx, kv_rows, NOPE + VHEAD))

    own_rows = ctx_rank * part
    own_normed = lax.dynamic_slice_in_dim(normed_all, own_rows, part, 0)
    latent_raw = mm(own_normed, reduce_full[:, :KVR])
    grad_latent_raw, _ = rms_backward(
        latent_raw, rms_factor(latent_raw), kv_gain, latent_sum[:, :KVR]
    )
    own_cos = lax.dynamic_slice_in_dim(cosine, own_rows, part, 0)
    own_sin = lax.dynamic_slice_in_dim(sine, own_rows, part, 0)
    grad_compressed = jnp.concatenate(
        [grad_latent_raw, unrotate(latent_sum[:, KVR:compressed_width], own_cos, own_sin)], axis=-1
    ).astype(bf16)
    grad_small = jnp.concatenate(
        [
            mm_tn(own_normed, grad_compressed).astype(bf16),
            grad_router.astype(bf16),
            grad_ffn_gain[:, None].astype(bf16),
            jnp.zeros((width, -(compressed_width + experts + 1) % 128), bf16),
        ],
        axis=1,
    ).reshape(ctx, fsdp, rows, -1)
    grad_small = scatter_fsdp(in_fsdp_order([grad_small[:, i] for i in range(fsdp)]))
    grad_small = jnp.sum(to_owner(grad_small.astype(bf16)).astype(f32), axis=0)
    grad_reduce = grad_small[:, :compressed_width]
    grad_normed = grad_normed + mm_nt(grad_compressed, reduce_full)
    attn_grad_in, _ = rms_backward(tokens, rms_factor(tokens), attn_gain, grad_normed)
    grad_hidden_in = (grad_residual + attn_grad_in)[None]

    def gain_grad(gain, pairs):
        total = sum(jnp.sum(w.astype(f32) * g, axis=-1) for w, g in pairs)
        return total / gain.astype(f32)

    grad_attn_gain = gain_grad(gain_attn, [(w_query, grad_query_w), (w_kv_down, grad_reduce)])
    grad_kv_gain = gain_grad(gain_kv, [(w_kv_up, grad_expand)])
    out_sum, kept, _ = lax.optimization_barrier((out_sum, residual, latent_sum))
    hidden_out = (kept + out_sum).astype(bf16)
    after = compressed_width + experts
    return (
        hidden_out[None],
        grad_hidden_in,
        grad_attn_gain,
        grad_query_w,
        grad_reduce,
        grad_kv_gain,
        grad_expand,
        grad_output,
        grad_small[:, after],
        grad_small[:, compressed_width:after],
        grad_shared_gate,
        grad_shared_up,
        grad_shared_down,
        grad_expert_gate,
        grad_expert_up,
        grad_expert_down,
    )


def solution(mesh):
    dense = P(("ctx", "fsdp"), None)
    gain = P(("ctx", "fsdp"))
    tokens = P("fsdp", "ctx", None)
    expert = P("ctx", None, "fsdp")
    return jax.shard_map(
        shards,
        mesh=mesh,
        in_specs=(
            tokens, gain, dense, dense, gain, dense, dense, gain, dense, dense, dense, dense,
            expert, expert, expert, tokens, tokens,
        ),
        out_specs=(
            tokens, tokens, gain, dense, dense, gain, dense, dense, gain, dense, dense, dense,
            dense, expert, expert, expert,
        ),
        check_vma=False,
    )
```

```python
import functools
import math

import jax
import jax.numpy as jnp
from jax import lax
from jax.experimental import pallas as pl
from jax.experimental.pallas import tpu as pltpu
from jax.sharding import PartitionSpec as P

HEADS = 16
NOPE = 128
ROPE = 64
VHEAD = 128
KVR = 512
TOP = 6
QK = NOPE + ROPE

epsilon = 1e-06
rope_base = 10000.0
masked_score = -1e30
score_scale = 1.0 / math.sqrt(QK)

bf16 = jnp.bfloat16
f32 = jnp.float32


def mm(left, right):
    return jnp.dot(left, right, preferred_element_type=f32)


def mm_nt(left, right):
    return lax.dot_general(left, right, (((1,), (1,)), ((), ())), preferred_element_type=f32)


def mm_tn(left, right):
    return lax.dot_general(left, right, (((0,), (0,)), ((), ())), preferred_element_type=f32)


def rms_factor(values):
    return lax.rsqrt(jnp.mean(values * values, axis=-1, keepdims=True) + epsilon)


def rms_backward(values, factor, gain, upstream):
    weighted = upstream * gain
    inner_mean = jnp.mean(weighted * values, axis=-1, keepdims=True)
    grad_in = factor * weighted - values * (factor * factor * factor) * inner_mean
    grad_gain = jnp.sum(upstream * values * factor, axis=0)
    return (grad_in, grad_gain)


def rope_tables(positions):
    half_width = ROPE // 2
    frequency = jnp.exp(jnp.arange(half_width, dtype=f32) * (-math.log(rope_base) / half_width))
    angles = positions.astype(f32)[:, None] * frequency[None, :]
    angles = jnp.concatenate([angles, angles], axis=-1)
    return (jnp.cos(angles), jnp.sin(angles))


def rotate(values, cosine, sine):
    half_width = values.shape[-1] // 2
    turned = jnp.concatenate([-values[..., half_width:], values[..., :half_width]], axis=-1)
    return values * cosine + turned * sine


def unrotate(upstream, cosine, sine):
    half_width = upstream.shape[-1] // 2
    rotated = upstream * sine
    turned = jnp.concatenate([rotated[..., half_width:], -rotated[..., :half_width]], axis=-1)
    return upstream * cosine + turned


def swiglu(gate_pre, up_pre):
    return (jax.nn.silu(gate_pre) * up_pre).astype(bf16)


def swiglu_grads(gate_pre, up_pre, grad_mid):
    squash = jax.nn.sigmoid(gate_pre)
    grad_gate = grad_mid * up_pre * squash * (1.0 + gate_pre * (1.0 - squash))
    grad_up = grad_mid * (gate_pre * squash)
    return (grad_gate.astype(bf16), grad_up.astype(bf16))


def exchanges():
    return lax.axis_size("ctx") == 16 and lax.axis_size("fsdp") == 2


def hop(value, mask):
    return lax.ppermute(value, "ctx", [(i, i ^ mask) for i in range(16)])


def together(*values):
    return lax.optimization_barrier(values)


def gather_ctx(block, *stages, early=False):
    held = None
    if not exchanges():
        whole = lax.all_gather(block, "ctx", axis=0)
        at = lambda piece, mask: [(whole, 8 * piece + 4 * group + mask) for group in (0, 1)]
        pieces = [[at(piece, mask) for mask in range(4)] for piece in range(whole.shape[0] // 8)]
        for stage in stages:
            held = stage(held, pieces)
        return pieces, held

    def end(number, *hops):
        nonlocal held
        if number < len(stages):
            held = stages[number](held, pieces)
        held, *hops = together(held, *hops)
        return hops

    pieces = []

    alone = lambda values: [(value[None], 0) for value in values]
    both = lambda values: [(values, 0), (values, 1)]
    near, far, one, two = end(0, *(hop(block, mask) for mask in (4, 8, 1, 2)))
    if early:
        far_near, three, *near_others = end(
            1, hop(far, 4), hop(two, 1), *(hop(near, mask) for mask in (1, 2, 3))
        )
        pieces = [[alone(v) for v in zip((block, one, two, three), (near, *near_others))]]
    else:
        far_near, three, *near_others = end(
            1, hop(far, 4), hop(two, 1), *(hop(near, mask) for mask in (1, 2))
        )
    pair = jnp.stack([far, far_near])
    relayed = () if early else (hop(three, 4),)
    far_one, far_two, *relayed = end(2, hop(pair, 1), hop(pair, 2), *relayed)
    if not early:
        near_others = [*near_others, *relayed]
        pieces = [[alone(v) for v in zip((block, one, two, three), (near, *near_others))]]
    far_three = end(3, hop(far_two[0], 1), hop(far_one[1], 2))
    return [*pieces, [both(pair), both(far_one), both(far_two), alone(far_three)]], held


def block_operands(piece):
    blocks = [block for mask in piece for block in mask]
    specs = [
        pl.BlockSpec(
            (1, *array.shape[1:]), lambda i, base, at=at: (at, 0, 0), pipeline_mode=pl.Buffered(1)
        )
        for array, at in blocks
    ]
    return [array for array, _ in blocks], specs


def block_of_step(refs, mask):
    return jnp.where(pl.program_id(0) == 0, refs[2 * mask][0], refs[2 * mask + 1][0])


def plus(*values):
    return sum(value.astype(f32) for value in values)


def plane_hops(pieces):
    return [[hop(value, mask) for mask, value in enumerate(piece) if mask] for piece in pieces]


def line_hops(pieces, arrived):
    near, far = (plus(piece[0], *values) for piece, values in zip(pieces, arrived))
    sent = ((near[1], 4), (far[0], 8), (far[1], 12))
    return near[0], [hop(value.astype(bf16), mask) for value, mask in sent]


def whole_sum(pieces):
    whole = jnp.stack([jnp.stack(piece, axis=1) for piece in pieces])
    whole = whole.reshape(-1, *whole.shape[3:])
    return lax.psum_scatter(whole, "ctx", scatter_dimension=0).astype(f32)


def scatter_ctx(pieces, beside_plane=(), beside_line=(), near=None):
    if not exchanges():
        return whole_sum(pieces), beside_plane, beside_line
    near = near or plane_hops(pieces[:1])
    near, far, beside_plane = together(near, plane_hops(pieces[1:]), beside_plane)
    own, arrived = line_hops(pieces, [*near, *far])
    arrived, beside_line = together(arrived, beside_line)
    return plus(own, *arrived), beside_plane, beside_line


def piece_place(piece):
    if not exchanges():
        return jnp.array([piece, 0, 0], jnp.int32)
    own = lax.axis_index("ctx")
    return jnp.stack([(own >> 3) ^ piece, own & 3, (own >> 2) & 1])


def swap_cores(value):
    return lax.ppermute(value, "fsdp", [(0, 1), (1, 0)])


def gather_fsdp(block):
    if lax.axis_size("fsdp") == 2:
        return [block, swap_cores(block)]
    whole = lax.all_gather(block, "fsdp", axis=0)
    return [whole[i] for i in range(lax.axis_size("fsdp"))]


def scatter_fsdp(parts):
    if lax.axis_size("fsdp") == 2:
        return parts[0].astype(f32) + swap_cores(parts[1].astype(bf16)).astype(f32)
    stacked = jnp.stack([part.astype(bf16) for part in parts])
    return lax.psum_scatter(stacked, "fsdp", scatter_dimension=0).astype(f32)


def in_fsdp_order(parts):
    if lax.axis_size("fsdp") == 2:
        low = lax.axis_index("fsdp") == 0
        return [jnp.where(low, parts[0], parts[1]), jnp.where(low, parts[1], parts[0])]
    return parts


def to_owner(blocks):
    return lax.all_to_all(blocks, "ctx", split_axis=0, concat_axis=0, tiled=True)


LANES = 128
WIDE = NOPE + 2 * ROPE
megabytes = 1024 * 1024


def turn_columns(weights):
    half = weights.shape[-1] // 2
    return jnp.concatenate([-weights[..., half:], weights[..., :half]], axis=-1)


def project_kernel(base_ref, *refs):
    token_refs = refs[:8]
    gain_ref, kv_gain_ref, table_ref, query_w_ref, reduce_ref, expand_ref = refs[8:14]
    normed_ref, query_ref, key_ref, value_ref, latent_ref = refs[-5:]
    part = token_refs[0].shape[1]
    first_half = lax.broadcasted_iota(jnp.int32, (part, LANES), 1) < ROPE
    for mask in range(4):
        span = pl.ds(pl.multiple_of((mask ^ base_ref[1]) * part, part), part)
        tokens = block_of_step(token_refs, mask).astype(f32)
        normed = (tokens * rms_factor(tokens) * gain_ref[...]).astype(bf16)
        normed_ref[span, :] = normed
        table = table_ref[span, :]

        def rope(values):
            scaled = values * table
            return scaled + pltpu.roll(scaled, ROPE, 1)

        queries = mm(normed, query_w_ref[...])
        query_ref[span, :NOPE] = queries[:, :NOPE].astype(bf16)
        query_ref[span, NOPE:] = jnp.where(first_half, rope(queries[:, NOPE:]), 0.0).astype(bf16)
        compressed = mm(normed, reduce_ref[...])
        raw = compressed[:, :KVR]
        latent = (raw * rms_factor(raw) * kv_gain_ref[...]).astype(bf16)
        latent_ref[span, :] = latent
        expanded = mm(latent, expand_ref[...]).astype(bf16)
        key_ref[span, :NOPE] = expanded[:, :NOPE]
        key_ref[span, NOPE:] = rope(compressed[:, KVR:]).astype(bf16)
        value_ref[span, :] = expanded[:, NOPE:]


def project(pieces, gain, kv_gain, table, query_w, reduce_w, expand):
    length, width = table.shape[0], query_w.shape[0]
    widths = [width, WIDE, WIDE, VHEAD, KVR]
    held = []
    for piece, blocks in enumerate(pieces):
        blocks, block_specs = block_operands(blocks)
        steps, part = 2, blocks[0].shape[1]
        tile = 4 * part
        at = lambda i, base: (base[0] * 2 + (i ^ base[2]), 0)
        fixed = lambda i, base: (0, 0)
        whole = lambda shape: pl.BlockSpec(shape, fixed, pipeline_mode=pl.Buffered(1))
        count = steps * tile
        held = pl.pallas_call(
            project_kernel,
            grid_spec=pltpu.PrefetchScalarGridSpec(
                num_scalar_prefetch=1,
                grid=(steps,),
                in_specs=block_specs
                + [
                    whole((1, width)),
                    whole((1, KVR)),
                    pl.BlockSpec((tile, LANES), at),
                    whole((width, WIDE)),
                    whole((width, KVR + LANES)),
                    whole((KVR, NOPE + VHEAD)),
                ]
                + [pl.BlockSpec(memory_space=pl.ANY)] * len(held),
                out_specs=[pl.BlockSpec((tile, w), at) for w in widths],
            ),
            out_shape=[jax.ShapeDtypeStruct((length, w), bf16) for w in widths],
            input_output_aliases={15 + i: i for i in range(len(held))},
            compiler_params=pltpu.CompilerParams(vmem_limit_bytes=56 * megabytes),
            cost_estimate=pl.CostEstimate(
                flops=2 * count * width * (WIDE + KVR + LANES),
                bytes_accessed=4 * count * width + 2 * width * (WIDE + KVR + LANES),
                transcendentals=0,
            ),
            name="project",
        )(piece_place(piece), *blocks, gain, kv_gain, table, query_w, reduce_w, expand, *held)
    return held


def attend_kernel(key_tile, reach, pos_ref, query_ref, key_ref, value_ref, out_ref, low_ref, lse_ref):
    queries = query_ref[...]
    rows = queries.shape[0]
    positions = pos_ref[...]
    tiles = (pl.program_id(0) + 1) * reach // key_tile

    def step(index, carry):
        top, total, running = carry
        keys = key_ref[pl.ds(index * key_tile, key_tile), :]
        values = value_ref[pl.ds(index * key_tile, key_tile), :]
        scores = mm_nt(queries, keys) * score_scale
        key_pos = index * key_tile + lax.broadcasted_iota(jnp.int32, scores.shape, 1)
        scores = jnp.where(key_pos <= positions, scores, masked_score)
        new_top = jnp.maximum(top, jnp.max(scores, axis=-1, keepdims=True))
        weights = jnp.exp(scores - new_top)
        shrink = jnp.exp(top - new_top)
        total = total * shrink + jnp.sum(weights, axis=-1, keepdims=True)
        running = running * shrink + mm(weights.astype(bf16), values)
        return (new_top, total, running)

    start = (
        jnp.full((rows, 1), masked_score, f32),
        jnp.zeros((rows, 1), f32),
        jnp.zeros((rows, VHEAD), f32),
    )
    top, total, running = lax.fori_loop(0, tiles, step, start)
    outcome = running / total
    out_ref[...] = outcome
    low_ref[...] = outcome.astype(bf16)
    lse_ref[...] = top + jnp.log(total)


def attend_grad_kernel(
    key_tile, reach, pos_ref, table_ref, query_ref, key_ref, value_ref, out_ref, lse_ref, grad_ref,
    expand_ref, dquery_ref, dexpand_ref, dlatent_ref, dkey_ref, dvalue_ref,
):
    @pl.when(pl.program_id(0) == 0)
    def clear():
        dkey_ref[...] = jnp.zeros_like(dkey_ref)
        dvalue_ref[...] = jnp.zeros_like(dvalue_ref)

    queries = query_ref[...]
    grads = grad_ref[...]
    positions = pos_ref[...]
    lse = lse_ref[...]
    delta = jnp.sum(grads.astype(f32) * out_ref[...], axis=-1, keepdims=True)
    tiles = (pl.program_id(0) + 1) * reach // key_tile

    def step(index, dquery):
        span = pl.ds(index * key_tile, key_tile)
        keys = key_ref[span, :]
        values = value_ref[span, :]
        scores = mm_nt(queries, keys) * score_scale
        key_pos = index * key_tile + lax.broadcasted_iota(jnp.int32, scores.shape, 1)
        probs = jnp.where(key_pos <= positions, jnp.exp(scores - lse), 0.0)
        dprobs = mm_nt(grads, values)
        dscores = (probs * (dprobs - delta)).astype(bf16)
        dvalue_ref[span, :] += mm_tn(probs.astype(bf16), grads)
        dkey_ref[span, :] += mm_tn(dscores, queries)
        return dquery + mm(dscores, keys)

    dquery = lax.fori_loop(0, tiles, step, jnp.zeros(queries.shape, f32)) * score_scale
    scaled = dquery[:, NOPE:] * table_ref[...]
    lanes = lax.broadcasted_iota(jnp.int32, scaled.shape, 1)
    half = ROPE // 2
    turned = jnp.where(lanes < half, pltpu.roll(scaled, half, 1), -pltpu.roll(scaled, LANES - half, 1))
    dquery_ref[:, :NOPE] = dquery[:, :NOPE].astype(bf16)
    dquery_ref[:, NOPE:] = (scaled + turned)[:, :ROPE].astype(bf16)

    @pl.when(pl.program_id(0) == pl.num_programs(0) - 1)
    def finish():
        def rows(index, carry):
            span = pl.ds(index * key_tile, key_tile)
            dkey = dkey_ref[span, :] * score_scale
            low = jnp.concatenate([dkey[:, :NOPE], dvalue_ref[span, :]], axis=-1).astype(bf16)
            dexpand_ref[span, :] = low
            dlatent_ref[span, :KVR] = mm_nt(low, expand_ref[...]).astype(bf16)
            dlatent_ref[span, KVR:] = dkey[:, NOPE : NOPE + ROPE].astype(bf16)
            return carry

        lax.fori_loop(0, dkey_ref.shape[0] // key_tile, rows, 0)


def attention_tiles(rows, keys):
    tile = min(512, keys)
    row_tile = rows * tile // keys
    return (row_tile, tile)


def attend(positions, queries, keys, values):
    rows, count = queries.shape[0], keys.shape[0]
    row_tile, tile = attention_tiles(rows, count)
    whole = lambda width: pl.BlockSpec((count, width), lambda i: (0, 0))
    part = lambda width: pl.BlockSpec((row_tile, width), lambda i: (i, 0))
    return pl.pallas_call(
        functools.partial(attend_kernel, tile, tile),
        grid=(rows // row_tile,),
        in_specs=[part(1), part(WIDE), whole(WIDE), whole(VHEAD)],
        out_specs=[part(VHEAD), part(VHEAD), part(1)],
        out_shape=[
            jax.ShapeDtypeStruct((rows, VHEAD), f32),
            jax.ShapeDtypeStruct((rows, VHEAD), bf16),
            jax.ShapeDtypeStruct((rows, 1), f32),
        ],
        compiler_params=pltpu.CompilerParams(vmem_limit_bytes=48 * megabytes),
        cost_estimate=pl.CostEstimate(
            flops=rows * count * (QK + VHEAD) * 2,
            bytes_accessed=4 * (rows + count) * (QK + VHEAD),
            transcendentals=rows * count // 2,
        ),
        name="attend",
    )(positions, queries, keys, values)


def attend_grad(positions, table, queries, keys, values, outcome, lse, grads, expand):
    rows, count = queries.shape[0], keys.shape[0]
    row_tile, tile = attention_tiles(rows, count)
    whole = lambda width: pl.BlockSpec((count, width), lambda i: (0, 0))
    part = lambda width: pl.BlockSpec((row_tile, width), lambda i: (i, 0))
    return pl.pallas_call(
        functools.partial(attend_grad_kernel, tile, tile),
        grid=(rows // row_tile,),
        in_specs=[
            part(1), part(LANES), part(WIDE), whole(WIDE), whole(VHEAD), part(VHEAD), part(1),
            part(VHEAD), pl.BlockSpec(expand.shape, lambda i: (0, 0)),
        ],
        out_specs=[part(QK), whole(NOPE + VHEAD), whole(KVR + ROPE)],
        out_shape=[
            jax.ShapeDtypeStruct((rows, QK), bf16),
            jax.ShapeDtypeStruct((count, NOPE + VHEAD), bf16),
            jax.ShapeDtypeStruct((count, KVR + ROPE), bf16),
        ],
        scratch_shapes=[pltpu.VMEM((count, WIDE), f32), pltpu.VMEM((count, VHEAD), f32)],
        compiler_params=pltpu.CompilerParams(vmem_limit_bytes=48 * megabytes),
        cost_estimate=pl.CostEstimate(
            flops=rows * count * (3 * QK + 2 * VHEAD) * 2,
            bytes_accessed=8 * (rows + count) * (QK + VHEAD),
            transcendentals=rows * count // 2,
        ),
        name="attend_grad",
    )(positions, table, queries, keys, values, outcome, lse, grads, expand)


def copy_blocks(base_ref, source, target, copied):
    step = pl.program_id(0)
    first = (base_ref[0] * 2 + (step ^ base_ref[2])) * 4

    def copies(group):
        return [
            pltpu.make_async_copy(
                source[2 * mask + group].at[0],
                target.at[first + (mask ^ base_ref[1])],
                copied.at[mask],
            )
            for mask in range(4)
        ]

    def each(act):
        for group in (0, 1):

            @pl.when(step == group)
            def run():
                for copy in copies(group):
                    act(copy)

    each(lambda copy: copy.start())
    return lambda: each(lambda copy: copy.wait())


def pick_all(pick_ref, gates_ref, blocks):
    return jnp.concatenate(
        [
            jnp.sum(pick_ref[block].astype(f32) * gates_ref[block], axis=-1, keepdims=True)
            for block in blocks
        ],
        axis=0,
    )


def forward_kernel(parts, base_ref, *refs):
    *refs, copied = refs
    ffn_refs, (pick_ref, gates_ref) = refs[:8], refs[8:10]
    gate_refs, rise_refs, down_refs = (refs[10 + i * parts : 10 + (i + 1) * parts] for i in range(3))
    sgate_ref, sup_ref, sdown_ref = refs[10 + 3 * parts : 13 + 3 * parts]
    outs = refs[-(10 + 3 * parts) :]
    out_refs, (tokens_ref, entries_ref, y_ref) = outs[:4], outs[4:7]
    mid_ref, sg_ref, su_ref = outs[7:10]
    m_refs, g_refs, u_refs = (outs[10 + i * parts : 10 + (i + 1) * parts] for i in range(3))
    slots = pick_ref.shape[1]
    blocks = [mask ^ base_ref[1] for mask in range(4)]
    spans = [slice(mask * slots, (mask + 1) * slots) for mask in range(4)]
    wait = copy_blocks(base_ref, ffn_refs, tokens_ref, copied)

    for mask, (block, span) in enumerate(zip(blocks, spans)):
        tokens = block_of_step(ffn_refs, mask)
        entries_ref[span, :] = mm(pick_ref[block], tokens).astype(bf16)
    gates = pick_all(pick_ref, gates_ref, blocks)
    entries = entries_ref[...]
    y = jnp.zeros(entries.shape, f32)
    for p in range(parts):
        gate = mm_nt(entries, gate_refs[p][...])
        rise = mm_nt(entries, rise_refs[p][...])
        g_refs[p][...] = gate.astype(bf16)
        u_refs[p][...] = rise.astype(bf16)
        middle = swiglu(gate, rise)
        m_refs[p][...] = middle
        y = y + mm(middle, down_refs[p][...])
    y = y.astype(bf16)
    y_ref[...] = y
    scaled = (gates * y.astype(f32)).astype(bf16)
    for mask, (block, span) in enumerate(zip(blocks, spans)):
        tokens = block_of_step(ffn_refs, mask)
        sgate = mm(tokens, sgate_ref[...])
        sup = mm(tokens, sup_ref[...])
        sg_ref[block] = sgate.astype(bf16)
        su_ref[block] = sup.astype(bf16)
        middle = swiglu(sgate, sup)
        mid_ref[block] = middle
        placed = mm_tn(pick_ref[block], scaled[span])
        out_refs[mask][0] = (mm(middle, sdown_ref[...]) + placed).astype(bf16)
    wait()


def backward_kernel(parts, base_ref, *refs):
    *refs, copied = refs
    up_refs, (pick_ref, gates_ref, y_ref, sg_ref, su_ref) = refs[:8], refs[8:13]
    g_refs, u_refs = (refs[13 + i * parts : 13 + (i + 1) * parts] for i in range(2))
    rest = refs[13 + 2 * parts :]
    gate_refs, rise_refs, down_refs = (rest[i * parts : (i + 1) * parts] for i in range(3))
    sgate_ref, sup_ref, sdown_ref = rest[3 * parts : 3 + 3 * parts]
    outs = refs[-(8 + 2 * parts) :]
    db_refs, (ups_ref, dy_ref, dgate_ref, pair_ref) = outs[:4], outs[4:8]
    dg_refs, du_refs = (outs[8 + i * parts : 8 + (i + 1) * parts] for i in range(2))
    slots = pick_ref.shape[1]
    blocks = [mask ^ base_ref[1] for mask in range(4)]
    spans = [slice(mask * slots, (mask + 1) * slots) for mask in range(4)]
    wait = copy_blocks(base_ref, up_refs, ups_ref, copied)

    for mask, (block, span) in enumerate(zip(blocks, spans)):
        upstream = block_of_step(up_refs, mask)
        dy_ref[span, :] = mm(pick_ref[block], upstream).astype(bf16)
    gates = pick_all(pick_ref, gates_ref, blocks)
    grad_rows = dy_ref[...].astype(f32)
    dgates = jnp.sum(grad_rows * y_ref[...].astype(f32), axis=-1, keepdims=True)
    dy = (gates * grad_rows).astype(bf16)
    dy_ref[...] = dy
    db = jnp.zeros(dy.shape, f32)
    for p in range(parts):
        dm = mm_nt(dy, down_refs[p][...])
        dg, du = swiglu_grads(g_refs[p][...].astype(f32), u_refs[p][...].astype(f32), dm)
        dg_refs[p][...] = dg
        du_refs[p][...] = du
        db = db + mm(dg, gate_refs[p][...]) + mm(du, rise_refs[p][...])
    db = db.astype(bf16)
    for mask, (block, span) in enumerate(zip(blocks, spans)):
        pick = pick_ref[block]
        dgate_ref[block] = jnp.sum(pick.astype(f32) * dgates[span], axis=0, keepdims=True)
        upstream = block_of_step(up_refs, mask)
        sgate, sup = sg_ref[block].astype(f32), su_ref[block].astype(f32)
        dsg, dsu = swiglu_grads(sgate, sup, mm_nt(upstream, sdown_ref[...]))
        pair_ref[0, block] = dsg
        pair_ref[1, block] = dsu
        db_refs[mask][0] = (
            mm_nt(dsg, sgate_ref[...]) + mm_nt(dsu, sup_ref[...]) + mm_tn(pick, db[span])
        ).astype(bf16)
    wait()


def expert_call(kernel, name, piece, blocks, tiled, weights, held_shapes, held, part, width, flops):
    operands, specs = block_operands(blocks)
    fixed = lambda i, base: (0, 0)

    groups = held_shapes[0][0].shape[0] // 4

    def spec(shape, axis=0):
        tile = tuple(n // groups if d == axis else n for d, n in enumerate(shape))
        at = lambda i, base: tuple(
            base[0] * 2 + (i ^ base[2]) if d == axis else 0 for d in range(len(shape))
        )
        return pl.BlockSpec(tile, at)

    out_specs = [pl.BlockSpec((1, part, width), lambda i, base: (i, 0, 0))] * 4
    for shape, axis in held_shapes:
        out_specs.append(
            pl.BlockSpec(memory_space=pl.ANY) if axis is None else spec(shape.shape, axis)
        )
    results = pl.pallas_call(
        kernel,
        grid_spec=pltpu.PrefetchScalarGridSpec(
            num_scalar_prefetch=1,
            grid=(2,),
            in_specs=specs
            + [spec(v.shape) for v in tiled]
            + [pl.BlockSpec(w.shape, fixed, pipeline_mode=pl.Buffered(1)) for w in weights]
            + [pl.BlockSpec(memory_space=pl.ANY)] * len(held),
            out_specs=out_specs,
            scratch_shapes=[pltpu.SemaphoreType.DMA((4,))],
        ),
        out_shape=[jax.ShapeDtypeStruct((2, part, width), bf16)] * 4
        + [shape for shape, _ in held_shapes],
        input_output_aliases={
            1 + len(operands) + len(tiled) + len(weights) + i: 4 + i for i in range(len(held))
        },
        compiler_params=pltpu.CompilerParams(vmem_limit_bytes=60 * megabytes),
        cost_estimate=pl.CostEstimate(
            flops=flops, bytes_accessed=40 * megabytes, transcendentals=1 << 20
        ),
        name=name,
    )(piece_place(piece), *operands, *tiled, *weights, *held)
    return results[:4], results[4:]


def expert_work(pick, gates, gate_w, up_w, down_w, sgate, sup, sdown):
    ctx, slots, part = pick.shape
    width, hidden = sgate.shape
    parts = len(gate_w)
    inner = [w.shape[0] for w in gate_w]
    weights = [*gate_w, *up_w, *down_w, sgate, sup, sdown]
    whole = lambda *shape, dtype=bf16: jax.ShapeDtypeStruct(shape, dtype)
    blocks = (whole(ctx, part, width), None)
    rows = (whole(ctx * slots, width), 0)
    units = [(whole(ctx * slots, w), 0) for w in inner]
    shared = (whole(ctx, part, hidden), 0)
    flops = 48 * (slots * width * sum(inner) + part * width * hidden)
    forward_shapes = [blocks, rows, rows, shared, shared, shared, *units * 3]
    dgates = (whole(ctx, 1, part, dtype=f32), 0)
    backward_shapes = [blocks, rows, dgates, (whole(2, ctx, part, hidden), 1), *units * 2]

    def forward(piece, tokens, held):
        return expert_call(
            functools.partial(forward_kernel, parts), "experts_forward", piece, tokens, [pick, gates],
            weights, forward_shapes, held, part, width, flops,
        )

    def backward(piece, upstream, done, held):
        _, _, y, _, sg, su, *units = done
        tiled = [pick, gates, y, sg, su, *units[parts:]]
        return expert_call(
            functools.partial(backward_kernel, parts), "experts_backward", piece, upstream, tiled,
            weights, backward_shapes, held, part, width, flops,
        )

    return forward, backward


def shards(
    hidden_in, gain_attn, w_query, w_kv_down, gain_kv, w_kv_up, w_out, gain_ffn, w_router,
    shared_gate, shared_up, shared_down, expert_gate, expert_up, expert_down, routes, cotangent,
):
    part, width = hidden_in.shape[1:]
    ctx, fsdp = lax.axis_size("ctx"), lax.axis_size("fsdp")
    ctx_rank = lax.axis_index("ctx")
    length = part * ctx
    rows = w_query.shape[0]
    experts = w_router.shape[1]
    parts_of_head = ctx // HEADS
    query_part = part // parts_of_head
    first_row = (ctx_rank % parts_of_head) * query_part
    everywhere = ("ctx", "fsdp")

    def join_rows(parts):
        if fsdp != 2:
            return jnp.stack(parts, axis=1).reshape(-1, parts[0].shape[-1])
        rank = lax.axis_index("fsdp")
        whole = jnp.zeros((ctx, 2) + parts[0].shape[1:], parts[0].dtype)
        for place, value in ((rank, parts[0]), (1 - rank, parts[1])):
            whole = lax.dynamic_update_slice_in_dim(whole, value[:, None], place, 1)
        return whole.reshape(-1, parts[0].shape[-1])

    def to_rows(columns, count):
        grid = columns.reshape(ctx, fsdp, count, columns.shape[-1])
        grid = scatter_fsdp(in_fsdp_order([grid[:, i] for i in range(fsdp)]))
        return to_owner(grid.astype(bf16)).astype(f32)

    def head_blocks(values):
        blocks = values.reshape(values.shape[0], HEADS, -1).transpose(1, 0, 2)
        return jnp.repeat(blocks, parts_of_head, axis=0)

    def from_head_blocks(blocks):
        blocks = blocks.reshape(HEADS, parts_of_head, *blocks.shape[1:]).sum(axis=1)
        return blocks.transpose(1, 0, 2).reshape(blocks.shape[1], -1)

    compressed_width = KVR + ROPE
    turned_width = compressed_width + ROPE
    kv_rows = gain_kv.shape[0]
    small_width = turned_width + experts + 3
    small = jnp.concatenate(
        [
            w_kv_down,
            turn_columns(w_kv_down[:, KVR:]),
            w_router,
            gain_attn[:, None],
            gain_ffn[:, None],
            jnp.pad(gain_kv, (0, rows - kv_rows))[:, None],
            jnp.zeros((rows, -small_width % 128), bf16),
        ],
        axis=1,
    )
    small_full = lax.all_gather(small, everywhere, axis=0, tiled=True)
    reduce_full = small_full[:, :compressed_width]
    router_full = small_full[:, turned_width : small_width - 3]

    tokens_low = hidden_in.reshape(part, width)
    upstream_low = cotangent.reshape(part, width)
    hidden_shared = shared_gate.shape[1] // ctx
    query_blocks = head_blocks(w_query)
    route_rows = routes.reshape(part, TOP)
    chosen_hot = route_rows[:, :, None] == jnp.arange(experts, dtype=jnp.int32)[None, None, :]
    columns = [
        query_blocks,
        turn_columns(query_blocks[..., NOPE:]),
        head_blocks(w_kv_up).reshape(ctx, rows, -1),
        jnp.any(chosen_hot, axis=1).astype(bf16).T.reshape(ctx, rows, -1),
    ]
    column_blocks = jnp.concatenate(columns, axis=-1)
    expand_end = WIDE + columns[2].shape[-1]

    def joined_stage(received, _):
        gains = small_full[:, small_width - 3 :].astype(f32)
        kv_gain = gains[:, 2].reshape(ctx * fsdp, rows)[:, :kv_rows].reshape(KVR)
        by_rows = join_rows(gather_fsdp(received[..., :expand_end]))
        return received, by_rows, gains[:, 0], gains[:, 1], kv_gain

    tokens_all, (received, by_rows, attn_gain, ffn_gain, kv_gain) = gather_ctx(
        tokens_low, *[lambda *_: None] * 2, lambda *_: to_owner(column_blocks), joined_stage
    )
    named_all = received[..., expand_end:].reshape(ctx, part)
    query_w = by_rows[:, :WIDE]
    expand = by_rows[:, WIDE:].reshape(KVR, NOPE + VHEAD)
    output_full = lax.all_gather(w_out, everywhere, axis=0, tiled=True)

    upstream_late, gate_late, up_late, _ = lax.optimization_barrier(
        (upstream_low, shared_gate, shared_up, tokens_all[-1][3][1][0])
    )
    columns = [v.reshape(rows, ctx, hidden_shared) for v in (gate_late, up_late)]
    shared_blocks = jnp.concatenate(columns, axis=2).transpose(1, 0, 2)
    shared_back = jnp.concatenate(in_fsdp_order(gather_fsdp(shared_down)), axis=0)
    gate_parts = gather_fsdp(expert_gate[0].T)
    up_parts = gather_fsdp(expert_up[0].T)
    down_parts = gather_fsdp(expert_down[0].T)

    slot_cap = min(part, part * TOP * 4 // (3 * experts))
    until = jnp.arange(part)[:, None] <= jnp.arange(part)[None, :]
    ordinal = mm(named_all, until.astype(bf16)) - 1.0
    slots = jnp.arange(slot_cap, dtype=f32)[None, :, None]
    pick = ((ordinal[:, None, :] == slots) & (named_all[:, None, :] > 0)).astype(bf16)

    cosine, sine = rope_tables(jnp.arange(length, dtype=jnp.int32))
    table = jnp.concatenate([cosine, sine], axis=-1)
    def query_rows(values):
        if parts_of_head == 1:
            return values
        blocks = values.reshape(ctx, part, values.shape[-1])
        blocks = lax.dynamic_slice_in_dim(blocks, first_row, query_part, 1)
        return blocks.reshape(ctx * query_part, values.shape[-1])

    def to_heads(values):
        split = values.reshape(parts_of_head, query_part, HEADS, values.shape[-1])
        sent = split.transpose(2, 0, 1, 3).reshape(ctx, query_part, values.shape[-1])
        return to_owner(sent).reshape(ctx * query_part, values.shape[-1])

    def from_heads(values):
        back = to_owner(values.reshape(ctx, query_part, values.shape[-1]))
        back = back.reshape(HEADS, parts_of_head, query_part, values.shape[-1])
        return back.transpose(1, 2, 0, 3).reshape(part, HEADS, values.shape[-1])

    query_pos = query_rows(jnp.arange(length, dtype=jnp.int32)[:, None])

    def first_stage(*_):
        return project(
            tokens_all, attn_gain[None], kv_gain[None], table, query_w, small_full, expand
        )

    def second_stage(projected, _):
        _, query_all, key_head, value_head, _ = projected
        return projected, attend(query_pos, query_rows(query_all), key_head, value_head)

    def third_stage(held, _):
        projected, (outcome, outcome_low, lse) = held
        return projected, outcome, lse, from_heads(outcome_low)

    def fourth_stage(held, _):
        return *held, to_owner(shared_blocks)

    upstream_all, (projected, outcome, lse, attended, shared_in) = gather_ctx(
        upstream_late, first_stage, second_stage, third_stage, fourth_stage
    )
    shared_in = join_rows(gather_fsdp(shared_in))
    shared_in = (shared_in[:, :hidden_shared], shared_in[:, hidden_shared:])
    normed_all, query_all, key_head, value_head, latent_all = projected
    query_head = query_rows(query_all)
    attended = attended.reshape(part, HEADS * VHEAD)
    tokens = tokens_low.astype(f32)
    residual = tokens + mm(attended, output_full)

    ffn_factor = rms_factor(residual)
    ffn_low = (residual * ffn_factor * ffn_gain).astype(bf16)
    logits = mm(ffn_low, router_full)
    chosen = jnp.sum(jnp.where(chosen_hot, logits[:, None, :], 0.0), axis=-1)
    gate_share = jax.nn.softmax(chosen, axis=-1)
    gates_own = jnp.sum(jnp.where(chosen_hot, gate_share[..., None], 0.0), axis=1)

    work = lambda gates_all: expert_work(
        pick, gates_all[:, None, :], gate_parts, up_parts, down_parts, *shared_in, shared_back
    )

    def near_forward(gates_all, pieces):
        forward, _ = work(gates_all)
        return gates_all, forward(0, pieces[0], [])

    def near_backward(held, _):
        gates_all, (out, done) = held
        arrived = plane_hops([out]) if exchanges() else []
        db, back = work(gates_all)[1](0, upstream_all[0], done, [])
        return gates_all, out, done, db, back, arrived

    ffn_all, (gates_all, out, done, db, back, out_arrived) = gather_ctx(
        ffn_low, lambda *_: None, lambda *_: to_owner(gates_own.T), near_forward, near_backward,
        early=True,
    )
    forward, backward = work(gates_all)
    out_parts, grad_parts, grad_arrived = [out], [db], []
    for piece in range(1, len(ffn_all)):
        if exchanges():
            grad_arrived = plane_hops([db])
        out, done = forward(piece, ffn_all[piece], done)
        out, done, grad_arrived = together(out, done, grad_arrived)
        if exchanges():
            out_arrived = [*out_arrived, *plane_hops([out])]
        db, back = backward(piece, upstream_all[piece], done, back)
        db, back, out_arrived = together(db, back, out_arrived)
        out_parts.append(out)
        grad_parts.append(db)
    query_late, _ = lax.optimization_barrier((w_query, ffn_all[-1][3][1][0]))
    query_full = lax.all_gather(query_late, everywhere, axis=0, tiled=True)
    tokens_flat, entries, _, shared_mid, _, _, *units = done
    middle = units[:fsdp]
    upstream_flat, grad_entries, token_dgates, shared_pair, *units = back
    gate_low, up_low = units[:fsdp], units[fsdp:]
    tokens_flat, upstream_flat, shared_mid, *shared_pair = (
        v.reshape(length, v.shape[-1])
        for v in (tokens_flat, upstream_flat, shared_mid, shared_pair[0], shared_pair[1])
    )

    sums = [(middle, grad_entries), (gate_low, entries), (up_low, entries)]
    sums = [[mm_tn(left, right) for left in lefts] for lefts, right in sums]
    sums = [[own, *(v.astype(bf16) for v in others)] for own, *others in sums]
    shared_sums = [mm_tn(shared_mid, upstream_flat), *(mm_tn(tokens_flat, v) for v in shared_pair)]
    ffn_grad, (sums, dgates_own), (shared_sums, query_full) = scatter_ctx(
        grad_parts, (sums, to_owner(token_dgates[:, 0])), (shared_sums, query_full), grad_arrived
    )
    grad_gates = jnp.sum(jnp.where(chosen_hot, dgates_own.T[:, None, :], 0.0), axis=-1)
    grad_chosen = gate_share * (
        grad_gates - jnp.sum(gate_share * grad_gates, axis=-1, keepdims=True)
    )
    grad_logits = jnp.sum(jnp.where(chosen_hot, grad_chosen[..., None], 0.0), axis=1).astype(bf16)
    grad_router = mm_tn(ffn_low, grad_logits)
    ffn_grad = ffn_grad + mm_nt(grad_logits, router_full)
    upstream = upstream_low.astype(f32)
    ffn_grad_in, grad_ffn_gain = rms_backward(residual, ffn_factor, ffn_gain, ffn_grad)
    grad_residual = upstream + ffn_grad_in
    grad_residual_low = grad_residual.astype(bf16)

    grad_attended = mm_nt(grad_residual_low, output_full).astype(bf16)
    grad_head = to_heads(grad_attended.reshape(part, HEADS, VHEAD))
    output_heads = attended.reshape(part, ctx, fsdp, rows)
    output_heads = in_fsdp_order([output_heads[:, :, i].reshape(part, -1) for i in range(fsdp)])
    grad_output = scatter_fsdp([mm_tn(v, grad_residual_low) for v in output_heads])
    grad_output = grad_output.astype(bf16).reshape(ctx, rows, width)
    grad_output = lax.psum_scatter(grad_output, "ctx", scatter_dimension=0).astype(f32)
    attention_grads = attend_grad(
        query_pos, query_rows(table), query_head, key_head, value_head, outcome, lse, grad_head, expand
    )
    if exchanges():
        out_sum, out_line = line_hops(out_parts, out_arrived)
        attention_grads, out_line = together(attention_grads, out_line)
        out_sum = plus(out_sum, *out_line)
    else:
        out_sum = whole_sum(out_parts)
    grad_query, grad_expanded, latent_part = attention_grads
    sums = [scatter_fsdp(v) for v in sums]
    latent_part, grad_query, grad_expanded, shared_sums, sums = together(
        to_owner(latent_part.reshape(ctx, part, -1)), grad_query, grad_expanded, shared_sums, sums
    )
    query_own = from_heads(grad_query)
    latent_sum = jnp.sum(latent_part.astype(f32), axis=0)
    grad_expert_down, grad_expert_gate, grad_expert_up = (v.T[None] for v in sums)
    down_rows = shared_down.shape[0]
    grad_back = shared_sums[0].reshape(fsdp, down_rows, width)
    grad_shared_down = scatter_fsdp(in_fsdp_order([grad_back[i] for i in range(fsdp)]))
    grad_in = to_rows(jnp.concatenate(shared_sums[1:], axis=-1), rows)

    grad_query_w = mm_tn(query_rows(normed_all), grad_query).reshape(ctx, fsdp, rows, QK)
    grad_expand = mm_tn(latent_all, grad_expanded).reshape(ctx, fsdp, rows, -1)
    by_heads = jnp.concatenate([grad_query_w, grad_expand], axis=-1)
    by_heads = to_rows(by_heads.reshape(width, by_heads.shape[-1]), rows)

    own_rows = ctx_rank * part
    own_normed = lax.dynamic_slice_in_dim(normed_all, own_rows, part, 0)
    latent_raw = mm(own_normed, reduce_full[:, :KVR])
    grad_latent_raw, _ = rms_backward(
        latent_raw, rms_factor(latent_raw), kv_gain, latent_sum[:, :KVR]
    )
    own_cos = lax.dynamic_slice_in_dim(cosine, own_rows, part, 0)
    own_sin = lax.dynamic_slice_in_dim(sine, own_rows, part, 0)
    grad_compressed = jnp.concatenate(
        [grad_latent_raw, unrotate(latent_sum[:, KVR:compressed_width], own_cos, own_sin)], axis=-1
    ).astype(bf16)
    grad_small = jnp.concatenate(
        [
            mm_tn(own_normed, grad_compressed).astype(bf16),
            grad_router.astype(bf16),
            grad_ffn_gain[:, None].astype(bf16),
            jnp.zeros((width, -(compressed_width + experts + 1) % 128), bf16),
        ],
        axis=1,
    ).reshape(ctx, fsdp, rows, -1)
    grad_small = scatter_fsdp(in_fsdp_order([grad_small[:, i] for i in range(fsdp)]))
    grad_small, by_heads, query_own, grad_in = together(
        grad_small.astype(bf16), by_heads, query_own, grad_in
    )
    grad_normed = mm_nt(query_own.reshape(part, HEADS * QK), query_full)
    grad_small, grad_normed = together(to_owner(grad_small), grad_normed)
    grad_small = jnp.sum(grad_small.astype(f32), axis=0)
    grad_in = grad_in.transpose(1, 0, 2)
    grad_shared_gate = grad_in[..., :hidden_shared].reshape(rows, ctx * hidden_shared)
    grad_shared_up = grad_in[..., hidden_shared:].reshape(rows, ctx * hidden_shared)
    grad_query_w = from_head_blocks(by_heads[..., :QK])
    grad_expand = from_head_blocks(by_heads[..., QK:].reshape(ctx, kv_rows, NOPE + VHEAD))
    grad_reduce = grad_small[:, :compressed_width]
    grad_normed = grad_normed + mm_nt(grad_compressed, reduce_full)
    attn_grad_in, _ = rms_backward(tokens, rms_factor(tokens), attn_gain, grad_normed)
    grad_hidden_in = (grad_residual + attn_grad_in)[None]

    def gain_grad(gain, pairs):
        total = sum(jnp.sum(w.astype(f32) * g, axis=-1) for w, g in pairs)
        return total / gain.astype(f32)

    grad_attn_gain = gain_grad(gain_attn, [(w_query, grad_query_w), (w_kv_down, grad_reduce)])
    grad_kv_gain = gain_grad(gain_kv, [(w_kv_up, grad_expand)])
    out_sum, kept, _ = lax.optimization_barrier((out_sum, residual, latent_sum))
    hidden_out = (kept + out_sum).astype(bf16)
    after = compressed_width + experts
    return (
        hidden_out[None],
        grad_hidden_in,
        grad_attn_gain,
        grad_query_w,
        grad_reduce,
        grad_kv_gain,
        grad_expand,
        grad_output,
        grad_small[:, after],
        grad_small[:, compressed_width:after],
        grad_shared_gate,
        grad_shared_up,
        grad_shared_down,
        grad_expert_gate,
        grad_expert_up,
        grad_expert_down,
    )


def solution(mesh):
    dense = P(("ctx", "fsdp"), None)
    gain = P(("ctx", "fsdp"))
    tokens = P("fsdp", "ctx", None)
    expert = P("ctx", None, "fsdp")
    return jax.shard_map(
        shards,
        mesh=mesh,
        in_specs=(
            tokens, gain, dense, dense, gain, dense, dense, gain, dense, dense, dense, dense,
            expert, expert, expert, tokens, tokens,
        ),
        out_specs=(
            tokens, tokens, gain, dense, dense, gain, dense, dense, gain, dense, dense, dense,
            dense, expert, expert, expert,
        ),
        check_vma=False,
    )
```

```python
import functools
import math

import jax
import jax.numpy as jnp
from jax import lax
from jax.experimental import pallas as pl
from jax.experimental.pallas import tpu as pltpu
from jax.sharding import PartitionSpec as P

HEADS = 16
NOPE = 128
ROPE = 64
VHEAD = 128
KVR = 512
TOP = 6
QK = NOPE + ROPE

epsilon = 1e-06
rope_base = 10000.0
masked_score = -1e30
score_scale = 1.0 / math.sqrt(QK)

bf16 = jnp.bfloat16
f32 = jnp.float32


def mm(left, right):
    return jnp.dot(left, right, preferred_element_type=f32)


def mm_nt(left, right):
    return lax.dot_general(left, right, (((1,), (1,)), ((), ())), preferred_element_type=f32)


def mm_tn(left, right):
    return lax.dot_general(left, right, (((0,), (0,)), ((), ())), preferred_element_type=f32)


def rms_factor(values):
    return lax.rsqrt(jnp.mean(values * values, axis=-1, keepdims=True) + epsilon)


def rms_backward(values, factor, gain, upstream):
    weighted = upstream * gain
    inner_mean = jnp.mean(weighted * values, axis=-1, keepdims=True)
    grad_in = factor * weighted - values * (factor * factor * factor) * inner_mean
    grad_gain = jnp.sum(upstream * values * factor, axis=0)
    return (grad_in, grad_gain)


def rope_tables(positions):
    half_width = ROPE // 2
    frequency = jnp.exp(jnp.arange(half_width, dtype=f32) * (-math.log(rope_base) / half_width))
    angles = positions.astype(f32)[:, None] * frequency[None, :]
    angles = jnp.concatenate([angles, angles], axis=-1)
    return (jnp.cos(angles), jnp.sin(angles))


def rotate(values, cosine, sine):
    half_width = values.shape[-1] // 2
    turned = jnp.concatenate([-values[..., half_width:], values[..., :half_width]], axis=-1)
    return values * cosine + turned * sine


def unrotate(upstream, cosine, sine):
    half_width = upstream.shape[-1] // 2
    rotated = upstream * sine
    turned = jnp.concatenate([rotated[..., half_width:], -rotated[..., :half_width]], axis=-1)
    return upstream * cosine + turned


def swiglu(gate_pre, up_pre):
    return (jax.nn.silu(gate_pre) * up_pre).astype(bf16)


def swiglu_grads(gate_pre, up_pre, grad_mid):
    squash = jax.nn.sigmoid(gate_pre)
    grad_gate = grad_mid * up_pre * squash * (1.0 + gate_pre * (1.0 - squash))
    grad_up = grad_mid * (gate_pre * squash)
    return (grad_gate.astype(bf16), grad_up.astype(bf16))


def exchanges():
    return lax.axis_size("ctx") == 16 and lax.axis_size("fsdp") == 2


def hop(value, mask):
    return lax.ppermute(value, "ctx", [(i, i ^ mask) for i in range(16)])


def together(*values):
    return lax.optimization_barrier(values)


def gather_ctx(block, *stages, early=False):
    held = None
    if not exchanges():
        whole = lax.all_gather(block, "ctx", axis=0)
        at = lambda piece, mask: [(whole, 8 * piece + 4 * group + mask) for group in (0, 1)]
        pieces = [[at(piece, mask) for mask in range(4)] for piece in range(whole.shape[0] // 8)]
        for stage in stages:
            held = stage(held, pieces)
        return pieces, held

    def end(number, *hops):
        nonlocal held
        if number < len(stages):
            held = stages[number](held, pieces)
        held, *hops = together(held, *hops)
        return hops

    pieces = []

    alone = lambda values: [(value[None], 0) for value in values]
    both = lambda values: [(values, 0), (values, 1)]
    near, far, one, two = end(0, *(hop(block, mask) for mask in (4, 8, 1, 2)))
    if early:
        far_near, three, *near_others = end(
            1, hop(far, 4), hop(two, 1), *(hop(near, mask) for mask in (1, 2, 3))
        )
        pieces = [[alone(v) for v in zip((block, one, two, three), (near, *near_others))]]
    else:
        far_near, three, *near_others = end(
            1, hop(far, 4), hop(two, 1), *(hop(near, mask) for mask in (1, 2))
        )
    pair = jnp.stack([far, far_near])
    relayed = () if early else (hop(three, 4),)
    far_one, far_two, *relayed = end(2, hop(pair, 1), hop(pair, 2), *relayed)
    if not early:
        near_others = [*near_others, *relayed]
        pieces = [[alone(v) for v in zip((block, one, two, three), (near, *near_others))]]
    far_three = end(3, hop(far_two[0], 1), hop(far_one[1], 2))
    return [*pieces, [both(pair), both(far_one), both(far_two), alone(far_three)]], held


def block_operands(piece):
    blocks = [block for mask in piece for block in mask]
    specs = [
        pl.BlockSpec(
            (1, *array.shape[1:]), lambda i, base, at=at: (at, 0, 0), pipeline_mode=pl.Buffered(1)
        )
        for array, at in blocks
    ]
    return [array for array, _ in blocks], specs


def block_of_step(refs, mask):
    return jnp.where(pl.program_id(0) == 0, refs[2 * mask][0], refs[2 * mask + 1][0])


def plus(*values):
    return sum(value.astype(f32) for value in values)


def plane_hops(pieces):
    return [[hop(value, mask) for mask, value in enumerate(piece) if mask] for piece in pieces]


def line_hops(pieces, arrived):
    near, far = (plus(piece[0], *values) for piece, values in zip(pieces, arrived))
    sent = ((near[1], 4), (far[0], 8), (far[1], 12))
    return near[0], [hop(value.astype(bf16), mask) for value, mask in sent]


def whole_sum(pieces):
    whole = jnp.stack([jnp.stack(piece, axis=1) for piece in pieces])
    whole = whole.reshape(-1, *whole.shape[3:])
    return lax.psum_scatter(whole, "ctx", scatter_dimension=0).astype(f32)


def scatter_ctx(pieces, beside_plane=(), beside_line=(), near=None):
    if not exchanges():
        return whole_sum(pieces), beside_plane, beside_line
    near = near or plane_hops(pieces[:1])
    near, far, beside_plane = together(near, plane_hops(pieces[1:]), beside_plane)
    own, arrived = line_hops(pieces, [*near, *far])
    arrived, beside_line = together(arrived, beside_line)
    return plus(own, *arrived), beside_plane, beside_line


def piece_place(piece):
    if not exchanges():
        return jnp.array([piece, 0, 0], jnp.int32)
    own = lax.axis_index("ctx")
    return jnp.stack([(own >> 3) ^ piece, own & 3, (own >> 2) & 1])


def swap_cores(value):
    return lax.ppermute(value, "fsdp", [(0, 1), (1, 0)])


def gather_fsdp(block):
    if lax.axis_size("fsdp") == 2:
        return [block, swap_cores(block)]
    whole = lax.all_gather(block, "fsdp", axis=0)
    return [whole[i] for i in range(lax.axis_size("fsdp"))]


def scatter_fsdp(parts):
    if lax.axis_size("fsdp") == 2:
        return parts[0].astype(f32) + swap_cores(parts[1].astype(bf16)).astype(f32)
    stacked = jnp.stack([part.astype(bf16) for part in parts])
    return lax.psum_scatter(stacked, "fsdp", scatter_dimension=0).astype(f32)


def in_fsdp_order(parts):
    if lax.axis_size("fsdp") == 2:
        low = lax.axis_index("fsdp") == 0
        return [jnp.where(low, parts[0], parts[1]), jnp.where(low, parts[1], parts[0])]
    return parts


def to_owner(blocks):
    return lax.all_to_all(blocks, "ctx", split_axis=0, concat_axis=0, tiled=True)


LANES = 128
WIDE = NOPE + 2 * ROPE
megabytes = 1024 * 1024


def turn_columns(weights):
    half = weights.shape[-1] // 2
    return jnp.concatenate([-weights[..., half:], weights[..., :half]], axis=-1)


def project_kernel(base_ref, *refs):
    token_refs = refs[:8]
    gain_ref, kv_gain_ref, table_ref, query_w_ref, reduce_ref, expand_ref = refs[8:14]
    normed_ref, query_ref, key_ref, value_ref, latent_ref = refs[-5:]
    part = token_refs[0].shape[1]
    first_half = lax.broadcasted_iota(jnp.int32, (part, LANES), 1) < ROPE
    for mask in range(4):
        span = pl.ds(pl.multiple_of((mask ^ base_ref[1]) * part, part), part)
        tokens = block_of_step(token_refs, mask).astype(f32)
        normed = (tokens * rms_factor(tokens) * gain_ref[...]).astype(bf16)
        normed_ref[span, :] = normed
        table = table_ref[span, :]

        def rope(values):
            scaled = values * table
            return scaled + pltpu.roll(scaled, ROPE, 1)

        queries = mm(normed, query_w_ref[...])
        query_ref[span, :NOPE] = queries[:, :NOPE].astype(bf16)
        query_ref[span, NOPE:] = jnp.where(first_half, rope(queries[:, NOPE:]), 0.0).astype(bf16)
        compressed = mm(normed, reduce_ref[...])
        raw = compressed[:, :KVR]
        latent = (raw * rms_factor(raw) * kv_gain_ref[...]).astype(bf16)
        latent_ref[span, :] = latent
        expanded = mm(latent, expand_ref[...]).astype(bf16)
        key_ref[span, :NOPE] = expanded[:, :NOPE]
        key_ref[span, NOPE:] = rope(compressed[:, KVR:]).astype(bf16)
        value_ref[span, :] = expanded[:, NOPE:]


def project(pieces, gain, kv_gain, table, query_w, reduce_w, expand):
    length, width = table.shape[0], query_w.shape[0]
    widths = [width, WIDE, WIDE, VHEAD, KVR]
    held = []
    for piece, blocks in enumerate(pieces):
        blocks, block_specs = block_operands(blocks)
        steps, part = 2, blocks[0].shape[1]
        tile = 4 * part
        at = lambda i, base: (base[0] * 2 + (i ^ base[2]), 0)
        fixed = lambda i, base: (0, 0)
        whole = lambda shape: pl.BlockSpec(shape, fixed, pipeline_mode=pl.Buffered(1))
        count = steps * tile
        held = pl.pallas_call(
            project_kernel,
            grid_spec=pltpu.PrefetchScalarGridSpec(
                num_scalar_prefetch=1,
                grid=(steps,),
                in_specs=block_specs
                + [
                    whole((1, width)),
                    whole((1, KVR)),
                    pl.BlockSpec((tile, LANES), at),
                    whole((width, WIDE)),
                    whole((width, KVR + LANES)),
                    whole((KVR, NOPE + VHEAD)),
                ]
                + [pl.BlockSpec(memory_space=pl.ANY)] * len(held),
                out_specs=[pl.BlockSpec((tile, w), at) for w in widths],
            ),
            out_shape=[jax.ShapeDtypeStruct((length, w), bf16) for w in widths],
            input_output_aliases={15 + i: i for i in range(len(held))},
            compiler_params=pltpu.CompilerParams(vmem_limit_bytes=56 * megabytes),
            cost_estimate=pl.CostEstimate(
                flops=2 * count * width * (WIDE + KVR + LANES),
                bytes_accessed=4 * count * width + 2 * width * (WIDE + KVR + LANES),
                transcendentals=0,
            ),
            name="project",
        )(piece_place(piece), *blocks, gain, kv_gain, table, query_w, reduce_w, expand, *held)
    return held


def attend_kernel(key_tile, reach, pos_ref, query_ref, key_ref, value_ref, out_ref, low_ref, lse_ref):
    queries = query_ref[...]
    rows = queries.shape[0]
    positions = pos_ref[...]
    tiles = (pl.program_id(0) + 1) * reach // key_tile

    def step(index, carry):
        top, total, running = carry
        keys = key_ref[pl.ds(index * key_tile, key_tile), :]
        values = value_ref[pl.ds(index * key_tile, key_tile), :]
        scores = mm_nt(queries, keys) * score_scale
        key_pos = index * key_tile + lax.broadcasted_iota(jnp.int32, scores.shape, 1)
        scores = jnp.where(key_pos <= positions, scores, masked_score)
        new_top = jnp.maximum(top, jnp.max(scores, axis=-1, keepdims=True))
        weights = jnp.exp(scores - new_top)
        shrink = jnp.exp(top - new_top)
        total = total * shrink + jnp.sum(weights, axis=-1, keepdims=True)
        running = running * shrink + mm(weights.astype(bf16), values)
        return (new_top, total, running)

    start = (
        jnp.full((rows, 1), masked_score, f32),
        jnp.zeros((rows, 1), f32),
        jnp.zeros((rows, VHEAD), f32),
    )
    top, total, running = lax.fori_loop(0, tiles, step, start)
    outcome = running / total
    out_ref[...] = outcome
    low_ref[...] = outcome.astype(bf16)
    lse_ref[...] = top + jnp.log(total)


def attend_grad_kernel(
    key_tile, reach, pos_ref, table_ref, query_ref, key_ref, value_ref, out_ref, lse_ref, grad_ref,
    expand_ref, dquery_ref, dexpand_ref, dlatent_ref, dkey_ref, dvalue_ref,
):
    @pl.when(pl.program_id(0) == 0)
    def clear():
        dkey_ref[...] = jnp.zeros_like(dkey_ref)
        dvalue_ref[...] = jnp.zeros_like(dvalue_ref)

    queries = query_ref[...]
    grads = grad_ref[...]
    positions = pos_ref[...]
    lse = lse_ref[...]
    delta = jnp.sum(grads.astype(f32) * out_ref[...], axis=-1, keepdims=True)
    tiles = (pl.program_id(0) + 1) * reach // key_tile

    def step(index, dquery):
        span = pl.ds(index * key_tile, key_tile)
        keys = key_ref[span, :]
        values = value_ref[span, :]
        scores = mm_nt(queries, keys) * score_scale
        key_pos = index * key_tile + lax.broadcasted_iota(jnp.int32, scores.shape, 1)
        probs = jnp.where(key_pos <= positions, jnp.exp(scores - lse), 0.0)
        dprobs = mm_nt(grads, values)
        dscores = (probs * (dprobs - delta)).astype(bf16)
        dvalue_ref[span, :] += mm_tn(probs.astype(bf16), grads)
        dkey_ref[span, :] += mm_tn(dscores, queries)
        return dquery + mm(dscores, keys)

    dquery = lax.fori_loop(0, tiles, step, jnp.zeros(queries.shape, f32)) * score_scale
    scaled = dquery[:, NOPE:] * table_ref[...]
    lanes = lax.broadcasted_iota(jnp.int32, scaled.shape, 1)
    half = ROPE // 2
    turned = jnp.where(lanes < half, pltpu.roll(scaled, half, 1), -pltpu.roll(scaled, LANES - half, 1))
    dquery_ref[:, :NOPE] = dquery[:, :NOPE].astype(bf16)
    dquery_ref[:, NOPE:] = (scaled + turned)[:, :ROPE].astype(bf16)

    @pl.when(pl.program_id(0) == pl.num_programs(0) - 1)
    def finish():
        def rows(index, carry):
            span = pl.ds(index * key_tile, key_tile)
            dkey = dkey_ref[span, :] * score_scale
            low = jnp.concatenate([dkey[:, :NOPE], dvalue_ref[span, :]], axis=-1).astype(bf16)
            dexpand_ref[span, :] = low
            dlatent_ref[span, :KVR] = mm_nt(low, expand_ref[...]).astype(bf16)
            dlatent_ref[span, KVR:] = dkey[:, NOPE : NOPE + ROPE].astype(bf16)
            return carry

        lax.fori_loop(0, dkey_ref.shape[0] // key_tile, rows, 0)


def attention_tiles(rows, keys):
    tile = min(512, keys)
    row_tile = rows * tile // keys
    return (row_tile, tile)


def attend(positions, queries, keys, values):
    rows, count = queries.shape[0], keys.shape[0]
    row_tile, tile = attention_tiles(rows, count)
    whole = lambda width: pl.BlockSpec((count, width), lambda i: (0, 0))
    part = lambda width: pl.BlockSpec((row_tile, width), lambda i: (i, 0))
    return pl.pallas_call(
        functools.partial(attend_kernel, tile, tile),
        grid=(rows // row_tile,),
        in_specs=[part(1), part(WIDE), whole(WIDE), whole(VHEAD)],
        out_specs=[part(VHEAD), part(VHEAD), part(1)],
        out_shape=[
            jax.ShapeDtypeStruct((rows, VHEAD), f32),
            jax.ShapeDtypeStruct((rows, VHEAD), bf16),
            jax.ShapeDtypeStruct((rows, 1), f32),
        ],
        compiler_params=pltpu.CompilerParams(vmem_limit_bytes=48 * megabytes),
        cost_estimate=pl.CostEstimate(
            flops=rows * count * (QK + VHEAD) * 2,
            bytes_accessed=4 * (rows + count) * (QK + VHEAD),
            transcendentals=rows * count // 2,
        ),
        name="attend",
    )(positions, queries, keys, values)


def attend_grad(positions, table, queries, keys, values, outcome, lse, grads, expand):
    rows, count = queries.shape[0], keys.shape[0]
    row_tile, tile = attention_tiles(rows, count)
    whole = lambda width: pl.BlockSpec((count, width), lambda i: (0, 0))
    part = lambda width: pl.BlockSpec((row_tile, width), lambda i: (i, 0))
    return pl.pallas_call(
        functools.partial(attend_grad_kernel, tile, tile),
        grid=(rows // row_tile,),
        in_specs=[
            part(1), part(LANES), part(WIDE), whole(WIDE), whole(VHEAD), part(VHEAD), part(1),
            part(VHEAD), pl.BlockSpec(expand.shape, lambda i: (0, 0)),
        ],
        out_specs=[part(QK), whole(NOPE + VHEAD), whole(KVR + ROPE)],
        out_shape=[
            jax.ShapeDtypeStruct((rows, QK), bf16),
            jax.ShapeDtypeStruct((count, NOPE + VHEAD), bf16),
            jax.ShapeDtypeStruct((count, KVR + ROPE), bf16),
        ],
        scratch_shapes=[pltpu.VMEM((count, WIDE), f32), pltpu.VMEM((count, VHEAD), f32)],
        compiler_params=pltpu.CompilerParams(vmem_limit_bytes=48 * megabytes),
        cost_estimate=pl.CostEstimate(
            flops=rows * count * (3 * QK + 2 * VHEAD) * 2,
            bytes_accessed=8 * (rows + count) * (QK + VHEAD),
            transcendentals=rows * count // 2,
        ),
        name="attend_grad",
    )(positions, table, queries, keys, values, outcome, lse, grads, expand)


def copy_blocks(base_ref, source, target, copied):
    step = pl.program_id(0)
    first = (base_ref[0] * 2 + (step ^ base_ref[2])) * 4

    def copies(group):
        return [
            pltpu.make_async_copy(
                source[2 * mask + group].at[0],
                target.at[first + (mask ^ base_ref[1])],
                copied.at[mask],
            )
            for mask in range(4)
        ]

    def each(act):
        for group in (0, 1):

            @pl.when(step == group)
            def run():
                for copy in copies(group):
                    act(copy)

    each(lambda copy: copy.start())
    return lambda: each(lambda copy: copy.wait())


def pick_all(pick_ref, gates_ref, blocks):
    return jnp.concatenate(
        [
            jnp.sum(pick_ref[block].astype(f32) * gates_ref[block], axis=-1, keepdims=True)
            for block in blocks
        ],
        axis=0,
    )


def forward_kernel(parts, base_ref, *refs):
    *refs, copied = refs
    ffn_refs, (pick_ref, gates_ref) = refs[:8], refs[8:10]
    gate_refs, rise_refs, down_refs = (refs[10 + i * parts : 10 + (i + 1) * parts] for i in range(3))
    sgate_ref, sup_ref, sdown_ref = refs[10 + 3 * parts : 13 + 3 * parts]
    outs = refs[-(10 + 3 * parts) :]
    out_refs, (tokens_ref, entries_ref, y_ref) = outs[:4], outs[4:7]
    mid_ref, sg_ref, su_ref = outs[7:10]
    m_refs, g_refs, u_refs = (outs[10 + i * parts : 10 + (i + 1) * parts] for i in range(3))
    slots = pick_ref.shape[1]
    blocks = [mask ^ base_ref[1] for mask in range(4)]
    spans = [slice(mask * slots, (mask + 1) * slots) for mask in range(4)]
    wait = copy_blocks(base_ref, ffn_refs, tokens_ref, copied)

    for mask, (block, span) in enumerate(zip(blocks, spans)):
        tokens = block_of_step(ffn_refs, mask)
        entries_ref[span, :] = mm(pick_ref[block], tokens).astype(bf16)
    gates = pick_all(pick_ref, gates_ref, blocks)
    entries = entries_ref[...]
    y = jnp.zeros(entries.shape, f32)
    for p in range(parts):
        gate = mm_nt(entries, gate_refs[p][...])
        rise = mm_nt(entries, rise_refs[p][...])
        g_refs[p][...] = gate.astype(bf16)
        u_refs[p][...] = rise.astype(bf16)
        middle = swiglu(gate, rise)
        m_refs[p][...] = middle
        y = y + mm(middle, down_refs[p][...])
    y = y.astype(bf16)
    y_ref[...] = y
    scaled = (gates * y.astype(f32)).astype(bf16)
    for mask, (block, span) in enumerate(zip(blocks, spans)):
        tokens = block_of_step(ffn_refs, mask)
        sgate = mm(tokens, sgate_ref[...])
        sup = mm(tokens, sup_ref[...])
        sg_ref[block] = sgate.astype(bf16)
        su_ref[block] = sup.astype(bf16)
        middle = swiglu(sgate, sup)
        mid_ref[block] = middle
        placed = mm_tn(pick_ref[block], scaled[span])
        out_refs[mask][0] = (mm(middle, sdown_ref[...]) + placed).astype(bf16)
    wait()


def backward_kernel(parts, base_ref, *refs):
    *refs, copied = refs
    up_refs, (pick_ref, gates_ref, y_ref, sg_ref, su_ref) = refs[:8], refs[8:13]
    g_refs, u_refs = (refs[13 + i * parts : 13 + (i + 1) * parts] for i in range(2))
    rest = refs[13 + 2 * parts :]
    gate_refs, rise_refs, down_refs = (rest[i * parts : (i + 1) * parts] for i in range(3))
    sgate_ref, sup_ref, sdown_ref = rest[3 * parts : 3 + 3 * parts]
    outs = refs[-(8 + 2 * parts) :]
    db_refs, (ups_ref, dy_ref, dgate_ref, pair_ref) = outs[:4], outs[4:8]
    dg_refs, du_refs = (outs[8 + i * parts : 8 + (i + 1) * parts] for i in range(2))
    slots = pick_ref.shape[1]
    blocks = [mask ^ base_ref[1] for mask in range(4)]
    spans = [slice(mask * slots, (mask + 1) * slots) for mask in range(4)]
    wait = copy_blocks(base_ref, up_refs, ups_ref, copied)

    for mask, (block, span) in enumerate(zip(blocks, spans)):
        upstream = block_of_step(up_refs, mask)
        dy_ref[span, :] = mm(pick_ref[block], upstream).astype(bf16)
    gates = pick_all(pick_ref, gates_ref, blocks)
    grad_rows = dy_ref[...].astype(f32)
    dgates = jnp.sum(grad_rows * y_ref[...].astype(f32), axis=-1, keepdims=True)
    dy = (gates * grad_rows).astype(bf16)
    dy_ref[...] = dy
    db = jnp.zeros(dy.shape, f32)
    for p in range(parts):
        dm = mm_nt(dy, down_refs[p][...])
        dg, du = swiglu_grads(g_refs[p][...].astype(f32), u_refs[p][...].astype(f32), dm)
        dg_refs[p][...] = dg
        du_refs[p][...] = du
        db = db + mm(dg, gate_refs[p][...]) + mm(du, rise_refs[p][...])
    db = db.astype(bf16)
    for mask, (block, span) in enumerate(zip(blocks, spans)):
        pick = pick_ref[block]
        dgate_ref[block] = jnp.sum(pick.astype(f32) * dgates[span], axis=0, keepdims=True)
        upstream = block_of_step(up_refs, mask)
        sgate, sup = sg_ref[block].astype(f32), su_ref[block].astype(f32)
        dsg, dsu = swiglu_grads(sgate, sup, mm_nt(upstream, sdown_ref[...]))
        pair_ref[0, block] = dsg
        pair_ref[1, block] = dsu
        db_refs[mask][0] = (
            mm_nt(dsg, sgate_ref[...]) + mm_nt(dsu, sup_ref[...]) + mm_tn(pick, db[span])
        ).astype(bf16)
    wait()


def expert_call(kernel, name, piece, blocks, tiled, weights, held_shapes, held, part, width, flops):
    operands, specs = block_operands(blocks)
    fixed = lambda i, base: (0, 0)

    groups = held_shapes[0][0].shape[0] // 4

    def spec(shape, axis=0):
        tile = tuple(n // groups if d == axis else n for d, n in enumerate(shape))
        at = lambda i, base: tuple(
            base[0] * 2 + (i ^ base[2]) if d == axis else 0 for d in range(len(shape))
        )
        return pl.BlockSpec(tile, at)

    out_specs = [pl.BlockSpec((1, part, width), lambda i, base: (i, 0, 0))] * 4
    for shape, axis in held_shapes:
        out_specs.append(
            pl.BlockSpec(memory_space=pl.ANY) if axis is None else spec(shape.shape, axis)
        )
    results = pl.pallas_call(
        kernel,
        grid_spec=pltpu.PrefetchScalarGridSpec(
            num_scalar_prefetch=1,
            grid=(2,),
            in_specs=specs
            + [spec(v.shape) for v in tiled]
            + [pl.BlockSpec(w.shape, fixed, pipeline_mode=pl.Buffered(1)) for w in weights]
            + [pl.BlockSpec(memory_space=pl.ANY)] * len(held),
            out_specs=out_specs,
            scratch_shapes=[pltpu.SemaphoreType.DMA((4,))],
        ),
        out_shape=[jax.ShapeDtypeStruct((2, part, width), bf16)] * 4
        + [shape for shape, _ in held_shapes],
        input_output_aliases={
            1 + len(operands) + len(tiled) + len(weights) + i: 4 + i for i in range(len(held))
        },
        compiler_params=pltpu.CompilerParams(vmem_limit_bytes=60 * megabytes),
        cost_estimate=pl.CostEstimate(
            flops=flops, bytes_accessed=40 * megabytes, transcendentals=1 << 20
        ),
        name=name,
    )(piece_place(piece), *operands, *tiled, *weights, *held)
    return results[:4], results[4:]


def expert_work(pick, gates, gate_w, up_w, down_w, sgate, sup, sdown):
    ctx, slots, part = pick.shape
    width, hidden = sgate.shape
    parts = len(gate_w)
    inner = [w.shape[0] for w in gate_w]
    weights = [*gate_w, *up_w, *down_w, sgate, sup, sdown]
    whole = lambda *shape, dtype=bf16: jax.ShapeDtypeStruct(shape, dtype)
    blocks = (whole(ctx, part, width), None)
    rows = (whole(ctx * slots, width), 0)
    units = [(whole(ctx * slots, w), 0) for w in inner]
    shared = (whole(ctx, part, hidden), 0)
    flops = 48 * (slots * width * sum(inner) + part * width * hidden)
    forward_shapes = [blocks, rows, rows, shared, shared, shared, *units * 3]
    dgates = (whole(ctx, 1, part, dtype=f32), 0)
    backward_shapes = [blocks, rows, dgates, (whole(2, ctx, part, hidden), 1), *units * 2]

    def forward(piece, tokens, held):
        return expert_call(
            functools.partial(forward_kernel, parts), "experts_forward", piece, tokens, [pick, gates],
            weights, forward_shapes, held, part, width, flops,
        )

    def backward(piece, upstream, done, held):
        _, _, y, _, sg, su, *units = done
        tiled = [pick, gates, y, sg, su, *units[parts:]]
        return expert_call(
            functools.partial(backward_kernel, parts), "experts_backward", piece, upstream, tiled,
            weights, backward_shapes, held, part, width, flops,
        )

    return forward, backward


def shards(
    hidden_in, gain_attn, w_query, w_kv_down, gain_kv, w_kv_up, w_out, gain_ffn, w_router,
    shared_gate, shared_up, shared_down, expert_gate, expert_up, expert_down, routes, cotangent,
):
    part, width = hidden_in.shape[1:]
    ctx, fsdp = lax.axis_size("ctx"), lax.axis_size("fsdp")
    ctx_rank = lax.axis_index("ctx")
    length = part * ctx
    rows = w_query.shape[0]
    experts = w_router.shape[1]
    parts_of_head = ctx // HEADS
    query_part = part // parts_of_head
    first_row = (ctx_rank % parts_of_head) * query_part
    everywhere = ("ctx", "fsdp")

    def join_rows(parts):
        if fsdp != 2:
            return jnp.stack(parts, axis=1).reshape(-1, parts[0].shape[-1])
        rank = lax.axis_index("fsdp")
        whole = jnp.zeros((ctx, 2) + parts[0].shape[1:], parts[0].dtype)
        for place, value in ((rank, parts[0]), (1 - rank, parts[1])):
            whole = lax.dynamic_update_slice_in_dim(whole, value[:, None], place, 1)
        return whole.reshape(-1, parts[0].shape[-1])

    def to_rows(columns, count):
        grid = columns.reshape(ctx, fsdp, count, columns.shape[-1])
        grid = scatter_fsdp(in_fsdp_order([grid[:, i] for i in range(fsdp)]))
        return to_owner(grid.astype(bf16)).astype(f32)

    def head_blocks(values):
        blocks = values.reshape(values.shape[0], HEADS, -1).transpose(1, 0, 2)
        return jnp.repeat(blocks, parts_of_head, axis=0)

    def from_head_blocks(blocks):
        blocks = blocks.reshape(HEADS, parts_of_head, *blocks.shape[1:]).sum(axis=1)
        return blocks.transpose(1, 0, 2).reshape(blocks.shape[1], -1)

    compressed_width = KVR + ROPE
    turned_width = compressed_width + ROPE
    kv_rows = gain_kv.shape[0]
    small_width = turned_width + experts + 3
    small = jnp.concatenate(
        [
            w_kv_down,
            turn_columns(w_kv_down[:, KVR:]),
            w_router,
            gain_attn[:, None],
            gain_ffn[:, None],
            jnp.pad(gain_kv, (0, rows - kv_rows))[:, None],
            jnp.zeros((rows, -small_width % 128), bf16),
        ],
        axis=1,
    )
    small_full = lax.all_gather(small, everywhere, axis=0, tiled=True)
    reduce_full = small_full[:, :compressed_width]
    router_full = small_full[:, turned_width : small_width - 3]

    tokens_low = hidden_in.reshape(part, width)
    upstream_low = cotangent.reshape(part, width)
    hidden_shared = shared_gate.shape[1] // ctx
    query_blocks = head_blocks(w_query)
    route_rows = routes.reshape(part, TOP)
    chosen_hot = route_rows[:, :, None] == jnp.arange(experts, dtype=jnp.int32)[None, None, :]
    columns = [
        query_blocks,
        turn_columns(query_blocks[..., NOPE:]),
        head_blocks(w_kv_up).reshape(ctx, rows, -1),
        jnp.any(chosen_hot, axis=1).astype(bf16).T.reshape(ctx, rows, -1),
    ]
    column_blocks = jnp.concatenate(columns, axis=-1)
    expand_end = WIDE + columns[2].shape[-1]

    def joined_stage(received, _):
        gains = small_full[:, small_width - 3 :].astype(f32)
        kv_gain = gains[:, 2].reshape(ctx * fsdp, rows)[:, :kv_rows].reshape(KVR)
        by_rows = join_rows(gather_fsdp(received[..., :expand_end]))
        return received, by_rows, gains[:, 0], gains[:, 1], kv_gain

    tokens_all, (received, by_rows, attn_gain, ffn_gain, kv_gain) = gather_ctx(
        tokens_low, *[lambda *_: None] * 2, lambda *_: to_owner(column_blocks), joined_stage
    )
    named_all = received[..., expand_end:].reshape(ctx, part)
    query_w = by_rows[:, :WIDE]
    expand = by_rows[:, WIDE:].reshape(KVR, NOPE + VHEAD)
    output_full = lax.all_gather(w_out, everywhere, axis=0, tiled=True)

    upstream_late, gate_late, up_late, _ = lax.optimization_barrier(
        (upstream_low, shared_gate, shared_up, tokens_all[-1][3][1][0])
    )
    columns = [v.reshape(rows, ctx, hidden_shared) for v in (gate_late, up_late)]
    shared_blocks = jnp.concatenate(columns, axis=2).transpose(1, 0, 2)
    shared_back = jnp.concatenate(in_fsdp_order(gather_fsdp(shared_down)), axis=0)
    gate_parts = gather_fsdp(expert_gate[0].T)
    up_parts = gather_fsdp(expert_up[0].T)
    down_parts = gather_fsdp(expert_down[0].T)

    slot_cap = min(part, part * TOP * 4 // (3 * experts))
    until = jnp.arange(part)[:, None] <= jnp.arange(part)[None, :]
    ordinal = mm(named_all, until.astype(bf16)) - 1.0
    slots = jnp.arange(slot_cap, dtype=f32)[None, :, None]
    pick = ((ordinal[:, None, :] == slots) & (named_all[:, None, :] > 0)).astype(bf16)

    cosine, sine = rope_tables(jnp.arange(length, dtype=jnp.int32))
    table = jnp.concatenate([cosine, sine], axis=-1)
    def query_rows(values):
        if parts_of_head == 1:
            return values
        blocks = values.reshape(ctx, part, values.shape[-1])
        blocks = lax.dynamic_slice_in_dim(blocks, first_row, query_part, 1)
        return blocks.reshape(ctx * query_part, values.shape[-1])

    def to_heads(values):
        split = values.reshape(parts_of_head, query_part, HEADS, values.shape[-1])
        sent = split.transpose(2, 0, 1, 3).reshape(ctx, query_part, values.shape[-1])
        return to_owner(sent).reshape(ctx * query_part, values.shape[-1])

    def from_heads(values):
        back = to_owner(values.reshape(ctx, query_part, values.shape[-1]))
        back = back.reshape(HEADS, parts_of_head, query_part, values.shape[-1])
        return back.transpose(1, 2, 0, 3).reshape(part, HEADS, values.shape[-1])

    query_pos = query_rows(jnp.arange(length, dtype=jnp.int32)[:, None])

    def first_stage(*_):
        return project(
            tokens_all, attn_gain[None], kv_gain[None], table, query_w, small_full, expand
        )

    def second_stage(projected, _):
        _, query_all, key_head, value_head, _ = projected
        return projected, attend(query_pos, query_rows(query_all), key_head, value_head)

    def third_stage(held, _):
        projected, (outcome, outcome_low, lse) = held
        return projected, outcome, lse, from_heads(outcome_low)

    def fourth_stage(held, _):
        return *held, to_owner(shared_blocks)

    upstream_all, (projected, outcome, lse, attended, shared_in) = gather_ctx(
        upstream_late, first_stage, second_stage, third_stage, fourth_stage
    )
    shared_in = join_rows(gather_fsdp(shared_in))
    shared_in = (shared_in[:, :hidden_shared], shared_in[:, hidden_shared:])
    normed_all, query_all, key_head, value_head, latent_all = projected
    query_head = query_rows(query_all)
    attended = attended.reshape(part, HEADS * VHEAD)
    tokens = tokens_low.astype(f32)
    residual = tokens + mm(attended, output_full)

    ffn_factor = rms_factor(residual)
    ffn_low = (residual * ffn_factor * ffn_gain).astype(bf16)
    logits = mm(ffn_low, router_full)
    chosen = jnp.sum(jnp.where(chosen_hot, logits[:, None, :], 0.0), axis=-1)
    gate_share = jax.nn.softmax(chosen, axis=-1)
    gates_own = jnp.sum(jnp.where(chosen_hot, gate_share[..., None], 0.0), axis=1)

    work = lambda gates_all: expert_work(
        pick, gates_all[:, None, :], gate_parts, up_parts, down_parts, *shared_in, shared_back
    )

    def near_forward(gates_all, pieces):
        forward, _ = work(gates_all)
        return gates_all, forward(0, pieces[0], [])

    def near_backward(held, _):
        gates_all, (out, done) = held
        arrived = plane_hops([out]) if exchanges() else []
        db, back = work(gates_all)[1](0, upstream_all[0], done, [])
        return gates_all, out, done, db, back, arrived

    ffn_all, (gates_all, out, done, db, back, out_arrived) = gather_ctx(
        ffn_low, lambda *_: None, lambda *_: to_owner(gates_own.T), near_forward, near_backward,
        early=True,
    )
    forward, backward = work(gates_all)
    out_parts, grad_parts, grad_arrived = [out], [db], []
    for piece in range(1, len(ffn_all)):
        if exchanges():
            grad_arrived = plane_hops([db])
        out, done = forward(piece, ffn_all[piece], done)
        out, done, grad_arrived = together(out, done, grad_arrived)
        if exchanges():
            out_arrived = [*out_arrived, *plane_hops([out])]
        db, back = backward(piece, upstream_all[piece], done, back)
        db, back, out_arrived = together(db, back, out_arrived)
        out_parts.append(out)
        grad_parts.append(db)
    query_late, _ = lax.optimization_barrier((w_query, ffn_all[-1][3][1][0]))
    query_full = lax.all_gather(query_late, everywhere, axis=0, tiled=True)
    tokens_flat, entries, _, shared_mid, _, _, *units = done
    middle = units[:fsdp]
    upstream_flat, grad_entries, token_dgates, shared_pair, *units = back
    gate_low, up_low = units[:fsdp], units[fsdp:]
    tokens_flat, upstream_flat, shared_mid, *shared_pair = (
        v.reshape(length, v.shape[-1])
        for v in (tokens_flat, upstream_flat, shared_mid, shared_pair[0], shared_pair[1])
    )

    sums = [(middle, grad_entries), (gate_low, entries), (up_low, entries)]
    sums = [[mm_tn(left, right) for left in lefts] for lefts, right in sums]
    sums = [[own, *(v.astype(bf16) for v in others)] for own, *others in sums]
    shared_sums = [mm_tn(shared_mid, upstream_flat), *(mm_tn(tokens_flat, v) for v in shared_pair)]
    ffn_grad, (sums, dgates_own), (shared_sums, query_full) = scatter_ctx(
        grad_parts, (sums, to_owner(token_dgates[:, 0])), (shared_sums, query_full), grad_arrived
    )
    grad_gates = jnp.sum(jnp.where(chosen_hot, dgates_own.T[:, None, :], 0.0), axis=-1)
    grad_chosen = gate_share * (
        grad_gates - jnp.sum(gate_share * grad_gates, axis=-1, keepdims=True)
    )
    grad_logits = jnp.sum(jnp.where(chosen_hot, grad_chosen[..., None], 0.0), axis=1).astype(bf16)
    grad_router = mm_tn(ffn_low, grad_logits)
    ffn_grad = ffn_grad + mm_nt(grad_logits, router_full)
    upstream = upstream_low.astype(f32)
    ffn_grad_in, grad_ffn_gain = rms_backward(residual, ffn_factor, ffn_gain, ffn_grad)
    grad_residual = upstream + ffn_grad_in
    grad_residual_low = grad_residual.astype(bf16)

    grad_attended = mm_nt(grad_residual_low, output_full).astype(bf16)
    grad_head = to_heads(grad_attended.reshape(part, HEADS, VHEAD))
    output_heads = attended.reshape(part, ctx, fsdp, rows)
    output_heads = in_fsdp_order([output_heads[:, :, i].reshape(part, -1) for i in range(fsdp)])
    grad_output = scatter_fsdp([mm_tn(v, grad_residual_low) for v in output_heads])
    grad_output = grad_output.astype(bf16).reshape(ctx, rows, width)
    grad_output = lax.psum_scatter(grad_output, "ctx", scatter_dimension=0).astype(f32)
    attention_grads = attend_grad(
        query_pos, query_rows(table), query_head, key_head, value_head, outcome, lse, grad_head, expand
    )
    if exchanges():
        out_sum, out_line = line_hops(out_parts, out_arrived)
        attention_grads, out_line = together(attention_grads, out_line)
        out_sum = plus(out_sum, *out_line)
    else:
        out_sum = whole_sum(out_parts)
    grad_query, grad_expanded, latent_part = attention_grads
    sums = [scatter_fsdp(v) for v in sums]
    latent_part, grad_query, grad_expanded, shared_sums, sums = together(
        to_owner(latent_part.reshape(ctx, part, -1)), grad_query, grad_expanded, shared_sums, sums
    )
    query_own = from_heads(grad_query)
    latent_sum = jnp.sum(latent_part.astype(f32), axis=0)
    grad_expert_down, grad_expert_gate, grad_expert_up = (v.T[None] for v in sums)
    down_rows = shared_down.shape[0]
    grad_back = shared_sums[0].reshape(fsdp, down_rows, width)
    grad_shared_down = scatter_fsdp(in_fsdp_order([grad_back[i] for i in range(fsdp)]))
    grad_in = jnp.concatenate(shared_sums[1:], axis=-1).reshape(ctx, fsdp, rows, -1)

    grad_query_w = mm_tn(query_rows(normed_all), grad_query).reshape(ctx, fsdp, rows, QK)
    grad_expand = mm_tn(latent_all, grad_expanded).reshape(ctx, fsdp, rows, -1)
    by_heads = jnp.concatenate([grad_query_w, grad_expand, grad_in], axis=-1)
    by_heads = to_rows(by_heads.reshape(width, by_heads.shape[-1]), rows)

    own_rows = ctx_rank * part
    own_normed = lax.dynamic_slice_in_dim(normed_all, own_rows, part, 0)
    latent_raw = mm(own_normed, reduce_full[:, :KVR])
    grad_latent_raw, _ = rms_backward(
        latent_raw, rms_factor(latent_raw), kv_gain, latent_sum[:, :KVR]
    )
    own_cos = lax.dynamic_slice_in_dim(cosine, own_rows, part, 0)
    own_sin = lax.dynamic_slice_in_dim(sine, own_rows, part, 0)
    grad_compressed = jnp.concatenate(
        [grad_latent_raw, unrotate(latent_sum[:, KVR:compressed_width], own_cos, own_sin)], axis=-1
    ).astype(bf16)
    grad_small = jnp.concatenate(
        [
            mm_tn(own_normed, grad_compressed).astype(bf16),
            grad_router.astype(bf16),
            grad_ffn_gain[:, None].astype(bf16),
            jnp.zeros((width, -(compressed_width + experts + 1) % 128), bf16),
        ],
        axis=1,
    ).reshape(ctx, fsdp, rows, -1)
    grad_small = scatter_fsdp(in_fsdp_order([grad_small[:, i] for i in range(fsdp)]))
    grad_small, by_heads, query_own = together(grad_small.astype(bf16), by_heads, query_own)
    grad_normed = mm_nt(query_own.reshape(part, HEADS * QK), query_full)
    grad_small, grad_normed = together(to_owner(grad_small), grad_normed)
    grad_small = jnp.sum(grad_small.astype(f32), axis=0)
    heads_end = by_heads.shape[-1] - 2 * hidden_shared
    grad_in = by_heads[..., heads_end:].transpose(1, 0, 2)
    grad_shared_gate = grad_in[..., :hidden_shared].reshape(rows, ctx * hidden_shared)
    grad_shared_up = grad_in[..., hidden_shared:].reshape(rows, ctx * hidden_shared)
    grad_query_w = from_head_blocks(by_heads[..., :QK])
    grad_expand = from_head_blocks(by_heads[..., QK:heads_end].reshape(ctx, kv_rows, NOPE + VHEAD))
    grad_reduce = grad_small[:, :compressed_width]
    grad_normed = grad_normed + mm_nt(grad_compressed, reduce_full)
    attn_grad_in, _ = rms_backward(tokens, rms_factor(tokens), attn_gain, grad_normed)
    grad_hidden_in = (grad_residual + attn_grad_in)[None]

    def gain_grad(gain, pairs):
        total = sum(jnp.sum(w.astype(f32) * g, axis=-1) for w, g in pairs)
        return total / gain.astype(f32)

    grad_attn_gain = gain_grad(gain_attn, [(w_query, grad_query_w), (w_kv_down, grad_reduce)])
    grad_kv_gain = gain_grad(gain_kv, [(w_kv_up, grad_expand)])
    out_sum, kept, _ = lax.optimization_barrier((out_sum, residual, latent_sum))
    hidden_out = (kept + out_sum).astype(bf16)
    after = compressed_width + experts
    return (
        hidden_out[None],
        grad_hidden_in,
        grad_attn_gain,
        grad_query_w,
        grad_reduce,
        grad_kv_gain,
        grad_expand,
        grad_output,
        grad_small[:, after],
        grad_small[:, compressed_width:after],
        grad_shared_gate,
        grad_shared_up,
        grad_shared_down,
        grad_expert_gate,
        grad_expert_up,
        grad_expert_down,
    )


def solution(mesh):
    dense = P(("ctx", "fsdp"), None)
    gain = P(("ctx", "fsdp"))
    tokens = P("fsdp", "ctx", None)
    expert = P("ctx", None, "fsdp")
    return jax.shard_map(
        shards,
        mesh=mesh,
        in_specs=(
            tokens, gain, dense, dense, gain, dense, dense, gain, dense, dense, dense, dense,
            expert, expert, expert, tokens, tokens,
        ),
        out_specs=(
            tokens, tokens, gain, dense, dense, gain, dense, dense, gain, dense, dense, dense,
            dense, expert, expert, expert,
        ),
        check_vma=False,
    )
```
